128 devices in a mesh: section: 2 (over core), dp: 64 (over y, z, x).
Axes of the slice: x: 4, y: 4, z: 4, core: 2. Of those that a mesh axis runs over, the one named last changes fastest.
Arguments:
- inputs: bfloat16 [2, 8192, 512], P(None, 'dp'), may hold values from -6 to 6
- groups: int32 [2, 8192], P(None, 'dp'), may hold values from 0 to 3, as said below
- cotangent: bfloat16 [2, 8192, 512], P(None, 'dp'), may hold values from -6 to 6
- w_query: bfloat16 [512, 512], replicated, may hold values from -0.25 to 0.25
- w_key: bfloat16 [512, 512], replicated, may hold values from -0.25 to 0.25
- w_value: bfloat16 [512, 512], replicated, may hold values from -0.25 to 0.25
- w_out: bfloat16 [512, 512], replicated, may hold values from -1 to 1
- w_up: bfloat16 [512, 2048], replicated, may hold values from -0.25 to 0.25
- w_down: bfloat16 [2048, 512], replicated, may hold values from -0.125 to 0.125
- gain_one: float32 [512], replicated, may hold values from 0.5 to 1.5
- shift_one: float32 [512], replicated, may hold values from -3 to 3
- gain_two: float32 [512], replicated, may hold values from 0.5 to 1.5
- shift_two: float32 [512], replicated, may hold values from -3 to 3
Outputs:
- output: bfloat16 [2, 8192, 512], P('section', 'dp')
- input_grad: bfloat16 [2, 8192, 512], P('section', 'dp')
- w_query_grad: float32 [512, 512], replicated
- w_key_grad: float32 [512, 512], replicated
- w_value_grad: float32 [512, 512], replicated
- w_out_grad: float32 [512, 512], replicated
- w_up_grad: float32 [512, 2048], replicated
- w_down_grad: float32 [2048, 512], replicated
- gain_one_grad: float32 [512], replicated
- shift_one_grad: float32 [512], replicated
- gain_two_grad: float32 [512], replicated
- shift_two_grad: float32 [512], replicated
The draws below stay inside these ranges and needn't reach their ends.
Inputs may be any that keep to these rules, and one draw needn't show every extreme that they name: Group ids come in runs of consecutive tokens; every one of the 4 groups occurs in every stream, and the first and the last token of a stream belong to the same group.
All inputs are finite; a program needn't handle non-finite values.
Results may differ from the reference program's by a relative error of at most 0.035.
Values may be sent and summed in bfloat16 or wider, within the bound.
A program may use at most 256 MiB of HBM per device.

```python
import jax
import jax.numpy as jnp
from jax import lax

D = 512
HEADS = 8
HEAD = 64
FF = 2048
MICRO = 2
GROUPS = 4
TOKENS = 8192


def draw_groups(key, part):
    key = jax.random.fold_in(key, 11)
    flag_key, table_key, order_key = jax.random.split(key, 3)
    run_span = max(8, TOKENS // 32)
    flags = (jax.random.randint(flag_key, (MICRO, TOKENS), 0, run_span) == 0).astype(jnp.int32)
    positions = jnp.arange(TOKENS, dtype=jnp.int32)
    planted = (positions == TOKENS // 8) | (positions == 2 * (TOKENS // 8)) | (positions == 3 * (TOKENS // 8)) | (positions == 4 * (TOKENS // 8))
    flags = jnp.where(planted[None, :], 1, flags)
    flags = jnp.where(positions[None, :] == 0, 0, flags)
    run_id = jnp.cumsum(flags, axis=1).astype(jnp.int32)
    order_keys = jax.random.split(order_key, MICRO)
    leading = jax.vmap(lambda sub: jax.random.permutation(sub, GROUPS).astype(jnp.int32))(order_keys)
    rest = jax.random.randint(table_key, (MICRO, TOKENS + 1), 0, GROUPS - 1).astype(jnp.int32)
    rest = rest + (rest >= leading[:, 0:1]).astype(jnp.int32)
    table = jnp.concatenate([leading, rest], axis=1)
    ids = jnp.take_along_axis(table, run_id, axis=1)
    last_run = run_id[:, -1:]
    ids = jnp.where(run_id == last_run, ids[:, 0:1], ids)
    return ids.astype(jnp.int32)


def block_levels(own_key, extent, shards, low, high):
    gain = 1.0
    for position, blocks in shards:
        heights = jax.random.uniform(jax.random.fold_in(jax.random.fold_in(own_key, 6), position), (blocks,), jnp.float32, low / len(shards), high / len(shards))
        gain = gain * jnp.repeat(jnp.exp(heights), extent[position] // blocks).reshape((-1,) + (1,) * (len(extent) - 1 - position))
    return gain


def bell_draw(stream_key, extent, width, bound, cuts=(), kind=jnp.bfloat16):
    factor_of = block_levels(stream_key, extent, cuts, -0.22, 0.18) if cuts else 1.0
    entries = jax.random.normal(stream_key, extent, jnp.float32) * width * factor_of
    return jnp.minimum(jnp.maximum(entries, -bound), bound).astype(kind)


def setup_inputs(seed: int = 0) -> dict:
    arg_keys = jax.random.split(jax.random.key(seed), 14)
    return {
        "inputs": bell_draw(arg_keys[0], (MICRO, TOKENS, D), 1.0, 6.0, ((1, 64),)),
        "groups": draw_groups(jax.random.fold_in(arg_keys[13], 71), 0),
        "cotangent": bell_draw(arg_keys[2], (MICRO, TOKENS, D), 1.0, 6.0, ((1, 64),)),
        "w_query": bell_draw(arg_keys[3], (D, D), D ** -0.5, 0.25),
        "w_key": bell_draw(arg_keys[4], (D, D), D ** -0.5, 0.25),
        "w_value": bell_draw(arg_keys[5], (D, D), D ** -0.5, 0.25),
        "w_out": bell_draw(arg_keys[6], (D, D), (D // 16) ** -0.5, 1.0),
        "w_up": bell_draw(arg_keys[7], (D, FF), D ** -0.5, 0.25),
        "w_down": bell_draw(arg_keys[8], (FF, D), FF ** -0.5, 0.125),
        "gain_one": jnp.clip(1.0 + 0.1 * jax.random.normal(arg_keys[9], (D,), jnp.float32), 0.5, 1.5),
        "shift_one": bell_draw(arg_keys[10], (D,), 0.5, 3.0, (), jnp.float32),
        "gain_two": jnp.clip(1.0 + 0.1 * jax.random.normal(arg_keys[11], (D,), jnp.float32), 0.5, 1.5),
        "shift_two": bell_draw(arg_keys[12], (D,), 0.5, 3.0, (), jnp.float32),
    }


@jax.custom_vjp
def low(v):
    return lax.optimization_barrier(v.astype(jnp.bfloat16)).astype(jnp.float32)

@jax.custom_vjp
def low_back(v):
    return v

def low_keep(v):
    return (low(v), None)

def low_pass(kept, grad):
    return (grad,)

def back_keep(v):
    return (v, None)

def back_low(kept, grad):
    return (low(grad),)
low.defvjp(low_keep, low_pass)
low_back.defvjp(back_keep, back_low)

def matmul(left, right):
    return jnp.dot(left, right, precision=lax.Precision.HIGHEST)

def layer_norm(values_in, gain_vec, shift_vec):
    centred = values_in - lax.optimization_barrier(jnp.mean(values_in, axis=-1, keepdims=True))
    factor = lax.rsqrt(lax.optimization_barrier(jnp.mean(centred * centred, axis=-1, keepdims=True)) + 1e-05)
    return centred * factor * gain_vec + shift_vec

def attention(queries, keys_all, values_all, group_row):
    length = queries.shape[0]
    span = min(512, length)
    factor = HEAD ** (-0.5)
    key_pos = jnp.arange(length, dtype=jnp.int32)

    def one_block(block_index):
        begin = (block_index * span).astype(jnp.int32)
        query_blk = lax.dynamic_slice_in_dim(queries, begin, span, 0)
        query_grp = lax.dynamic_slice_in_dim(group_row, begin, span, 0)
        query_pos = begin + jnp.arange(span, dtype=jnp.int32)
        raw_scores = low_back(jnp.einsum('thd,shd->hts', query_blk, keys_all, precision=lax.Precision.HIGHEST))
        scores = raw_scores * factor
        allowed = (key_pos[None, :] <= query_pos[:, None]) & (group_row[None, :] == query_grp[:, None])
        scores = jnp.where(allowed[None], scores, -1e+30)
        highest = lax.optimization_barrier(jnp.max(scores, axis=-1, keepdims=True))
        probs = jnp.where(allowed[None], jnp.exp(scores - highest), 0.0)
        probs = probs / lax.optimization_barrier(jnp.sum(probs, axis=-1, keepdims=True))
        return jnp.einsum('hts,shd->thd', low(probs), values_all, precision=lax.Precision.HIGHEST)
    blocks = lax.map(jax.checkpoint(one_block), jnp.arange(length // span, dtype=jnp.int32))
    return blocks.reshape(length, HEADS * HEAD)

def visit(hidden, group_row, w_query, w_key, w_value, w_out, w_up, w_down, gain_one, shift_one, gain_two, shift_two):
    length = hidden.shape[0]
    queries = low(low_back(matmul(hidden, w_query))).reshape(length, HEADS, HEAD)
    keys_all = low(low_back(matmul(hidden, w_key))).reshape(length, HEADS, HEAD)
    values_all = low(low_back(matmul(hidden, w_value))).reshape(length, HEADS, HEAD)
    attended = low(low_back(attention(queries, keys_all, values_all, group_row)))
    first = layer_norm(hidden + low_back(matmul(attended, w_out)), gain_one, shift_one)
    pre_act = low_back(matmul(low(first), w_up))
    act_low = low(jax.nn.gelu(pre_act, approximate=True))
    return layer_norm(first + low_back(matmul(act_low, w_down)), gain_two, shift_two)

def reference(inputs, groups, cotangent, w_query, w_key, w_value, w_out, w_up, w_down, gain_one, shift_one, gain_two, shift_two):
    weights = (w_query.astype(jnp.float32), w_key.astype(jnp.float32), w_value.astype(jnp.float32), w_out.astype(jnp.float32), w_up.astype(jnp.float32), w_down.astype(jnp.float32), gain_one.astype(jnp.float32), shift_one.astype(jnp.float32), gain_two.astype(jnp.float32), shift_two.astype(jnp.float32))

    def forward(stream_in, *params):
        results = []
        for batch_index in range(MICRO):
            middle = visit(stream_in[batch_index], groups[batch_index], *params)
            middle = low(low_back(middle))
            results.append(visit(middle, groups[batch_index], *params))
        return jnp.stack(results)
    produced, pull_back = jax.vjp(forward, inputs.astype(jnp.float32), *weights)
    grads = pull_back(cotangent.astype(jnp.float32))
    return (produced.astype(jnp.bfloat16), grads[0].astype(jnp.bfloat16), grads[1], grads[2], grads[3], grads[4], grads[5], grads[6], grads[7], grads[8], grads[9], grads[10])
```

```python
from types import SimpleNamespace

import jax
import jax.numpy as jnp
from jax import lax
from jax.experimental import pallas as pl
from jax.experimental.pallas import tpu as pltpu
from jax.sharding import PartitionSpec as P

F32, BF = jnp.float32, jnp.bfloat16
BIG = 1e30
ROWS, D, FF, HEADS = 128, 512, 2048, 8
MESH = pl.DeviceIdType.MESH
FWD_C, BWD_C = 8, 4


def nt(a, b):
    return lax.dot_general(a, b, (((1,), (1,)), ((), ())), preferred_element_type=F32)


def nn(a, b):
    return lax.dot_general(a, b, (((1,), (0,)), ((), ())), preferred_element_type=F32)


def tn(a, b):
    return lax.dot_general(a, b, (((0,), (0,)), ((), ())), preferred_element_type=F32)


def lanes(shape):
    return lax.broadcasted_iota(jnp.int32, shape, len(shape) - 1)


def subs(shape):
    return lax.broadcasted_iota(jnp.int32, shape, len(shape) - 2)


def ds(start, size):
    if isinstance(start, int):
        return pl.ds(start, size)
    return pl.ds(pl.multiple_of(start, size), size)


def split3(x):
    a = x.astype(BF).astype(F32)
    b = (x - a).astype(BF).astype(F32)
    return a, b, (x - a - b).astype(BF).astype(F32)


def tile_of(r, t):
    return 8 * (r // 2) + jnp.where(r % 2 == 0, t, 7 - t)


def mean(x):
    return jnp.mean(x, axis=-1, keepdims=True)


def norm(x):
    centred = x - mean(x)
    factor = lax.rsqrt(mean(centred * centred) + 1e-05)
    return centred * factor, factor


def norm_back(dy, n, factor, gain):
    u = dy * gain
    return factor * (u - mean(u) - n * mean(u * n))


GELU_C = 0.7978845608028654


def gelu(x):
    return 0.5 * x * (1.0 + jnp.tanh(GELU_C * (x + 0.044715 * x * x * x)))


def gelu_slope(x):
    sq = x * x
    th = jnp.tanh(GELU_C * x * (1.0 + 0.044715 * sq))
    return 0.5 * (1.0 + th) + 0.5 * x * (1.0 - th * th) * (GELU_C * (1.0 + 3 * 0.044715 * sq))


class Place:
    def __init__(self):
        self.me = lax.axis_index("dp")
        self.s = lax.axis_index("section")
        me = self.me
        self.t = me % 4
        self.head = (me // 4) % 8
        self.micro = me // 32
        w = (me // 2) % 8
        low = w < 4
        self.own_t = jnp.where(low, w, 7 - w)
        self.own_slot = 4 * (me // 16) + jnp.where(low, 0, 2) + me % 2
        mine = self.micro == self.s
        self.self_kv = mine & (me % 2 == self.s)
        self.self_q = mine & (self.own_t == self.t)

    def chip(self, h, t):
        return (self.s * 8 + h) * 4 + t

    def send(self, src, dst, send_sem, recv_sem, section, dp):
        to_self = (section == self.s) & (dp == self.me)

        @pl.when(jnp.logical_not(to_self))
        def _():
            pltpu.make_async_remote_copy(
                src_ref=src,
                dst_ref=dst,
                send_sem=send_sem,
                recv_sem=recv_sem,
                device_id=(section, dp),
                device_id_type=MESH,
            ).start()

        @pl.when(to_self)
        def _():
            pltpu.make_async_copy(src, dst, recv_sem).start()


def wait_all(ref, sem):
    pltpu.make_async_copy(ref, ref, sem).wait()


def wait_sent(ref, sem, to_self, count):
    @pl.when(to_self)
    def _():
        wait_all(ref.at[pl.ds(0, count - 1)], sem)

    @pl.when(jnp.logical_not(to_self))
    def _():
        wait_all(ref.at[pl.ds(0, count)], sem)


def barrier(place):
    sem = pltpu.get_barrier_semaphore()

    @pl.loop(1, 128)
    def _(k):
        other = (place.s * 64 + place.me + k) % 128
        pl.semaphore_signal(sem, inc=1, device_id=(other // 64, other % 64), device_id_type=MESH)

    pl.semaphore_wait(sem, 127)


def project(v, r):
    hid = r.hid[v]
    q = nn(hid, r.w_query[...]).astype(BF).astype(F32) * 0.125
    k = nn(hid, r.w_key[...]).astype(BF).astype(F32)
    w = nn(hid, r.w_value[...]).astype(BF).astype(F32)
    ln = lanes((ROWS, 128))
    low = ln < 64
    aug = r.own_aug[...]
    for h in range(HEADS):
        cols = slice(128 * (h // 2), 128 * (h // 2) + 128)
        qt, kt, vt = q[:, cols], k[:, cols], w[:, cols]
        if h % 2 == 0:
            vt = pltpu.roll(vt, 64, 1)
        else:
            qt, kt = pltpu.roll(qt, 64, 1), pltpu.roll(kt, 64, 1)
        r.q_out[v, h] = jnp.where(low, qt, aug).astype(BF)
        r.kv_out[v, h] = jnp.where(low, kt, vt).astype(BF)


def send_qkv(v, r, place):
    @pl.loop(0, HEADS)
    def _(h):
        for t in range(4):
            place.send(
                r.kv_out.at[v, h],
                r.kv_in.at[v, place.me // 2],
                r.sems.at[0, v],
                r.sems.at[1, v],
                place.me % 2,
                place.chip(h, t),
            )
        for core in range(2):
            place.send(
                r.q_out.at[v, h],
                r.q_in.at[v, place.own_slot],
                r.sems.at[2, v],
                r.sems.at[3, v],
                core,
                place.chip(h, place.own_t),
            )


def send_groups(r, place):
    r.grp_out[0] = jnp.broadcast_to(r.groups[pl.ds(place.s, 1), :], (8, 128))

    @pl.loop(0, HEADS)
    def _(h):
        for t in range(4):
            place.send(
                r.grp_out.at[0],
                r.grp_in.at[place.me // 2],
                r.gsems.at[0],
                r.gsems.at[1],
                place.me % 2,
                place.chip(h, t),
            )


def column_of(row):
    return jnp.transpose(jnp.broadcast_to(row.astype(F32), (128, 128)))


def make_own_aug(r, place):
    ln = lanes((ROWS, 128))
    g = column_of(r.groups[pl.ds(place.s, 1), :]).astype(jnp.int32)
    r.own_aug[...] = jnp.where(ln - 64 == g, 1.0, 0.0)


def make_key_aug(r):
    ln = lanes((ROWS, 128))

    @pl.loop(0, 32)
    def _(n):
        g = column_of(r.grp_in[n][0:1, :]).astype(jnp.int32)
        inside = (ln >= 64) & (ln < 68)
        aug = jnp.where(inside, jnp.where(ln - 64 == g, 0.0, -BIG), 0.0)
        r.key_aug[n] = jnp.where((ln >= 68) & (ln < 71), 1.0, aug).astype(BF)


def make_kv(v, r):
    ln = lanes((ROWS, 128))
    low = ln < 64
    ones = jnp.where(ln < 3, 1.0, 0.0)

    @pl.loop(0, 32)
    def _(n):
        rows = ds(n * 128, 128)
        kv = r.kv_in[v, n].astype(F32)
        r.ka[v, rows, :] = jnp.where(low, kv, r.key_aug[n].astype(F32)).astype(BF)
        r.va[v, rows, :] = jnp.where(low, ones, kv).astype(BF)


def fwd_tile(v, i, r, place):
    width = FWD_C * 128
    u = tile_of(i, place.t)
    q = jnp.concatenate([r.q_in[v, 2 * i], r.q_in[v, 2 * i + 1]], axis=0)

    def step(c, carry, masked):
        top, acc = carry
        rows = ds(c * width, width)
        sc = nt(q, r.ka[v, rows, :])
        if masked:
            col, row = lanes((256, width)), subs((256, width))
            at = 256 * (col // 128) + col % 128 + (256 * FWD_C * c + 128 * place.s - 256 * u)
            sc = jnp.where(at <= row, sc, -BIG)
        new = jnp.maximum(top, jnp.max(sc, axis=1, keepdims=True))
        p = jnp.exp(sc - new).astype(BF)
        return new, acc * jnp.exp(top - new) + nn(p, r.va[v, rows, :])

    start = (jnp.full((256, 1), -2 * BIG, F32), jnp.zeros((256, 128), F32))
    full = u // FWD_C
    carry = lax.fori_loop(0, full, lambda c, x: step(c, x, False), start)
    top, acc = step(full, carry, True)
    total = acc[:, 0:1]
    a, b, c = split3(top + jnp.log(total))
    ln = lanes((256, 128))
    aux = jnp.where(ln == 0, a, jnp.where(ln == 1, b, jnp.where(ln == 2, c, 0.0)))
    out = jnp.where(ln >= 64, acc / total, aux).astype(BF)
    r.o_out[v, 2 * i] = out[:128]
    r.o_out[v, 2 * i + 1] = out[128:]
    for half in range(2):
        place.send(
            r.o_out.at[v, 2 * i + half],
            r.o_in.at[v, 2 * place.head + place.s],
            r.sems.at[4, v],
            r.sems.at[5, v],
            place.micro,
            2 * u + half,
        )


def after_attention(v, r):
    ln = lanes((ROWS, 128))
    low = ln < 64
    att = []
    for h in range(HEADS):
        parts = [r.o_in[v, 2 * h + core].astype(F32) for core in range(2)]
        logs = [x[:, 0:1] + x[:, 1:2] + x[:, 2:3] for x in parts]
        top = jnp.maximum(logs[0], logs[1])
        weights = [jnp.exp(x - top) for x in logs]
        total = weights[0] + weights[1]
        whole = (parts[0] * weights[0] + parts[1] * weights[1]) / total
        log_total = top + jnp.log(total)
        r.att[v, h] = jnp.where(low, jnp.where(ln == 0, log_total, 0.0), whole)
        att.append(whole)
    for i in range(HEADS // 2):
        pair = jnp.where(low, pltpu.roll(att[2 * i], 64, 1), att[2 * i + 1])
        r.att_low[v, :, 128 * i : 128 * i + 128] = pair.astype(BF)
    mixed = r.hid[v].astype(F32) + nn(r.att_low[v], r.w_out[...])
    n_one, f_one = norm(mixed)
    first = n_one * r.gain_one[...] + r.shift_one[...]
    first_low = first.astype(BF)
    r.n_one[v] = n_one
    r.f_one[v] = jnp.broadcast_to(f_one, (ROWS, 128))
    r.first_low[v] = first_low
    r.work[...] = first

    @pl.loop(0, 4)
    def _(j):
        cols = ds(j * 512, 512)
        pre = nn(r.first_low[v], r.w_up[:, cols])
        r.pre[v, :, cols] = pre
        act = gelu(pre).astype(BF)
        r.act[v, :, cols] = act
        r.work[...] += nn(act, r.w_down[cols, :])

    n_two, f_two = norm(r.work[...])
    r.n_two[v] = n_two
    r.f_two[v] = jnp.broadcast_to(f_two, (ROWS, 128))
    r.hid[v + 1] = (n_two * r.gain_two[...] + r.shift_two[...]).astype(BF)


def before_attention_back(v, r):
    dy = r.dy[...]
    n_two = r.n_two[v]
    r.vec[2:3, :] += jnp.sum(dy * n_two, axis=0, keepdims=True)
    r.vec[3:4, :] += jnp.sum(dy, axis=0, keepdims=True)
    grad_two = norm_back(dy, n_two, r.f_two[v][:, 0:1], r.gain_two[...])
    r.down_low[v] = grad_two.astype(BF)
    r.work[...] = grad_two

    @pl.loop(0, 4)
    def _(j):
        cols = ds(j * 512, 512)
        grad = nt(r.down_low[v], r.w_down[cols, :])
        up = (grad * gelu_slope(r.pre[v, :, cols])).astype(BF)
        r.up_low[v, :, cols] = up
        r.work[...] += nt(up, r.w_up[:, cols])

    dz = r.work[...]
    n_one = r.n_one[v]
    r.vec[0:1, :] += jnp.sum(dz * n_one, axis=0, keepdims=True)
    r.vec[1:2, :] += jnp.sum(dz, axis=0, keepdims=True)
    grad_one = norm_back(dz, n_one, r.f_one[v][:, 0:1], r.gain_one[...])
    out_low = grad_one.astype(BF)
    r.out_low[v] = out_low
    r.work[...] = grad_one
    grad_att = nt(out_low, r.w_out[...]).astype(BF).astype(F32)
    ln = lanes((ROWS, 128))
    low = ln < 64
    for h in range(HEADS):
        tile = grad_att[:, 128 * (h // 2) : 128 * (h // 2) + 128]
        if h % 2 == 0:
            tile = pltpu.roll(tile, 64, 1)
        att = r.att[v, h]
        delta = jnp.sum(jnp.where(low, 0.0, tile * att), axis=1, keepdims=True)
        parts = split3(-delta) + split3(-att[:, 0:1])
        aux = jnp.zeros((ROWS, 128), F32)
        for i, part in enumerate(parts):
            aux = jnp.where(ln == i, part, aux)
        r.do_out[v, h] = jnp.where(low, aux, tile).astype(BF)


def send_do(v, r, place):
    @pl.loop(0, HEADS)
    def _(h):
        for core in range(2):
            place.send(
                r.do_out.at[v, h],
                r.do_in.at[v, place.own_slot],
                r.sems.at[6, v],
                r.sems.at[7, v],
                core,
                place.chip(h, place.own_t),
            )


def bwd_tile(v, i, r, place):
    width = BWD_C * 128
    u = tile_of(i, place.t)
    q = jnp.concatenate([r.q_in[v, 2 * i], r.q_in[v, 2 * i + 1]], axis=0).astype(F32)
    do = jnp.concatenate([r.do_in[v, 2 * i], r.do_in[v, 2 * i + 1]], axis=0).astype(F32)
    ln = lanes((256, 128))
    lq = jnp.where((ln >= 68) & (ln < 71), pltpu.roll(do, 65, 1), q).astype(BF)
    ld = jnp.where((ln >= 3) & (ln < 64), 0.0, do).astype(BF)
    qz = jnp.where(ln < 64, q, 0.0).astype(BF)
    dz = jnp.where(ln >= 64, do, 0.0).astype(BF)

    def step(c, dqt, masked):
        rows = ds(c * width, width)
        x = nt(r.ka[v, rows, :], lq)
        if masked:
            row, col = subs((width, 256)), lanes((width, 256))
            at = 256 * (row // 128) + row % 128 + (256 * BWD_C * c + 128 * place.s - 256 * u)
            x = jnp.where(at <= col, x, -BIG)
        p = jnp.exp(x)
        dp = nt(r.va[v, rows, :], ld)
        dsc = (p * dp).astype(BF)
        r.dkv_acc[rows, :] += nn(dsc, qz) + nn(p.astype(BF), dz)
        return dqt + nn(r.kat[:, rows], dsc)

    full = u // BWD_C
    dqt = lax.fori_loop(0, full, lambda c, x: step(c, x, False), jnp.zeros((64, 256), F32))
    dqt = step(full, dqt, True)
    dq = jnp.transpose(jnp.concatenate([dqt, jnp.zeros((64, 256), F32)], axis=0)).astype(BF)
    r.dq_out[v, 2 * i] = dq[:128]
    r.dq_out[v, 2 * i + 1] = dq[128:]
    for half in range(2):
        place.send(
            r.dq_out.at[v, 2 * i + half],
            r.dq_in.at[v, 2 * place.head + place.s],
            r.sems.at[8, v],
            r.sems.at[9, v],
            place.micro,
            2 * u + half,
        )


def attention_back(v, r, place):
    r.dkv_acc[...] = jnp.zeros_like(r.dkv_acc)

    @pl.loop(0, 8)
    def _(i):
        rows = ds(i * 512, 512)
        r.kat[:, rows] = jnp.transpose(r.ka[v, rows, :].astype(F32))[:64].astype(BF)

    @pl.loop(0, 8)
    def _(i):
        bwd_tile(v, i, r, place)

    @pl.loop(0, 32)
    def _(n):
        r.dkv_out[v, n] = r.dkv_acc[ds(n * 128, 128), :].astype(BF)
        place.send(
            r.dkv_out.at[v, n],
            r.dkv_in.at[v, 4 * place.head + place.t],
            r.sems.at[10, v],
            r.sems.at[11, v],
            place.micro,
            2 * n + place.s,
        )


def after_attention_back(v, r):
    ln = lanes((ROWS, 128))
    low = ln < 64
    for i in range(HEADS // 2):
        cols = slice(128 * i, 128 * i + 128)
        dq, dkv = [], []
        for h in (2 * i, 2 * i + 1):
            both = r.dq_in[v, 2 * h].astype(F32) + r.dq_in[v, 2 * h + 1].astype(F32)
            dq.append(both * 0.125)
            four = [r.dkv_in[v, 4 * h + t].astype(F32) for t in range(4)]
            dkv.append((four[0] + four[1]) + (four[2] + four[3]))
        r.dq[v, :, cols] = jnp.where(low, dq[0], pltpu.roll(dq[1], 64, 1)).astype(BF)
        r.dk[v, :, cols] = jnp.where(low, dkv[0], pltpu.roll(dkv[1], 64, 1)).astype(BF)
        r.dv[v, :, cols] = jnp.where(low, pltpu.roll(dkv[0], 64, 1), dkv[1]).astype(BF)
    r.work[...] += (
        nt(r.dq[v], r.w_query[...]) + nt(r.dk[v], r.w_key[...]) + nt(r.dv[v], r.w_value[...])
    )


def both(ref):
    return jnp.concatenate([ref[0], ref[1]], axis=0)


def weight_grads(r):
    hid = jnp.concatenate([r.hid[0], r.hid[1]], axis=0)
    r.g_query[...] = tn(hid, both(r.dq))
    r.g_key[...] = tn(hid, both(r.dk))
    r.g_value[...] = tn(hid, both(r.dv))
    r.g_out[...] = tn(both(r.att_low), both(r.out_low))

    @pl.loop(0, 4)
    def _(j):
        cols = ds(j * 512, 512)
        up = jnp.concatenate([r.up_low[0, :, cols], r.up_low[1, :, cols]], axis=0)
        r.g_up[:, cols] = tn(both(r.first_low), up)
        act = jnp.concatenate([r.act[0, :, cols], r.act[1, :, cols]], axis=0)
        r.g_down[cols, :] = tn(act, both(r.down_low))


INPUTS = ["inputs", "groups", "cotangent", "w_query", "w_key", "w_value", "w_out", "w_up", "w_down"]
INPUTS += ["gain_one", "shift_one", "gain_two", "shift_two"]
OUTPUTS = {
    "output": ((1, ROWS, D), BF),
    "input_grad": ((1, ROWS, D), BF),
    "g_query": ((D, D), F32),
    "g_key": ((D, D), F32),
    "g_value": ((D, D), F32),
    "g_out": ((D, D), F32),
    "g_up": ((D, FF), F32),
    "g_down": ((FF, D), F32),
    "vec": ((8, D), F32),
}
SCRATCH = {
    "hid": ((3, ROWS, D), BF),
    "own_aug": ((ROWS, 128), F32),
    "q_out": ((2, 8, ROWS, 128), BF),
    "kv_out": ((2, 8, ROWS, 128), BF),
    "q_in": ((2, 16, ROWS, 128), BF),
    "kv_in": ((2, 32, ROWS, 128), BF),
    "grp_out": ((1, 8, 128), jnp.int32),
    "grp_in": ((32, 8, 128), jnp.int32),
    "key_aug": ((32, ROWS, 128), BF),
    "ka": ((2, 4096, 128), BF),
    "va": ((2, 4096, 128), BF),
    "kat": ((64, 4096), BF),
    "o_out": ((2, 16, ROWS, 128), BF),
    "o_in": ((2, 16, ROWS, 128), BF),
    "att": ((2, 8, ROWS, 128), F32),
    "att_low": ((2, ROWS, D), BF),
    "n_one": ((2, ROWS, D), F32),
    "f_one": ((2, ROWS, 128), F32),
    "first_low": ((2, ROWS, D), BF),
    "pre": ((2, ROWS, FF), F32),
    "act": ((2, ROWS, FF), BF),
    "n_two": ((2, ROWS, D), F32),
    "f_two": ((2, ROWS, 128), F32),
    "work": ((ROWS, D), F32),
    "dy": ((ROWS, D), F32),
    "down_low": ((2, ROWS, D), BF),
    "up_low": ((2, ROWS, FF), BF),
    "out_low": ((2, ROWS, D), BF),
    "do_out": ((2, 8, ROWS, 128), BF),
    "do_in": ((2, 16, ROWS, 128), BF),
    "dq_out": ((2, 16, ROWS, 128), BF),
    "dq_in": ((2, 16, ROWS, 128), BF),
    "dkv_acc": ((4096, 128), F32),
    "dkv_out": ((2, 32, ROWS, 128), BF),
    "dkv_in": ((2, 32, ROWS, 128), BF),
    "dq": ((2, ROWS, D), BF),
    "dk": ((2, ROWS, D), BF),
    "dv": ((2, ROWS, D), BF),
}


def kernel(*refs):
    names = INPUTS + list(OUTPUTS) + list(SCRATCH) + ["sems", "gsems"]
    r = SimpleNamespace(**dict(zip(names, refs)))
    place = Place()
    barrier(place)
    send_groups(r, place)
    make_own_aug(r, place)
    r.vec[...] = jnp.zeros_like(r.vec)
    r.hid[0] = r.inputs[place.s]

    @pl.loop(0, 2)
    def _(v):
        project(v, r)
        send_qkv(v, r, place)

        @pl.when(v == 0)
        def _():
            wait_all(r.grp_in, r.gsems.at[1])
            make_key_aug(r)

        wait_all(r.kv_in.at[v], r.sems.at[1, v])
        make_kv(v, r)
        wait_all(r.q_in.at[v], r.sems.at[3, v])

        @pl.loop(0, 8)
        def _(i):
            fwd_tile(v, i, r, place)

        wait_all(r.o_in.at[v], r.sems.at[5, v])
        after_attention(v, r)

    r.output[0] = r.hid[2]
    r.dy[...] = r.cotangent[place.s].astype(F32)

    @pl.loop(0, 2)
    def _(step):
        v = 1 - step
        before_attention_back(v, r)
        send_do(v, r, place)
        wait_all(r.do_in.at[v], r.sems.at[7, v])
        attention_back(v, r, place)
        wait_all(r.dq_in.at[v], r.sems.at[9, v])
        wait_all(r.dkv_in.at[v], r.sems.at[11, v])
        after_attention_back(v, r)
        r.dy[...] = r.work[...].astype(BF).astype(F32)

    r.input_grad[0] = r.dy[...].astype(BF)
    weight_grads(r)

    wait_sent(r.grp_in, r.gsems.at[0], place.self_kv, 32)

    @pl.loop(0, 2)
    def _(v):
        wait_sent(r.kv_in.at[v], r.sems.at[0, v], place.self_kv, 32)
        wait_sent(r.q_in.at[v], r.sems.at[2, v], place.self_q, 16)
        wait_sent(r.o_in.at[v], r.sems.at[4, v], place.self_q, 16)
        wait_sent(r.do_in.at[v], r.sems.at[6, v], place.self_q, 16)
        wait_sent(r.dq_in.at[v], r.sems.at[8, v], place.self_q, 16)
        wait_sent(r.dkv_in.at[v], r.sems.at[10, v], place.self_kv, 32)


def on_device(inputs, groups, cotangent, *params):
    vectors = [x.reshape(1, D) for x in params[6:]]
    vmem = pl.BlockSpec(memory_space=pltpu.VMEM)
    out = pl.pallas_call(
        kernel,
        out_shape=[jax.ShapeDtypeStruct(shape, kind) for shape, kind in OUTPUTS.values()],
        in_specs=[vmem] * len(INPUTS),
        out_specs=[vmem] * len(OUTPUTS),
        scratch_shapes=[pltpu.VMEM(shape, kind) for shape, kind in SCRATCH.values()]
        + [pltpu.SemaphoreType.DMA((12, 2)), pltpu.SemaphoreType.DMA((2,))],
        compiler_params=pltpu.CompilerParams(
            collective_id=0, has_side_effects=True, vmem_limit_bytes=60 * 2**20
        ),
        name="visits",
    )(inputs, groups, cotangent, *params[:6], *vectors)
    sums = lax.psum(tuple(out[2:]), ("section", "dp"))
    vec = sums[6]
    return (*out[:2], *sums[:6], vec[0], vec[1], vec[2], vec[3])


def solution(mesh):
    rows = P(None, "dp", None)
    return jax.shard_map(
        on_device,
        mesh=mesh,
        in_specs=(rows, P(None, "dp"), rows) + (P(),) * 10,
        out_specs=(P("section", "dp", None),) * 2 + (P(),) * 10,
        check_vma=False,
    )
```

```python
from types import SimpleNamespace

import jax
import jax.numpy as jnp
from jax import lax
from jax.experimental import pallas as pl
from jax.experimental.pallas import tpu as pltpu
from jax.sharding import PartitionSpec as P

F32, BF = jnp.float32, jnp.bfloat16
BIG = 1e30
ROWS, D, FF, HEADS = 128, 512, 2048, 8
MESH = pl.DeviceIdType.MESH
FWD_C, BWD_C = 8, 4


def nt(a, b):
    return lax.dot_general(a, b, (((1,), (1,)), ((), ())), preferred_element_type=F32)


def nn(a, b):
    return lax.dot_general(a, b, (((1,), (0,)), ((), ())), preferred_element_type=F32)


def tn(a, b):
    return lax.dot_general(a, b, (((0,), (0,)), ((), ())), preferred_element_type=F32)


def lanes(shape):
    return lax.broadcasted_iota(jnp.int32, shape, len(shape) - 1)


def subs(shape):
    return lax.broadcasted_iota(jnp.int32, shape, len(shape) - 2)


def ds(start, size):
    if isinstance(start, int):
        return pl.ds(start, size)
    return pl.ds(pl.multiple_of(start, size), size)


def split3(x):
    a = x.astype(BF).astype(F32)
    b = (x - a).astype(BF).astype(F32)
    return a, b, (x - a - b).astype(BF).astype(F32)


def tile_of(r, t):
    return 8 * (r // 2) + jnp.where(r % 2 == 0, t, 7 - t)


def mean(x):
    return jnp.mean(x, axis=-1, keepdims=True)


def norm(x):
    centred = x - mean(x)
    factor = lax.rsqrt(mean(centred * centred) + 1e-05)
    return centred * factor, factor


def norm_back(dy, n, factor, gain):
    u = dy * gain
    return factor * (u - mean(u) - n * mean(u * n))


GELU_C = 0.7978845608028654


def gelu(x):
    return 0.5 * x * (1.0 + jnp.tanh(GELU_C * (x + 0.044715 * x * x * x)))


def gelu_slope(x):
    sq = x * x
    th = jnp.tanh(GELU_C * x * (1.0 + 0.044715 * sq))
    return 0.5 * (1.0 + th) + 0.5 * x * (1.0 - th * th) * (GELU_C * (1.0 + 3 * 0.044715 * sq))


class Place:
    def __init__(self):
        self.me = lax.axis_index("dp")
        self.s = lax.axis_index("section")
        me = self.me
        self.coords = (me % 4, me // 16, (me // 4) % 4)
        self.t = me % 4
        self.head = (me // 4) % 8
        self.micro = me // 32
        w = (me // 2) % 8
        low = w < 4
        self.own_t = jnp.where(low, w, 7 - w)
        self.own_slot = 4 * (me // 16) + jnp.where(low, 0, 2) + me % 2
        mine = self.micro == self.s
        self.self_kv = mine & (me % 2 == self.s)
        self.self_q = mine & (self.own_t == self.t)

    def along(self, axis, d):
        c = self.coords[axis]
        return self.me + ((c + d) % 4 - c) * (1, 16, 4)[axis]

    def chip(self, h, t):
        return (self.s * 8 + h) * 4 + t

    def send(self, src, dst, send_sem, recv_sem, section, dp):
        to_self = (section == self.s) & (dp == self.me)

        @pl.when(jnp.logical_not(to_self))
        def _():
            pltpu.make_async_remote_copy(
                src_ref=src,
                dst_ref=dst,
                send_sem=send_sem,
                recv_sem=recv_sem,
                device_id=(section, dp),
                device_id_type=MESH,
            ).start()

        @pl.when(to_self)
        def _():
            pltpu.make_async_copy(src, dst, recv_sem).start()


def wait_all(ref, sem):
    pltpu.make_async_copy(ref, ref, sem).wait()


def wait_sent(ref, sem, to_self, count):
    @pl.when(to_self)
    def _():
        wait_all(ref.at[pl.ds(0, count - 1)], sem)

    @pl.when(jnp.logical_not(to_self))
    def _():
        wait_all(ref.at[pl.ds(0, count)], sem)


def barrier(place):
    sem = pltpu.get_barrier_semaphore()

    @pl.loop(1, 128)
    def _(k):
        other = (place.s * 64 + place.me + k) % 128
        pl.semaphore_signal(sem, inc=1, device_id=(other // 64, other % 64), device_id_type=MESH)

    pl.semaphore_wait(sem, 127)


def project(v, r):
    hid = r.hid[v]
    q = nn(hid, r.w_query[...]).astype(BF).astype(F32) * 0.125
    k = nn(hid, r.w_key[...]).astype(BF).astype(F32)
    w = nn(hid, r.w_value[...]).astype(BF).astype(F32)
    ln = lanes((ROWS, 128))
    low = ln < 64
    aug = r.own_aug[...]
    for h in range(HEADS):
        cols = slice(128 * (h // 2), 128 * (h // 2) + 128)
        qt, kt, vt = q[:, cols], k[:, cols], w[:, cols]
        if h % 2 == 0:
            vt = pltpu.roll(vt, 64, 1)
        else:
            qt, kt = pltpu.roll(qt, 64, 1), pltpu.roll(kt, 64, 1)
        r.q_out[v, h] = jnp.where(low, qt, aug).astype(BF)
        r.kv_out[v, h] = jnp.where(low, kt, vt).astype(BF)


def send_qkv(v, r, place):
    @pl.loop(0, HEADS)
    def _(a):
        h = (place.me // 8 + a) % 8
        for b in range(4):
            place.send(
                r.kv_out.at[v, h],
                r.kv_in.at[v, place.me // 2],
                r.sems.at[0, v],
                r.sems.at[1, v],
                place.me % 2,
                place.chip(h, (place.me // 2 + b) % 4),
            )
        h = (place.own_slot // 2 + a) % 8
        for b in range(2):
            place.send(
                r.q_out.at[v, h],
                r.q_in.at[v, place.own_slot],
                r.sems.at[2, v],
                r.sems.at[3, v],
                (place.me + b) % 2,
                place.chip(h, place.own_t),
            )


def send_groups(r, place):
    r.grp_out[0] = jnp.broadcast_to(r.groups[pl.ds(place.s, 1), :], (8, 128))

    @pl.loop(0, HEADS)
    def _(a):
        h = (place.me // 8 + a) % 8
        for b in range(4):
            place.send(
                r.grp_out.at[0],
                r.grp_in.at[place.me // 2],
                r.gsems.at[0],
                r.gsems.at[1],
                place.me % 2,
                place.chip(h, (place.me // 2 + b) % 4),
            )


def column_of(row):
    return jnp.transpose(jnp.broadcast_to(row.astype(F32), (128, 128)))


def make_own_aug(r, place):
    ln = lanes((ROWS, 128))
    g = column_of(r.groups[pl.ds(place.s, 1), :]).astype(jnp.int32)
    r.own_aug[...] = jnp.where(ln - 64 == g, 1.0, 0.0)


def make_key_aug(r):
    ln = lanes((ROWS, 128))

    @pl.loop(0, 32)
    def _(n):
        g = column_of(r.grp_in[n][0:1, :]).astype(jnp.int32)
        inside = (ln >= 64) & (ln < 68)
        aug = jnp.where(inside, jnp.where(ln - 64 == g, 0.0, -BIG), 0.0)
        r.key_aug[n] = jnp.where((ln >= 68) & (ln < 71), 1.0, aug).astype(BF)


def make_kv(v, r):
    ln = lanes((ROWS, 128))
    low = ln < 64
    ones = jnp.where(ln < 3, 1.0, 0.0)

    @pl.loop(0, 32)
    def _(n):
        rows = ds(n * 128, 128)
        kv = r.kv_in[v, n].astype(F32)
        r.ka[v, rows, :] = jnp.where(low, kv, r.key_aug[n].astype(F32)).astype(BF)
        r.va[v, rows, :] = jnp.where(low, ones, kv).astype(BF)


def fwd_tile(v, i, r, place):
    width = FWD_C * 128
    u = tile_of(i, place.t)
    q = jnp.concatenate([r.q_in[v, 2 * i], r.q_in[v, 2 * i + 1]], axis=0)

    def step(c, carry, masked):
        top, acc = carry
        rows = ds(c * width, width)
        sc = nt(q, r.ka[v, rows, :])
        if masked:
            col, row = lanes((256, width)), subs((256, width))
            at = 256 * (col // 128) + col % 128 + (256 * FWD_C * c + 128 * place.s - 256 * u)
            sc = jnp.where(at <= row, sc, -BIG)
        new = jnp.maximum(top, jnp.max(sc, axis=1, keepdims=True))
        p = jnp.exp(sc - new).astype(BF)
        return new, acc * jnp.exp(top - new) + nn(p, r.va[v, rows, :])

    start = (jnp.full((256, 1), -2 * BIG, F32), jnp.zeros((256, 128), F32))
    full = u // FWD_C
    carry = lax.fori_loop(0, full, lambda c, x: step(c, x, False), start)
    top, acc = step(full, carry, True)
    total = acc[:, 0:1]
    a, b, c = split3(top + jnp.log(total))
    ln = lanes((256, 128))
    aux = jnp.where(ln == 0, a, jnp.where(ln == 1, b, jnp.where(ln == 2, c, 0.0)))
    out = jnp.where(ln >= 64, acc / total, aux).astype(BF)
    r.o_out[v, 2 * i] = out[:128]
    r.o_out[v, 2 * i + 1] = out[128:]
    for turn in range(2):
        half = (turn + place.s) % 2
        place.send(
            r.o_out.at[v, 2 * i + half],
            r.o_in.at[v, 2 * place.head + place.s],
            r.sems.at[4, v],
            r.sems.at[5, v],
            place.micro,
            2 * u + half,
        )


def after_attention(v, r):
    ln = lanes((ROWS, 128))
    low = ln < 64
    att = []
    for h in range(HEADS):
        parts = [r.o_in[v, 2 * h + core].astype(F32) for core in range(2)]
        logs = [x[:, 0:1] + x[:, 1:2] + x[:, 2:3] for x in parts]
        top = jnp.maximum(logs[0], logs[1])
        weights = [jnp.exp(x - top) for x in logs]
        total = weights[0] + weights[1]
        whole = (parts[0] * weights[0] + parts[1] * weights[1]) / total
        log_total = top + jnp.log(total)
        r.att[v, h] = jnp.where(low, jnp.where(ln == 0, log_total, 0.0), whole)
        att.append(whole)
    for i in range(HEADS // 2):
        pair = jnp.where(low, pltpu.roll(att[2 * i], 64, 1), att[2 * i + 1])
        r.att_low[v, :, 128 * i : 128 * i + 128] = pair.astype(BF)
    mixed = r.hid[v].astype(F32) + nn(r.att_low[v], r.w_out[...])
    n_one, f_one = norm(mixed)
    first = n_one * r.gain_one[...] + r.shift_one[...]
    first_low = first.astype(BF)
    r.n_one[v] = n_one
    r.f_one[v] = jnp.broadcast_to(f_one, (ROWS, 128))
    r.first_low[v] = first_low
    r.work[...] = first

    @pl.loop(0, 4)
    def _(j):
        cols = ds(j * 512, 512)
        pre = nn(r.first_low[v], r.w_up[:, cols])
        r.pre[v, :, cols] = pre
        act = gelu(pre).astype(BF)
        r.act[v, :, cols] = act
        r.work[...] += nn(act, r.w_down[cols, :])

    n_two, f_two = norm(r.work[...])
    r.n_two[v] = n_two
    r.f_two[v] = jnp.broadcast_to(f_two, (ROWS, 128))
    r.hid[v + 1] = (n_two * r.gain_two[...] + r.shift_two[...]).astype(BF)


def before_attention_back(v, r):
    dy = r.dy[...]
    n_two = r.n_two[v]
    r.vec_own[2:3, :] += jnp.sum(dy * n_two, axis=0, keepdims=True)
    r.vec_own[3:4, :] += jnp.sum(dy, axis=0, keepdims=True)
    grad_two = norm_back(dy, n_two, r.f_two[v][:, 0:1], r.gain_two[...])
    r.down_low[v] = grad_two.astype(BF)
    r.work[...] = grad_two

    @pl.loop(0, 4)
    def _(j):
        cols = ds(j * 512, 512)
        grad = nt(r.down_low[v], r.w_down[cols, :])
        up = (grad * gelu_slope(r.pre[v, :, cols])).astype(BF)
        r.up_low[v, :, cols] = up
        r.work[...] += nt(up, r.w_up[:, cols])

    dz = r.work[...]
    n_one = r.n_one[v]
    r.vec_own[0:1, :] += jnp.sum(dz * n_one, axis=0, keepdims=True)
    r.vec_own[1:2, :] += jnp.sum(dz, axis=0, keepdims=True)
    grad_one = norm_back(dz, n_one, r.f_one[v][:, 0:1], r.gain_one[...])
    out_low = grad_one.astype(BF)
    r.out_low[v] = out_low
    r.work[...] = grad_one
    grad_att = nt(out_low, r.w_out[...]).astype(BF).astype(F32)
    ln = lanes((ROWS, 128))
    low = ln < 64
    for h in range(HEADS):
        tile = grad_att[:, 128 * (h // 2) : 128 * (h // 2) + 128]
        if h % 2 == 0:
            tile = pltpu.roll(tile, 64, 1)
        att = r.att[v, h]
        delta = jnp.sum(jnp.where(low, 0.0, tile * att), axis=1, keepdims=True)
        parts = split3(-delta) + split3(-att[:, 0:1])
        aux = jnp.zeros((ROWS, 128), F32)
        for i, part in enumerate(parts):
            aux = jnp.where(ln == i, part, aux)
        r.do_out[v, h] = jnp.where(low, aux, tile).astype(BF)


def send_do(v, r, place):
    @pl.loop(0, HEADS)
    def _(a):
        h = (place.own_slot // 2 + a) % 8
        for b in range(2):
            place.send(
                r.do_out.at[v, h],
                r.do_in.at[v, place.own_slot],
                r.sems.at[6, v],
                r.sems.at[7, v],
                (place.me + b) % 2,
                place.chip(h, place.own_t),
            )


def bwd_tile(v, i, r, place):
    width = BWD_C * 128
    u = tile_of(i, place.t)
    q = jnp.concatenate([r.q_in[v, 2 * i], r.q_in[v, 2 * i + 1]], axis=0).astype(F32)
    do = jnp.concatenate([r.do_in[v, 2 * i], r.do_in[v, 2 * i + 1]], axis=0).astype(F32)
    ln = lanes((256, 128))
    lq = jnp.where((ln >= 68) & (ln < 71), pltpu.roll(do, 65, 1), q).astype(BF)
    ld = jnp.where((ln >= 3) & (ln < 64), 0.0, do).astype(BF)
    qz = jnp.where(ln < 64, q, 0.0).astype(BF)
    dz = jnp.where(ln >= 64, do, 0.0).astype(BF)

    def step(c, dqt, masked):
        rows = ds(c * width, width)
        x = nt(r.ka[v, rows, :], lq)
        if masked:
            row, col = subs((width, 256)), lanes((width, 256))
            at = 256 * (row // 128) + row % 128 + (256 * BWD_C * c + 128 * place.s - 256 * u)
            x = jnp.where(at <= col, x, -BIG)
        p = jnp.exp(x)
        dp = nt(r.va[v, rows, :], ld)
        dsc = (p * dp).astype(BF)
        r.dkv_acc[rows, :] += nn(dsc, qz) + nn(p.astype(BF), dz)
        return dqt + nn(r.kat[:, rows], dsc)

    full = u // BWD_C
    dqt = lax.fori_loop(0, full, lambda c, x: step(c, x, False), jnp.zeros((64, 256), F32))
    dqt = step(full, dqt, True)
    dq = jnp.transpose(jnp.concatenate([dqt, jnp.zeros((64, 256), F32)], axis=0)).astype(BF)
    r.dq_out[v, 2 * i] = dq[:128]
    r.dq_out[v, 2 * i + 1] = dq[128:]
    for turn in range(2):
        half = (turn + place.s) % 2
        place.send(
            r.dq_out.at[v, 2 * i + half],
            r.dq_in.at[v, 2 * place.head + place.s],
            r.sems.at[8, v],
            r.sems.at[9, v],
            place.micro,
            2 * u + half,
        )


def attention_back(v, r, place):
    r.dkv_acc[...] = jnp.zeros_like(r.dkv_acc)

    @pl.loop(0, 8)
    def _(i):
        rows = ds(i * 512, 512)
        r.kat[:, rows] = jnp.transpose(r.ka[v, rows, :].astype(F32))[:64].astype(BF)

    @pl.loop(0, 8)
    def _(i):
        bwd_tile(v, (i + place.head) % 8, r, place)
        for after, step in SUM_DURING_BACK:

            @pl.when((v == 0) & (i == after))
            def _():
                SUM_STEPS[step](0, r, place)

    @pl.loop(0, 32)
    def _(k):
        n = (k + 4 * place.head + place.t) % 32
        r.dkv_out[v, n] = r.dkv_acc[ds(n * 128, 128), :].astype(BF)
        place.send(
            r.dkv_out.at[v, n],
            r.dkv_in.at[v, 4 * place.head + place.t],
            r.sems.at[10, v],
            r.sems.at[11, v],
            place.micro,
            2 * n + place.s,
        )


def after_attention_back(v, r):
    ln = lanes((ROWS, 128))
    low = ln < 64
    for i in range(HEADS // 2):
        cols = slice(128 * i, 128 * i + 128)
        dq, dkv = [], []
        for h in (2 * i, 2 * i + 1):
            both = r.dq_in[v, 2 * h].astype(F32) + r.dq_in[v, 2 * h + 1].astype(F32)
            dq.append(both * 0.125)
            four = [r.dkv_in[v, 4 * h + t].astype(F32) for t in range(4)]
            dkv.append((four[0] + four[1]) + (four[2] + four[3]))
        r.dq[v, :, cols] = jnp.where(low, dq[0], pltpu.roll(dq[1], 64, 1)).astype(BF)
        r.dk[v, :, cols] = jnp.where(low, dkv[0], pltpu.roll(dkv[1], 64, 1)).astype(BF)
        r.dv[v, :, cols] = jnp.where(low, pltpu.roll(dkv[0], 64, 1), dkv[1]).astype(BF)
    r.work[...] += (
        nt(r.dq[v], r.w_query[...]) + nt(r.dk[v], r.w_key[...]) + nt(r.dv[v], r.w_value[...])
    )


def both(ref):
    return jnp.concatenate([ref[0], ref[1]], axis=0)


def put(ref, unit, tile):
    ref[ds(unit * 512, 512), :] = tile.astype(BF)


def weight_grads_early(r):
    @pl.loop(0, 4)
    def _(j):
        cols = ds(j * 512, 512)
        up = jnp.concatenate([r.up_low[0, :, cols], r.up_low[1, :, cols]], axis=0)
        grad = tn(both(r.first_low), up)
        for k in range(4):
            put(r.sum_in0, 4 * j + k, grad[:, 128 * k : 128 * k + 128])
        act = jnp.concatenate([r.act[0, :, cols], r.act[1, :, cols]], axis=0)
        grad = tn(act, both(r.down_low))
        for k in range(4):
            put(r.sum_in0, 16 + 4 * k + j, grad[:, 128 * k : 128 * k + 128])

    grad = tn(both(r.att_low), both(r.out_low))
    for k in range(4):
        put(r.sum_in0, 32 + k, grad[:, 128 * k : 128 * k + 128])


def weight_grads_late(r):
    hid = jnp.concatenate([r.hid[0], r.hid[1]], axis=0)
    for i, ref in enumerate((r.dq, r.dk, r.dv)):
        grad = tn(hid, both(ref))
        for k in range(4):
            put(r.sum_in1, 4 * i + k, grad[:, 128 * k : 128 * k + 128])


SUM_ROWS = (3072, 1024)
ORDERS = ((0, 1, 2), (1, 2, 0), (2, 0, 1))


def sum_refs(g, r):
    names = ("in", "x", "r0", "r1", "r2", "s0", "s1", "t", "sems")
    return SimpleNamespace(**{n: getattr(r, "sum_" + n + str(g)) for n in names})


def remote(src, dst, send_sem, recv_sem, section, dp):
    pltpu.make_async_remote_copy(
        src_ref=src,
        dst_ref=dst,
        send_sem=send_sem,
        recv_sem=recv_sem,
        device_id=(section, dp),
        device_id_type=MESH,
    ).start()


def offsets(p, rows, place):
    out, at = [], 0
    for k in range(3):
        at = at + place.coords[ORDERS[p][k]] * (rows // 4 ** (k + 1))
        out.append(at)
    return out


def exchange_start(g, r, place):
    q, rows = sum_refs(g, r), SUM_ROWS[g]
    for p in range(3):
        remote(
            q.__dict__["in"].at[ds((1 - place.s) * 3 * rows + p * rows, rows)],
            q.x.at[pl.ds(p * rows, rows)],
            q.sems.at[0, 0, p],
            q.sems.at[1, 0, p],
            1 - place.s,
            place.me,
        )


def scatter_send(g, p, k, src, base, q, place):
    size = SUM_ROWS[g] // 4 ** (k + 1)
    dst = (q.r0, q.r1, q.r2)[k]
    axis = ORDERS[p][k]
    for d in (2, 1, 3):
        c = (place.coords[axis] + d) % 4
        remote(
            src.at[ds(base + c * size, size)],
            dst.at[p, d - 1],
            q.sems.at[0, 1 + k, p],
            q.sems.at[1, 1 + k, p],
            place.s,
            place.along(axis, d),
        )


def exchange_done(g, r, place):
    q, rows = sum_refs(g, r), SUM_ROWS[g]
    src = q.__dict__["in"]
    for p in range(3):
        base = place.s * 3 * rows + p * rows
        wait_all(q.x.at[pl.ds(p * rows, rows)], q.sems.at[1, 0, p])

        @pl.loop(0, rows // 512)
        def _(k):
            at = ds(base + k * 512, 512)
            other = q.x[ds(p * rows + k * 512, 512), :]
            src[at, :] = (src[at, :].astype(F32) + other.astype(F32)).astype(BF)

        scatter_send(g, p, 0, src, base, q, place)


def scatter_done(k, g, r, place):
    q, rows = sum_refs(g, r), SUM_ROWS[g]
    size = rows // 4 ** (k + 1)
    got = (q.r0, q.r1, q.r2)[k]
    for p in range(3):
        wait_all(got.at[p], q.sems.at[1, 1 + k, p])
        c = place.coords[ORDERS[p][k]]
        if k == 0:
            own = q.__dict__["in"][ds(place.s * 3 * rows + p * rows + c * size, size), :]
        else:
            own = (q.s0, q.s1)[k - 1][p, ds(c * size, size), :]
        total = own.astype(F32)
        for d in range(3):
            total = total + got[p, d].astype(F32)
        if k < 2:
            dst = (q.s0, q.s1)[k]
            dst[p] = total.astype(BF)
            scatter_send(g, p, k + 1, dst.at[p], 0, q, place)
        else:
            q.t[place.s, p, ds(offsets(p, rows, place)[2], size), :] = total.astype(BF)
            gather_send(g, p, 2, q, place)


def gather_send(g, p, k, q, place):
    rows = SUM_ROWS[g]
    size = rows // 4 ** (k + 1)
    block = q.t.at[place.s, p, ds(offsets(p, rows, place)[k], size)]
    axis = ORDERS[p][k]
    for d in (2, 1, 3):
        sem = 4 + k if k else 6 + d
        remote(
            block, block, q.sems.at[0, sem, p], q.sems.at[1, sem, p], place.s, place.along(axis, d)
        )


def cross_send(p, start, size, q, place):
    block = q.t.at[place.s, p, ds(start, size)]
    remote(block, block, q.sems.at[0, 4, p], q.sems.at[1, 4, p], 1 - place.s, place.me)


def gather_done(k, g, r, place):
    q, rows = sum_refs(g, r), SUM_ROWS[g]
    for p in range(3):
        wait_all(
            q.t.at[0, p, pl.ds(0, 3 * rows // 4 ** (k + 1))],
            q.sems.at[1, 4 + k, p],
        )
        gather_send(g, p, k - 1, q, place)
        if k == 1:
            cross_send(p, offsets(p, rows, place)[0], rows // 4, q, place)


def gather_last(g, r, place):
    q, rows = sum_refs(g, r), SUM_ROWS[g]
    size = rows // 4
    for d in (1, 3, 2):
        for p in range(3):
            wait_all(q.t.at[0, p, pl.ds(0, size)], q.sems.at[1, 6 + d, p])
            c = (place.coords[ORDERS[p][0]] - d + 4) % 4
            cross_send(p, c * size, size, q, place)


def sum_out(g, r, place):
    q = sum_refs(g, r)
    for p in range(3):
        wait_all(q.t.at[0, p], q.sems.at[1, 4, p])
    pltpu.make_async_copy(q.t, (r.sums0, r.sums1)[g], r.vsems.at[2, g]).start()


def sum_drain(g, r, place):
    q, rows = sum_refs(g, r), SUM_ROWS[g]
    for p in range(3):
        wait_all(q.x.at[pl.ds(0, rows)], q.sems.at[0, 0, p])
        for k in range(3):
            wait_all(q.t.at[0, p, pl.ds(0, 3 * rows // 4 ** (k + 1))], q.sems.at[0, 1 + k, p])
        for k in (1, 2):
            wait_all(q.t.at[0, p, pl.ds(0, 3 * rows // 4 ** (k + 1))], q.sems.at[0, 4 + k, p])
        for d in range(1, 4):
            wait_all(q.t.at[0, p, pl.ds(0, rows // 4)], q.sems.at[0, 6 + d, p])
        wait_all(q.t.at[0, p], q.sems.at[0, 4, p])
    pltpu.make_async_copy(q.t, (r.sums0, r.sums1)[g], r.vsems.at[2, g]).wait()


def vec_exchange(r, place):
    remote(r.vec_own, r.vec_x, r.vsems.at[0, 0], r.vsems.at[1, 0], 1 - place.s, place.me)


def vec_send(axis, r, place):
    c = place.coords[axis]
    for d in (1, 2, 3):
        remote(
            r.vec_in.at[axis, c],
            r.vec_in.at[axis, c],
            r.vsems.at[0, 1 + axis],
            r.vsems.at[1, 1 + axis],
            place.s,
            place.along(axis, d),
        )


def vec_step(axis, r, place):
    if axis == 0:
        wait_all(r.vec_x, r.vsems.at[1, 0])
        total = r.vec_own[...] + r.vec_x[...]
    else:
        wait_all(r.vec_in.at[axis - 1, pl.ds(0, 3)], r.vsems.at[1, axis])
        total = (r.vec_in[axis - 1, 0] + r.vec_in[axis - 1, 1]) + (
            r.vec_in[axis - 1, 2] + r.vec_in[axis - 1, 3]
        )
    if axis < 3:
        r.vec_in[axis, place.coords[axis]] = total
        vec_send(axis, r, place)
    else:
        r.vec[...] = total


def vec_drain(r):
    wait_all(r.vec_x, r.vsems.at[0, 0])
    for axis in range(3):
        wait_all(r.vec_in.at[axis, pl.ds(0, 3)], r.vsems.at[0, 1 + axis])


def step_exchange(g, r, place):
    exchange_start(g, r, place)
    if g == 0:
        vec_exchange(r, place)


def step_scatter(g, r, place):
    exchange_done(g, r, place)
    if g == 0:
        vec_step(0, r, place)


def step_between(k, g, r, place):
    scatter_done(k, g, r, place)
    if g == 0:
        vec_step(k + 1, r, place)


SUM_STEPS = (
    step_exchange,
    step_scatter,
    lambda *a: step_between(0, *a),
    lambda *a: step_between(1, *a),
    lambda *a: step_between(2, *a),
    lambda *a: gather_done(2, *a),
    lambda *a: gather_done(1, *a),
    gather_last,
    sum_out,
)
SUM_DURING_BACK = ((1, 1), (4, 2), (5, 3), (6, 4), (7, 5))


INPUTS = ["inputs", "groups", "cotangent", "w_query", "w_key", "w_value", "w_out", "w_up", "w_down"]
INPUTS += ["gain_one", "shift_one", "gain_two", "shift_two"]
OUTPUTS = {
    "output": ((1, ROWS, D), BF),
    "input_grad": ((1, ROWS, D), BF),
    "sums0": ((2, 3, 3072, 128), BF),
    "sums1": ((2, 3, 1024, 128), BF),
    "vec": ((8, D), F32),
}
SCRATCH = {
    "hid": ((3, ROWS, D), BF),
    "own_aug": ((ROWS, 128), F32),
    "q_out": ((2, 8, ROWS, 128), BF),
    "kv_out": ((2, 8, ROWS, 128), BF),
    "q_in": ((2, 16, ROWS, 128), BF),
    "kv_in": ((2, 32, ROWS, 128), BF),
    "grp_out": ((1, 8, 128), jnp.int32),
    "grp_in": ((32, 8, 128), jnp.int32),
    "key_aug": ((32, ROWS, 128), BF),
    "ka": ((2, 4096, 128), BF),
    "va": ((2, 4096, 128), BF),
    "kat": ((64, 4096), BF),
    "o_out": ((2, 16, ROWS, 128), BF),
    "o_in": ((2, 16, ROWS, 128), BF),
    "att": ((2, 8, ROWS, 128), F32),
    "att_low": ((2, ROWS, D), BF),
    "n_one": ((2, ROWS, D), F32),
    "f_one": ((2, ROWS, 128), F32),
    "first_low": ((2, ROWS, D), BF),
    "pre": ((2, ROWS, FF), F32),
    "act": ((2, ROWS, FF), BF),
    "n_two": ((2, ROWS, D), F32),
    "f_two": ((2, ROWS, 128), F32),
    "work": ((ROWS, D), F32),
    "dy": ((ROWS, D), F32),
    "down_low": ((2, ROWS, D), BF),
    "up_low": ((2, ROWS, FF), BF),
    "out_low": ((2, ROWS, D), BF),
    "do_out": ((2, 8, ROWS, 128), BF),
    "do_in": ((2, 16, ROWS, 128), BF),
    "dq_out": ((2, 16, ROWS, 128), BF),
    "dq_in": ((2, 16, ROWS, 128), BF),
    "dkv_acc": ((4096, 128), F32),
    "dkv_out": ((2, 32, ROWS, 128), BF),
    "dkv_in": ((2, 32, ROWS, 128), BF),
    "dq": ((2, ROWS, D), BF),
    "dk": ((2, ROWS, D), BF),
    "dv": ((2, ROWS, D), BF),
    "vec_own": ((8, D), F32),
    "vec_x": ((8, D), F32),
    "vec_in": ((3, 4, 8, D), F32),
}
for g, rows in enumerate(SUM_ROWS):
    SCRATCH |= {
        f"sum_in{g}": ((6 * rows, 128), BF),
        f"sum_x{g}": ((3 * rows, 128), BF),
        f"sum_r0{g}": ((3, 3, rows // 4, 128), BF),
        f"sum_r1{g}": ((3, 3, rows // 16, 128), BF),
        f"sum_r2{g}": ((3, 3, rows // 64, 128), BF),
        f"sum_s0{g}": ((3, rows // 4, 128), BF),
        f"sum_s1{g}": ((3, rows // 16, 128), BF),
        f"sum_t{g}": ((2, 3, rows, 128), BF),
    }
SEMS = {"sems": (12, 2), "gsems": (2,), "sum_sems0": (2, 10, 3), "sum_sems1": (2, 10, 3), "vsems": (3, 4)}


def kernel(*refs):
    names = INPUTS + list(OUTPUTS) + list(SCRATCH) + list(SEMS)
    r = SimpleNamespace(**dict(zip(names, refs)))
    place = Place()
    barrier(place)
    send_groups(r, place)
    make_own_aug(r, place)
    r.vec_own[...] = jnp.zeros_like(r.vec_own)
    r.hid[0] = r.inputs[place.s]

    @pl.loop(0, 2)
    def _(v):
        project(v, r)
        send_qkv(v, r, place)

        @pl.when(v == 0)
        def _():
            wait_all(r.grp_in, r.gsems.at[1])
            make_key_aug(r)

        wait_all(r.kv_in.at[v], r.sems.at[1, v])
        make_kv(v, r)
        wait_all(r.q_in.at[v], r.sems.at[3, v])

        @pl.loop(0, 8)
        def _(i):
            fwd_tile(v, (i + place.head) % 8, r, place)

        wait_all(r.o_in.at[v], r.sems.at[5, v])
        after_attention(v, r)

    r.output[0] = r.hid[2]
    r.dy[...] = r.cotangent[place.s].astype(F32)

    @pl.loop(0, 2)
    def _(step):
        v = 1 - step
        before_attention_back(v, r)
        send_do(v, r, place)

        @pl.when(v == 0)
        def _():
            weight_grads_early(r)
            SUM_STEPS[0](0, r, place)

        wait_all(r.do_in.at[v], r.sems.at[7, v])
        attention_back(v, r, place)

        @pl.when(v == 0)
        def _():
            SUM_STEPS[6](0, r, place)

        wait_all(r.dq_in.at[v], r.sems.at[9, v])
        wait_all(r.dkv_in.at[v], r.sems.at[11, v])
        after_attention_back(v, r)
        r.dy[...] = r.work[...].astype(BF).astype(F32)

    r.input_grad[0] = r.dy[...].astype(BF)
    weight_grads_late(r)
    SUM_STEPS[0](1, r, place)
    SUM_STEPS[7](0, r, place)
    for step in SUM_STEPS[1:5]:
        step(1, r, place)
    SUM_STEPS[8](0, r, place)
    for step in SUM_STEPS[5:]:
        step(1, r, place)

    vec_drain(r)
    for g in range(2):
        sum_drain(g, r, place)
    wait_sent(r.grp_in, r.gsems.at[0], place.self_kv, 32)

    @pl.loop(0, 2)
    def _(v):
        wait_sent(r.kv_in.at[v], r.sems.at[0, v], place.self_kv, 32)
        wait_sent(r.q_in.at[v], r.sems.at[2, v], place.self_q, 16)
        wait_sent(r.o_in.at[v], r.sems.at[4, v], place.self_q, 16)
        wait_sent(r.do_in.at[v], r.sems.at[6, v], place.self_q, 16)
        wait_sent(r.dq_in.at[v], r.sems.at[8, v], place.self_q, 16)
        wait_sent(r.dkv_in.at[v], r.sems.at[10, v], place.self_kv, 32)


def on_device(inputs, groups, cotangent, *params):
    vectors = [x.reshape(1, D) for x in params[6:]]
    vmem = pl.BlockSpec(memory_space=pltpu.VMEM)
    out = pl.pallas_call(
        kernel,
        out_shape=[jax.ShapeDtypeStruct(shape, kind) for shape, kind in OUTPUTS.values()],
        in_specs=[vmem] * len(INPUTS),
        out_specs=[
            pl.BlockSpec(memory_space=pl.ANY) if n.startswith("sums") else vmem for n in OUTPUTS
        ],
        scratch_shapes=[pltpu.VMEM(shape, kind) for shape, kind in SCRATCH.values()]
        + [pltpu.SemaphoreType.DMA(shape) for shape in SEMS.values()],
        compiler_params=pltpu.CompilerParams(
            collective_id=0, has_side_effects=True, vmem_limit_bytes=60 * 2**20
        ),
        name="visits",
    )(inputs, groups, cotangent, *params[:6], *vectors)
    early, late = out[2].reshape(36, 512, 128), out[3].reshape(12, 512, 128)

    def whole(tiles):
        return tiles.transpose(1, 0, 2).reshape(tiles.shape[1], -1).astype(F32)

    down = early[16:32].reshape(4, FF, 128)
    grads = [whole(x) for x in (late[:4], late[4:8], late[8:], early[32:], early[:16], down)]
    vec = out[4]
    return (*out[:2], *grads, vec[0], vec[1], vec[2], vec[3])


def solution(mesh):
    rows = P(None, "dp", None)
    return jax.shard_map(
        on_device,
        mesh=mesh,
        in_specs=(rows, P(None, "dp"), rows) + (P(),) * 10,
        out_specs=(P("section", "dp", None),) * 2 + (P(),) * 10,
        check_vma=False,
    )
```

```python
from types import SimpleNamespace

import jax
import jax.numpy as jnp
from jax import lax
from jax.experimental import pallas as pl
from jax.experimental.pallas import tpu as pltpu
from jax.sharding import PartitionSpec as P

F32, BF = jnp.float32, jnp.bfloat16
BIG = 1e30
ROWS, D, FF, HEADS = 128, 512, 2048, 8
MESH = pl.DeviceIdType.MESH
BWD_C = 4


def nt(a, b):
    return lax.dot_general(a, b, (((1,), (1,)), ((), ())), preferred_element_type=F32)


def nn(a, b):
    return lax.dot_general(a, b, (((1,), (0,)), ((), ())), preferred_element_type=F32)


def tn(a, b):
    return lax.dot_general(a, b, (((0,), (0,)), ((), ())), preferred_element_type=F32)


def lanes(shape):
    return lax.broadcasted_iota(jnp.int32, shape, len(shape) - 1)


def subs(shape):
    return lax.broadcasted_iota(jnp.int32, shape, len(shape) - 2)


def ds(start, size):
    if isinstance(start, int):
        return pl.ds(start, size)
    return pl.ds(pl.multiple_of(start, size), size)


def split3(x):
    a = x.astype(BF).astype(F32)
    b = (x - a).astype(BF).astype(F32)
    return a, b, (x - a - b).astype(BF).astype(F32)


def tile_of(r, t):
    return 4 * r + (r + t) % 4


def mean(x):
    return jnp.mean(x, axis=-1, keepdims=True)


def norm(x):
    centred = x - mean(x)
    factor = lax.rsqrt(mean(centred * centred) + 1e-05)
    return centred * factor, factor


def norm_back(dy, n, factor, gain):
    u = dy * gain
    return factor * (u - mean(u) - n * mean(u * n))


GELU_C = 0.7978845608028654


def gelu(x):
    return 0.5 * x * (1.0 + jnp.tanh(GELU_C * (x + 0.044715 * x * x * x)))


def gelu_slope(x):
    sq = x * x
    th = jnp.tanh(GELU_C * x * (1.0 + 0.044715 * sq))
    return 0.5 * (1.0 + th) + 0.5 * x * (1.0 - th * th) * (GELU_C * (1.0 + 3 * 0.044715 * sq))


class Place:
    def __init__(self):
        self.me = lax.axis_index("dp")
        self.s = lax.axis_index("section")
        me = self.me
        self.coords = (me % 4, me // 16, (me // 4) % 4)
        x, y, z = self.coords
        self.t = (x + y + z) % 4
        self.head = 4 * (y % 2) + x
        self.micro = y // 2
        self.own_t = ((me // 2) % 4 - me // 8 + 32) % 4
        self.own_slot = 2 * (me // 8) + me % 2
        mine = self.micro == self.s
        self.self_kv = mine & (me % 2 == self.s)
        self.self_q = mine & (self.own_t == self.t)

    def along(self, axis, d):
        c = self.coords[axis]
        return self.me + ((c + d) % 4 - c) * (1, 16, 4)[axis]

    def chip(self, h, t):
        x, y = h % 4, 2 * self.s + h // 4
        return 16 * y + 4 * ((t - x - y + 8) % 4) + x

    def send(self, src, dst, send_sem, recv_sem, section, dp):
        to_self = (section == self.s) & (dp == self.me)

        @pl.when(jnp.logical_not(to_self))
        def _():
            pltpu.make_async_remote_copy(
                src_ref=src,
                dst_ref=dst,
                send_sem=send_sem,
                recv_sem=recv_sem,
                device_id=(section, dp),
                device_id_type=MESH,
            ).start()

        @pl.when(to_self)
        def _():
            pltpu.make_async_copy(src, dst, recv_sem).start()


def wait_all(ref, sem):
    pltpu.make_async_copy(ref, ref, sem).wait()


def wait_sent(ref, sem, to_self, count):
    @pl.when(to_self)
    def _():
        wait_all(ref.at[pl.ds(0, count - 1)], sem)

    @pl.when(jnp.logical_not(to_self))
    def _():
        wait_all(ref.at[pl.ds(0, count)], sem)


def barrier(place):
    sem = pltpu.get_barrier_semaphore()

    @pl.loop(1, 128)
    def _(k):
        other = (place.s * 64 + place.me + k) % 128
        pl.semaphore_signal(sem, inc=1, device_id=(other // 64, other % 64), device_id_type=MESH)

    pl.semaphore_wait(sem, 127)


def project(v, r):
    hid = r.hid[v]
    q = nn(hid, r.w_query[...]).astype(BF).astype(F32) * 0.125
    k = nn(hid, r.w_key[...]).astype(BF).astype(F32)
    w = nn(hid, r.w_value[...]).astype(BF).astype(F32)
    ln = lanes((ROWS, 128))
    low = ln < 64
    aug = r.own_aug[...]
    for h in range(HEADS):
        cols = slice(128 * (h // 2), 128 * (h // 2) + 128)
        qt, kt, vt = q[:, cols], k[:, cols], w[:, cols]
        if h % 2 == 0:
            vt = pltpu.roll(vt, 64, 1)
        else:
            qt, kt = pltpu.roll(qt, 64, 1), pltpu.roll(kt, 64, 1)
        r.q_out[v, h] = jnp.where(low, qt, aug).astype(BF)
        r.kv_out[v, h] = jnp.where(low, kt, vt).astype(BF)


def send_qkv(v, r, place):
    @pl.loop(0, HEADS)
    def _(a):
        h = (place.me // 8 + a) % 8
        for b in range(4):
            place.send(
                r.kv_out.at[v, h],
                r.kv_in.at[v, place.me // 2],
                r.sems.at[0, v],
                r.sems.at[1, v],
                place.me % 2,
                place.chip(h, (place.me // 2 + b) % 4),
            )
        h = (place.me // 4 + a) % 8
        for b in range(2):
            place.send(
                r.q_out.at[v, h],
                r.q_in.at[v, place.own_slot],
                r.sems.at[2, v],
                r.sems.at[3, v],
                (place.me + b) % 2,
                place.chip(h, place.own_t),
            )


def send_groups(r, place):
    r.grp_out[0] = jnp.broadcast_to(r.groups[pl.ds(place.s, 1), :], (8, 128))

    @pl.loop(0, HEADS)
    def _(a):
        h = (place.me // 8 + a) % 8
        for b in range(4):
            place.send(
                r.grp_out.at[0],
                r.grp_in.at[place.me // 2],
                r.gsems.at[0],
                r.gsems.at[1],
                place.me % 2,
                place.chip(h, (place.me // 2 + b) % 4),
            )


def column_of(row):
    return jnp.transpose(jnp.broadcast_to(row.astype(F32), (128, 128)))


def make_own_aug(r, place):
    ln = lanes((ROWS, 128))
    g = column_of(r.groups[pl.ds(place.s, 1), :]).astype(jnp.int32)
    r.own_aug[...] = jnp.where(ln - 64 == g, 1.0, 0.0)


def make_key_aug(r):
    ln = lanes((ROWS, 128))

    @pl.loop(0, 32)
    def _(n):
        g = column_of(r.grp_in[n][0:1, :]).astype(jnp.int32)
        inside = (ln >= 64) & (ln < 68)
        aug = jnp.where(inside, jnp.where(ln - 64 == g, 0.0, -BIG), 0.0)
        aug = jnp.where((ln >= 68) & (ln < 71), 1.0, aug).astype(BF)
        for v in range(2):
            r.ka[v, ds(n * 128, 128), :] = aug


def make_kv(v, r):
    ln = lanes((ROWS, 128))
    low = ln < 64
    ones = jnp.where(ln < 3, 1.0, 0.0)

    @pl.loop(0, 32)
    def _(n):
        rows = ds(n * 128, 128)
        kv = r.kv_in[v, n].astype(F32)
        r.ka[v, rows, :] = jnp.where(low, kv, r.ka[v, rows, :].astype(F32)).astype(BF)
        r.va[v, rows, :] = jnp.where(low, ones, kv).astype(BF)


def fwd_pair(v, j, r, place):
    width = 1024
    tiles = [tile_of(2 * j + k, place.t) for k in range(2)]
    q = jnp.concatenate([r.q_in[v, 4 * j + k] for k in range(4)], axis=0)

    def step(c, carry, masked):
        top, acc = carry
        rows = ds(c * width, width)
        sc = nt(q, r.ka[v, rows, :])
        if masked:
            col, row = lanes((512, width)), subs((512, width))
            at = 256 * (col // 128) + col % 128 + (2048 * c + 128 * place.s)
            limit = row % 256 + 256 * jnp.where(row < 256, tiles[0], tiles[1])
            sc = jnp.where(at <= limit, sc, -BIG)
        new = jnp.maximum(top, jnp.max(sc, axis=1, keepdims=True))
        p = jnp.exp(sc - new).astype(BF)
        return new, acc * jnp.exp(top - new) + nn(p, r.va[v, rows, :])

    start = (jnp.full((512, 1), -2 * BIG, F32), jnp.zeros((512, 128), F32))
    carry = lax.fori_loop(0, j, lambda c, x: step(c, x, False), start)
    top, acc = step(j, carry, True)
    total = acc[:, 0:1]
    a, b, c = split3(top + jnp.log(total))
    ln = lanes((512, 128))
    aux = jnp.where(ln == 0, a, jnp.where(ln == 1, b, jnp.where(ln == 2, c, 0.0)))
    out = jnp.where(ln >= 64, acc / total, aux).astype(BF)
    for k in range(4):
        r.o_out[v, 4 * j + k] = out[128 * k : 128 * k + 128]
    for k in range(2):
        for turn in range(2):
            half = (turn + place.s) % 2
            place.send(
                r.o_out.at[v, 4 * j + 2 * k + half],
                r.o_in.at[v, 2 * place.head + place.s],
                r.sems.at[4, v],
                r.sems.at[5, v],
                place.micro,
                2 * tiles[k] + half,
            )


def after_attention(v, r):
    ln = lanes((ROWS, 128))
    low = ln < 64
    att = []
    for h in range(HEADS):
        parts = [r.o_in[v, 2 * h + core].astype(F32) for core in range(2)]
        logs = [x[:, 0:1] + x[:, 1:2] + x[:, 2:3] for x in parts]
        top = jnp.maximum(logs[0], logs[1])
        weights = [jnp.exp(x - top) for x in logs]
        total = weights[0] + weights[1]
        whole = (parts[0] * weights[0] + parts[1] * weights[1]) / total
        log_total = top + jnp.log(total)
        r.att[v, h] = jnp.where(low, jnp.where(ln == 0, log_total, 0.0), whole)
        att.append(whole)
    for i in range(HEADS // 2):
        pair = jnp.where(low, pltpu.roll(att[2 * i], 64, 1), att[2 * i + 1])
        r.att_low[v, :, 128 * i : 128 * i + 128] = pair.astype(BF)
    mixed = r.hid[v].astype(F32) + nn(r.att_low[v], r.w_out[...])
    n_one, f_one = norm(mixed)
    first = n_one * r.gain_one[...] + r.shift_one[...]
    first_low = first.astype(BF)
    r.n_one[v] = n_one
    r.f_one[v] = jnp.broadcast_to(f_one, (ROWS, 128))
    r.first_low[v] = first_low
    r.work[...] = first

    @pl.loop(0, 4)
    def _(j):
        cols = ds(j * 512, 512)
        pre = nn(r.first_low[v], r.w_up[:, cols])
        r.pre[v, :, cols] = pre
        act = gelu(pre).astype(BF)
        r.act[v, :, cols] = act
        r.work[...] += nn(act, r.w_down[cols, :])

    n_two, f_two = norm(r.work[...])
    r.n_two[v] = n_two
    r.f_two[v] = jnp.broadcast_to(f_two, (ROWS, 128))
    r.hid[v + 1] = (n_two * r.gain_two[...] + r.shift_two[...]).astype(BF)


def before_attention_back(v, r):
    dy = r.dy[...]
    n_two = r.n_two[v]
    r.vec_own[2:3, :] += jnp.sum(dy * n_two, axis=0, keepdims=True)
    r.vec_own[3:4, :] += jnp.sum(dy, axis=0, keepdims=True)
    grad_two = norm_back(dy, n_two, r.f_two[v][:, 0:1], r.gain_two[...])
    r.down_low[v] = grad_two.astype(BF)
    r.work[...] = grad_two

    @pl.loop(0, 4)
    def _(j):
        cols = ds(j * 512, 512)
        grad = nt(r.down_low[v], r.w_down[cols, :])
        up = (grad * gelu_slope(r.pre[v, :, cols])).astype(BF)
        r.up_low[v, :, cols] = up
        r.work[...] += nt(up, r.w_up[:, cols])

    dz = r.work[...]
    n_one = r.n_one[v]
    r.vec_own[0:1, :] += jnp.sum(dz * n_one, axis=0, keepdims=True)
    r.vec_own[1:2, :] += jnp.sum(dz, axis=0, keepdims=True)
    grad_one = norm_back(dz, n_one, r.f_one[v][:, 0:1], r.gain_one[...])
    out_low = grad_one.astype(BF)
    r.out_low[v] = out_low
    r.work[...] = grad_one
    grad_att = nt(out_low, r.w_out[...]).astype(BF).astype(F32)
    ln = lanes((ROWS, 128))
    low = ln < 64
    for h in range(HEADS):
        tile = grad_att[:, 128 * (h // 2) : 128 * (h // 2) + 128]
        if h % 2 == 0:
            tile = pltpu.roll(tile, 64, 1)
        att = r.att[v, h]
        delta = jnp.sum(jnp.where(low, 0.0, tile * att), axis=1, keepdims=True)
        parts = split3(-delta) + split3(-att[:, 0:1])
        aux = jnp.zeros((ROWS, 128), F32)
        for i, part in enumerate(parts):
            aux = jnp.where(ln == i, part, aux)
        r.do_out[v, h] = jnp.where(low, aux, tile).astype(BF)


def send_do(v, r, place):
    @pl.loop(0, HEADS)
    def _(a):
        h = (place.me // 4 + a) % 8
        for b in range(2):
            place.send(
                r.do_out.at[v, h],
                r.do_in.at[v, place.own_slot],
                r.sems.at[6, v],
                r.sems.at[7, v],
                (place.me + b) % 2,
                place.chip(h, place.own_t),
            )


def bwd_tile(v, i, r, place):
    width = BWD_C * 128
    u = tile_of(i, place.t)
    q = jnp.concatenate([r.q_in[v, 2 * i], r.q_in[v, 2 * i + 1]], axis=0).astype(F32)
    do = jnp.concatenate([r.do_in[v, 2 * i], r.do_in[v, 2 * i + 1]], axis=0).astype(F32)
    ln = lanes((256, 128))
    lq = jnp.where((ln >= 68) & (ln < 71), pltpu.roll(do, 65, 1), q).astype(BF)
    ld = jnp.where((ln >= 3) & (ln < 64), 0.0, do).astype(BF)
    qz = jnp.where(ln < 64, q, 0.0).astype(BF)
    dz = jnp.where(ln >= 64, do, 0.0).astype(BF)

    def step(c, dqt, masked):
        rows = ds(c * width, width)
        x = nt(r.ka[v, rows, :], lq)
        if masked:
            row, col = subs((width, 256)), lanes((width, 256))
            at = 256 * (row // 128) + row % 128 + (256 * BWD_C * c + 128 * place.s - 256 * u)
            x = jnp.where(at <= col, x, -BIG)
        p = jnp.exp(x)
        dp = nt(r.va[v, rows, :], ld)
        dsc = (p * dp).astype(BF)
        r.dkv_acc[rows, :] += nn(dsc, qz) + nn(p.astype(BF), dz)
        return dqt + nn(r.kat[:, rows], dsc)

    full = u // BWD_C
    dqt = lax.fori_loop(0, full, lambda c, x: step(c, x, False), jnp.zeros((64, 256), F32))
    dqt = step(full, dqt, True)
    dq = jnp.transpose(jnp.concatenate([dqt, jnp.zeros((64, 256), F32)], axis=0)).astype(BF)
    r.dq_out[v, 2 * i] = dq[:128]
    r.dq_out[v, 2 * i + 1] = dq[128:]
    for turn in range(2):
        half = (turn + place.s) % 2
        place.send(
            r.dq_out.at[v, 2 * i + half],
            r.dq_in.at[v, 2 * place.head + place.s],
            r.sems.at[8, v],
            r.sems.at[9, v],
            place.micro,
            2 * u + half,
        )


def attention_back(v, r, place):
    r.dkv_acc[...] = jnp.zeros_like(r.dkv_acc)

    @pl.loop(0, 8)
    def _(i):
        rows = ds(i * 512, 512)
        r.kat[:, rows] = jnp.transpose(r.ka[v, rows, :].astype(F32))[:64].astype(BF)

    @pl.loop(0, 8)
    def _(i):
        bwd_tile(v, (i + place.head) % 8, r, place)
        for after, step in SUM_DURING_BACK:

            @pl.when((v == 0) & (i == after))
            def _():
                SUM_STEPS[step](0, r, place)

    @pl.when(v == 0)
    def _():
        wait_sent(r.dkv_in.at[1], r.sems.at[10, 1], place.self_kv, 32)

    @pl.loop(0, 32)
    def _(k):
        n = (k + 4 * place.head + place.t) % 32
        r.dkv_out[n] = r.dkv_acc[ds(n * 128, 128), :].astype(BF)
        place.send(
            r.dkv_out.at[n],
            r.dkv_in.at[v, 4 * place.head + place.t],
            r.sems.at[10, v],
            r.sems.at[11, v],
            place.micro,
            2 * n + place.s,
        )


def after_attention_back(v, r):
    ln = lanes((ROWS, 128))
    low = ln < 64
    for i in range(HEADS // 2):
        cols = slice(128 * i, 128 * i + 128)
        dq, dkv = [], []
        for h in (2 * i, 2 * i + 1):
            both = r.dq_in[v, 2 * h].astype(F32) + r.dq_in[v, 2 * h + 1].astype(F32)
            dq.append(both * 0.125)
            four = [r.dkv_in[v, 4 * h + t].astype(F32) for t in range(4)]
            dkv.append((four[0] + four[1]) + (four[2] + four[3]))
        r.dq[v, :, cols] = jnp.where(low, dq[0], pltpu.roll(dq[1], 64, 1)).astype(BF)
        r.dk[v, :, cols] = jnp.where(low, dkv[0], pltpu.roll(dkv[1], 64, 1)).astype(BF)
        r.dv[v, :, cols] = jnp.where(low, pltpu.roll(dkv[0], 64, 1), dkv[1]).astype(BF)
    r.work[...] += (
        nt(r.dq[v], r.w_query[...]) + nt(r.dk[v], r.w_key[...]) + nt(r.dv[v], r.w_value[...])
    )


def both(ref):
    return jnp.concatenate([ref[0], ref[1]], axis=0)


def put(ref, unit, tile):
    ref[ds(unit * 512, 512), :] = tile.astype(BF)


def weight_grads_early(r):
    @pl.loop(0, 4)
    def _(j):
        cols = ds(j * 512, 512)
        up = jnp.concatenate([r.up_low[0, :, cols], r.up_low[1, :, cols]], axis=0)
        grad = tn(both(r.first_low), up)
        for k in range(4):
            put(r.sum_in0, 4 * j + k, grad[:, 128 * k : 128 * k + 128])
        act = jnp.concatenate([r.act[0, :, cols], r.act[1, :, cols]], axis=0)
        grad = tn(act, both(r.down_low))
        for k in range(4):
            put(r.sum_in0, 16 + 4 * k + j, grad[:, 128 * k : 128 * k + 128])

    grad = tn(both(r.att_low), both(r.out_low))
    for k in range(4):
        put(r.sum_in0, 32 + k, grad[:, 128 * k : 128 * k + 128])


def weight_grads_late(r):
    hid = jnp.concatenate([r.hid[0], r.hid[1]], axis=0)
    for i, ref in enumerate((r.dq, r.dk, r.dv)):
        grad = tn(hid, both(ref))
        for k in range(4):
            put(r.sum_in1, 4 * i + k, grad[:, 128 * k : 128 * k + 128])


SUM_ROWS = (3072, 1024)
ORDERS = ((0, 1, 2), (1, 2, 0), (2, 0, 1))


def sum_refs(g, r):
    names = ("in", "x", "r0", "r1", "r2", "s0", "s1", "t", "sems")
    return SimpleNamespace(**{n: getattr(r, "sum_" + n + str(g)) for n in names})


def remote(src, dst, send_sem, recv_sem, section, dp):
    pltpu.make_async_remote_copy(
        src_ref=src,
        dst_ref=dst,
        send_sem=send_sem,
        recv_sem=recv_sem,
        device_id=(section, dp),
        device_id_type=MESH,
    ).start()


def offsets(p, rows, place):
    out, at = [], 0
    for k in range(3):
        at = at + place.coords[ORDERS[p][k]] * (rows // 4 ** (k + 1))
        out.append(at)
    return out


def exchange_start(g, r, place):
    q, rows = sum_refs(g, r), SUM_ROWS[g]
    for p in range(3):
        remote(
            q.__dict__["in"].at[ds((1 - place.s) * 3 * rows + p * rows, rows)],
            q.x.at[pl.ds(p * rows, rows)],
            q.sems.at[0, 0, p],
            q.sems.at[1, 0, p],
            1 - place.s,
            place.me,
        )


def scatter_send(g, p, k, src, base, q, place):
    size = SUM_ROWS[g] // 4 ** (k + 1)
    dst = (q.r0, q.r1, q.r2)[k]
    axis = ORDERS[p][k]
    for d in (2, 1, 3):
        c = (place.coords[axis] + d) % 4
        remote(
            src.at[ds(base + c * size, size)],
            dst.at[p, d - 1],
            q.sems.at[0, 1 + k, p],
            q.sems.at[1, 1 + k, p],
            place.s,
            place.along(axis, d),
        )


def exchange_done(g, r, place):
    q, rows = sum_refs(g, r), SUM_ROWS[g]
    src = q.__dict__["in"]
    for p in range(3):
        base = place.s * 3 * rows + p * rows
        wait_all(q.x.at[pl.ds(p * rows, rows)], q.sems.at[1, 0, p])

        @pl.loop(0, rows // 512)
        def _(k):
            at = ds(base + k * 512, 512)
            other = q.x[ds(p * rows + k * 512, 512), :]
            src[at, :] = (src[at, :].astype(F32) + other.astype(F32)).astype(BF)

        scatter_send(g, p, 0, src, base, q, place)


def scatter_done(k, g, r, place):
    q, rows = sum_refs(g, r), SUM_ROWS[g]
    size = rows // 4 ** (k + 1)
    got = (q.r0, q.r1, q.r2)[k]
    for p in range(3):
        wait_all(got.at[p], q.sems.at[1, 1 + k, p])
        c = place.coords[ORDERS[p][k]]
        if k == 0:
            own = q.__dict__["in"][ds(place.s * 3 * rows + p * rows + c * size, size), :]
        else:
            own = (q.s0, q.s1)[k - 1][p, ds(c * size, size), :]
        total = own.astype(F32)
        for d in range(3):
            total = total + got[p, d].astype(F32)
        if k < 2:
            dst = (q.s0, q.s1)[k]
            dst[p] = total.astype(BF)
            scatter_send(g, p, k + 1, dst.at[p], 0, q, place)
        else:
            q.t[place.s, p, ds(offsets(p, rows, place)[2], size), :] = total.astype(BF)
            gather_send(g, p, 2, q, place)


def gather_send(g, p, k, q, place):
    rows = SUM_ROWS[g]
    size = rows // 4 ** (k + 1)
    block = q.t.at[place.s, p, ds(offsets(p, rows, place)[k], size)]
    axis = ORDERS[p][k]
    for d in (2, 1, 3):
        sem = 4 + k if k else 6 + d
        remote(
            block, block, q.sems.at[0, sem, p], q.sems.at[1, sem, p], place.s, place.along(axis, d)
        )


def cross_send(p, start, size, q, place):
    block = q.t.at[place.s, p, ds(start, size)]
    remote(block, block, q.sems.at[0, 4, p], q.sems.at[1, 4, p], 1 - place.s, place.me)


def gather_done(k, g, r, place):
    q, rows = sum_refs(g, r), SUM_ROWS[g]
    for p in range(3):
        wait_all(
            q.t.at[0, p, pl.ds(0, 3 * rows // 4 ** (k + 1))],
            q.sems.at[1, 4 + k, p],
        )
        gather_send(g, p, k - 1, q, place)
        if k == 1:
            cross_send(p, offsets(p, rows, place)[0], rows // 4, q, place)


def gather_last(g, r, place):
    q, rows = sum_refs(g, r), SUM_ROWS[g]
    size = rows // 4
    for d in (1, 3, 2):
        for p in range(3):
            wait_all(q.t.at[0, p, pl.ds(0, size)], q.sems.at[1, 6 + d, p])
            c = (place.coords[ORDERS[p][0]] - d + 4) % 4
            cross_send(p, c * size, size, q, place)


def sum_out(g, r, place):
    q = sum_refs(g, r)
    for p in range(3):
        wait_all(q.t.at[0, p], q.sems.at[1, 4, p])
    pltpu.make_async_copy(q.t, (r.sums0, r.sums1)[g], r.vsems.at[2, g]).start()


def sum_drain(g, r, place):
    q, rows = sum_refs(g, r), SUM_ROWS[g]
    for p in range(3):
        wait_all(q.x.at[pl.ds(0, rows)], q.sems.at[0, 0, p])
        for k in range(3):
            wait_all(q.t.at[0, p, pl.ds(0, 3 * rows // 4 ** (k + 1))], q.sems.at[0, 1 + k, p])
        for k in (1, 2):
            wait_all(q.t.at[0, p, pl.ds(0, 3 * rows // 4 ** (k + 1))], q.sems.at[0, 4 + k, p])
        for d in range(1, 4):
            wait_all(q.t.at[0, p, pl.ds(0, rows // 4)], q.sems.at[0, 6 + d, p])
        wait_all(q.t.at[0, p], q.sems.at[0, 4, p])
    pltpu.make_async_copy(q.t, (r.sums0, r.sums1)[g], r.vsems.at[2, g]).wait()


def vec_exchange(r, place):
    remote(r.vec_own, r.vec_x, r.vsems.at[0, 0], r.vsems.at[1, 0], 1 - place.s, place.me)


def vec_send(axis, r, place):
    c = place.coords[axis]
    for d in (1, 2, 3):
        remote(
            r.vec_in.at[axis, c],
            r.vec_in.at[axis, c],
            r.vsems.at[0, 1 + axis],
            r.vsems.at[1, 1 + axis],
            place.s,
            place.along(axis, d),
        )


def vec_step(axis, r, place):
    if axis == 0:
        wait_all(r.vec_x, r.vsems.at[1, 0])
        total = r.vec_own[...] + r.vec_x[...]
    else:
        wait_all(r.vec_in.at[axis - 1, pl.ds(0, 3)], r.vsems.at[1, axis])
        total = (r.vec_in[axis - 1, 0] + r.vec_in[axis - 1, 1]) + (
            r.vec_in[axis - 1, 2] + r.vec_in[axis - 1, 3]
        )
    if axis < 3:
        r.vec_in[axis, place.coords[axis]] = total
        vec_send(axis, r, place)
    else:
        r.vec[...] = total


def vec_drain(r):
    wait_all(r.vec_x, r.vsems.at[0, 0])
    for axis in range(3):
        wait_all(r.vec_in.at[axis, pl.ds(0, 3)], r.vsems.at[0, 1 + axis])


def step_exchange(g, r, place):
    exchange_start(g, r, place)
    if g == 0:
        vec_exchange(r, place)


def step_scatter(g, r, place):
    exchange_done(g, r, place)
    if g == 0:
        vec_step(0, r, place)


def step_between(k, g, r, place):
    scatter_done(k, g, r, place)
    if g == 0:
        vec_step(k + 1, r, place)


SUM_STEPS = (
    step_exchange,
    step_scatter,
    lambda *a: step_between(0, *a),
    lambda *a: step_between(1, *a),
    lambda *a: step_between(2, *a),
    lambda *a: gather_done(2, *a),
    lambda *a: gather_done(1, *a),
    gather_last,
    sum_out,
)
SUM_DURING_BACK = ((1, 1), (4, 2), (5, 3), (6, 4), (7, 5))


INPUTS = ["inputs", "groups", "cotangent", "w_query", "w_key", "w_value", "w_out", "w_up", "w_down"]
INPUTS += ["gain_one", "shift_one", "gain_two", "shift_two"]
OUTPUTS = {
    "output": ((1, ROWS, D), BF),
    "input_grad": ((1, ROWS, D), BF),
    "sums0": ((2, 3, 3072, 128), BF),
    "sums1": ((2, 3, 1024, 128), BF),
    "vec": ((8, D), F32),
}
SCRATCH = {
    "hid": ((3, ROWS, D), BF),
    "own_aug": ((ROWS, 128), F32),
    "q_out": ((2, 8, ROWS, 128), BF),
    "kv_out": ((2, 8, ROWS, 128), BF),
    "q_in": ((2, 16, ROWS, 128), BF),
    "kv_in": ((2, 32, ROWS, 128), BF),
    "grp_out": ((1, 8, 128), jnp.int32),
    "grp_in": ((32, 8, 128), jnp.int32),
    "ka": ((2, 4096, 128), BF),
    "va": ((2, 4096, 128), BF),
    "kat": ((64, 4096), BF),
    "o_out": ((2, 16, ROWS, 128), BF),
    "o_in": ((2, 16, ROWS, 128), BF),
    "att": ((2, 8, ROWS, 128), F32),
    "att_low": ((2, ROWS, D), BF),
    "n_one": ((2, ROWS, D), F32),
    "f_one": ((2, ROWS, 128), F32),
    "first_low": ((2, ROWS, D), BF),
    "pre": ((2, ROWS, FF), F32),
    "act": ((2, ROWS, FF), BF),
    "n_two": ((2, ROWS, D), F32),
    "f_two": ((2, ROWS, 128), F32),
    "work": ((ROWS, D), F32),
    "dy": ((ROWS, D), F32),
    "down_low": ((2, ROWS, D), BF),
    "up_low": ((2, ROWS, FF), BF),
    "out_low": ((2, ROWS, D), BF),
    "do_out": ((2, 8, ROWS, 128), BF),
    "do_in": ((2, 16, ROWS, 128), BF),
    "dq_out": ((2, 16, ROWS, 128), BF),
    "dq_in": ((2, 16, ROWS, 128), BF),
    "dkv_acc": ((4096, 128), F32),
    "dkv_out": ((32, ROWS, 128), BF),
    "dkv_in": ((2, 32, ROWS, 128), BF),
    "dq": ((2, ROWS, D), BF),
    "dk": ((2, ROWS, D), BF),
    "dv": ((2, ROWS, D), BF),
    "vec_own": ((8, D), F32),
    "vec_x": ((8, D), F32),
    "vec_in": ((3, 4, 8, D), F32),
}
for g, rows in enumerate(SUM_ROWS):
    SCRATCH |= {
        f"sum_in{g}": ((6 * rows, 128), BF),
        f"sum_x{g}": ((3 * rows, 128), BF),
        f"sum_r0{g}": ((3, 3, rows // 4, 128), BF),
        f"sum_r1{g}": ((3, 3, rows // 16, 128), BF),
        f"sum_r2{g}": ((3, 3, rows // 64, 128), BF),
        f"sum_s0{g}": ((3, rows // 4, 128), BF),
        f"sum_s1{g}": ((3, rows // 16, 128), BF),
        f"sum_t{g}": ((2, 3, rows, 128), BF),
    }
SEMS = {"sems": (12, 2), "gsems": (2,), "sum_sems0": (2, 10, 3), "sum_sems1": (2, 10, 3), "vsems": (3, 4)}


def kernel(*refs):
    names = INPUTS + list(OUTPUTS) + list(SCRATCH) + list(SEMS)
    r = SimpleNamespace(**dict(zip(names, refs)))
    place = Place()
    barrier(place)
    send_groups(r, place)
    make_own_aug(r, place)
    r.vec_own[...] = jnp.zeros_like(r.vec_own)
    r.hid[0] = r.inputs[place.s]

    @pl.loop(0, 2)
    def _(v):
        project(v, r)
        send_qkv(v, r, place)

        @pl.when(v == 0)
        def _():
            wait_all(r.grp_in, r.gsems.at[1])
            make_key_aug(r)

        wait_all(r.kv_in.at[v], r.sems.at[1, v])
        make_kv(v, r)
        wait_all(r.q_in.at[v], r.sems.at[3, v])

        @pl.loop(0, 4)
        def _(j):
            fwd_pair(v, (j + place.head) % 4, r, place)

        wait_all(r.o_in.at[v], r.sems.at[5, v])
        after_attention(v, r)

    r.output[0] = r.hid[2]
    r.dy[...] = r.cotangent[place.s].astype(F32)

    @pl.loop(0, 2)
    def _(step):
        v = 1 - step
        before_attention_back(v, r)
        send_do(v, r, place)

        @pl.when(v == 0)
        def _():
            weight_grads_early(r)
            SUM_STEPS[0](0, r, place)

        wait_all(r.do_in.at[v], r.sems.at[7, v])
        attention_back(v, r, place)

        @pl.when(v == 0)
        def _():
            SUM_STEPS[6](0, r, place)

        wait_all(r.dq_in.at[v], r.sems.at[9, v])
        wait_all(r.dkv_in.at[v], r.sems.at[11, v])
        after_attention_back(v, r)
        r.dy[...] = r.work[...].astype(BF).astype(F32)

    r.input_grad[0] = r.dy[...].astype(BF)
    weight_grads_late(r)
    SUM_STEPS[0](1, r, place)
    SUM_STEPS[7](0, r, place)
    for step in SUM_STEPS[1:5]:
        step(1, r, place)
    SUM_STEPS[8](0, r, place)
    for step in SUM_STEPS[5:]:
        step(1, r, place)

    vec_drain(r)
    for g in range(2):
        sum_drain(g, r, place)
    wait_sent(r.grp_in, r.gsems.at[0], place.self_kv, 32)

    @pl.loop(0, 2)
    def _(v):
        wait_sent(r.kv_in.at[v], r.sems.at[0, v], place.self_kv, 32)
        wait_sent(r.q_in.at[v], r.sems.at[2, v], place.self_q, 16)
        wait_sent(r.o_in.at[v], r.sems.at[4, v], place.self_q, 16)
        wait_sent(r.do_in.at[v], r.sems.at[6, v], place.self_q, 16)
        wait_sent(r.dq_in.at[v], r.sems.at[8, v], place.self_q, 16)

    wait_sent(r.dkv_in.at[0], r.sems.at[10, 0], place.self_kv, 32)


def unpack(early, late):
    def body(early, late, query, key, value, out, up, down, got, small, up_f, down_f, sin, sout):
        loads = []
        for j in range(12):
            src = late.at[pl.ds(4 * j, 4)] if j < 3 else early.at[pl.ds(4 * (j - 3), 4)]
            loads.append(pltpu.make_async_copy(src, got.at[pl.ds(4 * j, 4)], sin.at[j]))
        order = [0, 1, 2, 11, 3, 4, 5, 6, 7, 8, 9, 10]
        for j in order:
            loads[j].start()
        stores = []

        def store(j, src, dst):
            stores.append(pltpu.make_async_copy(src, dst, sout.at[j]))
            stores[-1].start()

        for j in order:
            loads[j].wait()
            tiles = [got[4 * j + k].astype(F32) for k in range(4)]
            cols = [slice(128 * k, 128 * k + 128) for k in range(4)]
            if j < 3 or j == 11:
                i = min(j, 3)
                for k in range(4):
                    small[i, :, cols[k]] = tiles[k]
                store(j, small.at[i], (query, key, value, out)[i])
            elif j < 7:
                at = 512 * (j - 3)
                for k in range(4):
                    up_f[:, at + 128 * k : at + 128 * k + 128] = tiles[k]
                store(j, up_f.at[:, pl.ds(at, 512)], up.at[:, pl.ds(at, 512)])
            else:
                for k in range(4):
                    down_f[512 * k : 512 * k + 512, cols[j - 7]] = tiles[k]
        store(7, down_f, down)
        for copy in stores:
            copy.wait()

    square, hbm = jax.ShapeDtypeStruct((D, D), F32), pl.BlockSpec(memory_space=pl.ANY)
    shapes = [square] * 4 + [jax.ShapeDtypeStruct((D, FF), F32), jax.ShapeDtypeStruct((FF, D), F32)]
    return pl.pallas_call(
        body,
        out_shape=shapes,
        in_specs=[hbm] * 2,
        out_specs=[hbm] * 6,
        scratch_shapes=[
            pltpu.VMEM((48, 512, 128), BF),
            pltpu.VMEM((4, D, D), F32),
            pltpu.VMEM((D, FF), F32),
            pltpu.VMEM((FF, D), F32),
            pltpu.SemaphoreType.DMA((12,)),
            pltpu.SemaphoreType.DMA((12,)),
        ],
        compiler_params=pltpu.CompilerParams(vmem_limit_bytes=40 * 2**20),
        name="unpack",
    )(early, late)


def on_device(inputs, groups, cotangent, *params):
    vectors = [x.reshape(1, D) for x in params[6:]]
    vmem = pl.BlockSpec(memory_space=pltpu.VMEM)
    out = pl.pallas_call(
        kernel,
        out_shape=[jax.ShapeDtypeStruct(shape, kind) for shape, kind in OUTPUTS.values()],
        in_specs=[vmem] * len(INPUTS),
        out_specs=[
            pl.BlockSpec(memory_space=pl.ANY) if n.startswith("sums") else vmem for n in OUTPUTS
        ],
        scratch_shapes=[pltpu.VMEM(shape, kind) for shape, kind in SCRATCH.values()]
        + [pltpu.SemaphoreType.DMA(shape) for shape in SEMS.values()],
        compiler_params=pltpu.CompilerParams(
            collective_id=0, has_side_effects=True, vmem_limit_bytes=62 * 2**20
        ),
        name="visits",
    )(inputs, groups, cotangent, *params[:6], *vectors)
    grads = unpack(out[2].reshape(36, 512, 128), out[3].reshape(12, 512, 128))
    vec = out[4]
    return (*out[:2], *grads, vec[0], vec[1], vec[2], vec[3])


def solution(mesh):
    rows = P(None, "dp", None)
    return jax.shard_map(
        on_device,
        mesh=mesh,
        in_specs=(rows, P(None, "dp"), rows) + (P(),) * 10,
        out_specs=(P("section", "dp", None),) * 2 + (P(),) * 10,
        check_vma=False,
    )
```

```python
from types import SimpleNamespace

import jax
import jax.numpy as jnp
from jax import lax
from jax.experimental import pallas as pl
from jax.experimental.pallas import tpu as pltpu
from jax.sharding import PartitionSpec as P

F32, BF = jnp.float32, jnp.bfloat16
BIG = 1e30
ROWS, D, FF, HEADS = 128, 512, 2048, 8
MESH = pl.DeviceIdType.MESH


def nt(a, b):
    return lax.dot_general(a, b, (((1,), (1,)), ((), ())), preferred_element_type=F32)


def nn(a, b):
    return lax.dot_general(a, b, (((1,), (0,)), ((), ())), preferred_element_type=F32)


def tn(a, b):
    return lax.dot_general(a, b, (((0,), (0,)), ((), ())), preferred_element_type=F32)


def lanes(shape):
    return lax.broadcasted_iota(jnp.int32, shape, len(shape) - 1)


def subs(shape):
    return lax.broadcasted_iota(jnp.int32, shape, len(shape) - 2)


def ds(start, size):
    if isinstance(start, int):
        return pl.ds(start, size)
    return pl.ds(pl.multiple_of(start, size), size)


def split3(x):
    a = x.astype(BF).astype(F32)
    b = (x - a).astype(BF).astype(F32)
    return a, b, (x - a - b).astype(BF).astype(F32)


def tile_of(r, t):
    return 4 * r + (r + t) % 4


def mean(x):
    return jnp.mean(x, axis=-1, keepdims=True)


def norm(x):
    centred = x - mean(x)
    factor = lax.rsqrt(mean(centred * centred) + 1e-05)
    return centred * factor, factor


def norm_back(dy, n, factor, gain):
    u = dy * gain
    return factor * (u - mean(u) - n * mean(u * n))


GELU_C = 0.7978845608028654


def gelu(x):
    return 0.5 * x * (1.0 + jnp.tanh(GELU_C * (x + 0.044715 * x * x * x)))


def gelu_slope(x):
    sq = x * x
    th = jnp.tanh(GELU_C * x * (1.0 + 0.044715 * sq))
    return 0.5 * (1.0 + th) + 0.5 * x * (1.0 - th * th) * (GELU_C * (1.0 + 3 * 0.044715 * sq))


class Place:
    def __init__(self):
        self.me = lax.axis_index("dp")
        self.s = lax.axis_index("section")
        me = self.me
        self.coords = (me % 4, me // 16, (me // 4) % 4)
        x, y, z = self.coords
        self.t = (x + y + z) % 4
        self.head = 4 * (y % 2) + x
        self.micro = y // 2
        self.own_t = ((me // 2) % 4 - me // 8 + 32) % 4
        self.own_slot = 2 * (me // 8) + me % 2
        mine = self.micro == self.s
        self.self_kv = mine & (me % 2 == self.s)
        self.self_q = mine & (self.own_t == self.t)

    def along(self, axis, d):
        c = self.coords[axis]
        return self.me + ((c + d) % 4 - c) * (1, 16, 4)[axis]

    def chip(self, h, t):
        x, y = h % 4, 2 * self.s + h // 4
        return 16 * y + 4 * ((t - x - y + 8) % 4) + x

    def send(self, src, dst, send_sem, recv_sem, section, dp):
        to_self = (section == self.s) & (dp == self.me)

        @pl.when(jnp.logical_not(to_self))
        def _():
            pltpu.make_async_remote_copy(
                src_ref=src,
                dst_ref=dst,
                send_sem=send_sem,
                recv_sem=recv_sem,
                device_id=(section, dp),
                device_id_type=MESH,
            ).start()

        @pl.when(to_self)
        def _():
            pltpu.make_async_copy(src, dst, recv_sem).start()


def wait_all(ref, sem):
    pltpu.make_async_copy(ref, ref, sem).wait()


def wait_sent(ref, sem, to_self, count):
    @pl.when(to_self)
    def _():
        wait_all(ref.at[pl.ds(0, count - 1)], sem)

    @pl.when(jnp.logical_not(to_self))
    def _():
        wait_all(ref.at[pl.ds(0, count)], sem)


def greet(place):
    sem = pltpu.get_barrier_semaphore()

    @pl.loop(1, 128)
    def _(k):
        other = (place.s * 64 + place.me + k) % 128
        pl.semaphore_signal(sem, inc=1, device_id=(other // 64, other % 64), device_id_type=MESH)


def all_here():
    pl.semaphore_wait(pltpu.get_barrier_semaphore(), 127)


LOADED = ["hid", "w_query", "w_key", "w_value", "w_out", "w_up", "w_down", "cot"]


def load(name, r, place):
    if name == "hid":
        return pltpu.make_async_copy(r.inputs.at[place.s], r.hid.at[0], r.load_sems.at[0])
    if name == "cot":
        return pltpu.make_async_copy(r.cotangent.at[place.s], r.cot, r.load_sems.at[7])
    return pltpu.make_async_copy(
        getattr(r, name + "_hbm"), getattr(r, name), r.load_sems.at[LOADED.index(name)]
    )


def pack(tile, odd):
    low = lanes((64, 128)) < 64
    if odd:
        return jnp.where(low, pltpu.roll(tile[:64], 64, 1), tile[64:])
    return jnp.where(low, tile[:64], pltpu.roll(tile[64:], 64, 1))


def spread(packed, odd):
    turned = pltpu.roll(packed, 64, 1)
    return jnp.concatenate([turned, packed] if odd else [packed, turned], axis=0)


def parts_in_rows(rows):
    at = subs((16, 128))
    out = jnp.zeros((16, 128), F32)
    for i, part in enumerate(rows):
        out = jnp.where(at == i, part, out)
    return out.astype(BF)


def project_queries(v, r):
    q = nn(r.hid[v], r.w_query[...]).astype(BF).astype(F32) * 0.125
    for h in range(HEADS):
        tile = q[:, 128 * (h // 2) : 128 * (h // 2) + 128]
        r.q_out[v, h] = pack(tile, h % 2 == 1).astype(BF)


def project_keys_values(v, r):
    hid = r.hid[v]
    k = nn(hid, r.w_key[...]).astype(BF).astype(F32)
    w = nn(hid, r.w_value[...]).astype(BF).astype(F32)
    low = lanes((ROWS, 128)) < 64
    for h in range(HEADS):
        cols = slice(128 * (h // 2), 128 * (h // 2) + 128)
        kt, vt = k[:, cols], w[:, cols]
        if h % 2 == 0:
            vt = pltpu.roll(vt, 64, 1)
        else:
            kt = pltpu.roll(kt, 64, 1)
        r.kv_out[v, h] = jnp.where(low, kt, vt).astype(BF)


def to_queries(src, dst, send_sem, recv_sem, place):
    @pl.loop(0, HEADS)
    def _(a):
        h = (place.me // 4 + a) % 8
        for b in range(2):
            core, chip = (place.me + b) % 2, place.chip(h, place.own_t)
            place.send(src(h), dst.at[place.own_slot], send_sem, recv_sem, core, chip)


def to_keys(src, dst, send_sem, recv_sem, place):
    n = place.me // 2

    @pl.loop(0, HEADS)
    def _(a):
        h = 2 * ((n // 8 + a // 2) % 4) + (n // 4 + a) % 2
        for b in range(4):
            chip = place.chip(h, (n + b) % 4)
            place.send(src(h), dst.at[n], send_sem, recv_sem, place.me % 2, chip)


def send_queries(v, r, place):
    to_queries(
        lambda h: r.q_out.at[v, h], r.q_in.at[v], r.sems.at[2, v], r.sems.at[3, v], place
    )


def send_keys_values(v, r, place):
    to_keys(
        lambda h: r.kv_out.at[v, h],
        r.kv_in.at[v],
        r.sems.at[0, v],
        r.kv_sems.at[v, place.me // 16],
        place,
    )


def send_groups(r, place):
    r.grp_out[0] = jnp.broadcast_to(r.groups[pl.ds(place.s, 1), :], (8, 128))
    to_queries(lambda h: r.grp_out.at[0], r.grp_q, r.gsems.at[2], r.gsems.at[3], place)
    to_keys(lambda h: r.grp_out.at[0], r.grp_in, r.gsems.at[0], r.gsems.at[1], place)


def column_of(row):
    return jnp.transpose(jnp.broadcast_to(row.astype(F32), (128, 128)))


def make_aug(r):
    ln = lanes((ROWS, 128))
    inside = (ln >= 64) & (ln < 68)

    @pl.loop(0, 32)
    def _(n):
        g = column_of(r.grp_in[n][0:1, :]).astype(jnp.int32)
        aug = jnp.where(inside & (ln - 64 != g), -BIG, 0.0).astype(BF)
        for v in range(2):
            r.ka[v, ds(n * 128, 128), :] = aug

    @pl.loop(0, 16)
    def _(n):
        g = column_of(r.grp_q[n][0:1, :]).astype(jnp.int32)
        aug = jnp.where(ln - 64 == g, 1.0, 0.0).astype(BF)
        for v in range(2):
            r.lq[v, ds(n * 128, 128), :] = aug


def make_queries(v, r):
    low = lanes((ROWS, 128)) < 64

    @pl.loop(0, 16)
    def _(n):
        rows = ds(n * 128, 128)
        q = spread(r.q_in[v, n].astype(F32), False)
        r.lq[v, rows, :] = jnp.where(low, q, r.lq[v, rows, :].astype(F32)).astype(BF)


def make_kv(v, c, r):
    ln = lanes((ROWS, 128))
    low = ln < 64
    ones = jnp.where(ln < 1, 1.0, 0.0)

    @pl.loop(0, 8)
    def _(k):
        n = 8 * c + k
        rows = ds(n * 128, 128)
        kv = r.kv_in[v, n].astype(F32)
        r.ka[v, rows, :] = jnp.where(low, kv, r.ka[v, rows, :].astype(F32)).astype(BF)
        r.va[v, rows, :] = jnp.where(low, ones, kv).astype(BF)


def fwd_body(v, c, j, masked, r, place):
    width = 1024
    rows = ds(c * width, width)
    sc = nt(r.lq[v, ds(512 * j, 512), :], r.ka[v, rows, :])
    if masked:
        col, row = lanes((512, width)), subs((512, width))
        tiles = [tile_of(2 * j + k, place.t) for k in range(2)]
        at = 256 * (col // 128) + col % 128 + (2048 * c + 128 * place.s)
        limit = row % 256 + 256 * jnp.where(row < 256, tiles[0], tiles[1])
        sc = jnp.where(at <= limit, sc, -BIG)
    top = r.f_top[j][:, 0:1]
    new = jnp.maximum(top, jnp.max(sc, axis=1, keepdims=True))
    p = jnp.exp(sc - new).astype(BF)
    r.f_acc[j] = r.f_acc[j] * jnp.exp(top - new) + nn(p, r.va[v, rows, :])
    r.f_top[j] = jnp.broadcast_to(new, (512, 128))


def fwd_finish(v, j, r, place):
    acc = r.f_acc[j]
    total = acc[:, 0:1]
    out = acc / total
    logs = jnp.broadcast_to(r.f_top[j][:, 0:1] + jnp.log(total), (512, 128))
    for k in range(4):
        rows = slice(128 * k, 128 * k + 128)
        r.o_out[v, 4 * j + k, 0:64] = pack(out[rows], True).astype(BF)
        row = jnp.transpose(logs[rows])[0:1]
        r.o_out[v, 4 * j + k, 64:80] = parts_in_rows(split3(row))
    for k in range(2):
        for turn in range(2):
            half = (turn + place.s) % 2
            place.send(
                r.o_out.at[v, 4 * j + 2 * k + half],
                r.o_in.at[v, 2 * place.head + place.s],
                r.sems.at[4, v],
                r.sems.at[5, v],
                place.micro,
                2 * tile_of(2 * j + k, place.t) + half,
            )


def attention(v, r, place):
    r.f_acc[...] = jnp.zeros_like(r.f_acc)
    r.f_top[...] = jnp.full_like(r.f_top, -2 * BIG)

    @pl.loop(0, 4)
    def _(a):
        c = (place.head // 2 + 4 - a) % 4

        @pl.loop(0, jnp.where(a == 3, c, 0))
        def _(j):
            fwd_finish(v, j, r, place)

        wait_all(r.kv_in.at[v, ds(8 * c, 8)], r.kv_sems.at[v, c])
        make_kv(v, c, r)
        fwd_body(v, c, c, True, r, place)

        @pl.when(a == 3)
        def _():
            fwd_finish(v, c, r, place)

        @pl.loop(c + 1, 4)
        def _(j):
            fwd_body(v, c, j, False, r, place)

            @pl.when(a == 3)
            def _():
                fwd_finish(v, j, r, place)


def after_attention(v, r):
    low = lanes((ROWS, 128)) < 64
    weights = [[], []]
    for h in range(HEADS):
        logs = []
        for core in range(2):
            x = r.o_in[v, 2 * h + core, 64:80].astype(F32)
            logs.append(x[0:1] + x[1:2] + x[2:3])
        top = jnp.maximum(logs[0], logs[1])
        w = [jnp.exp(x - top) for x in logs]
        total = w[0] + w[1]
        r.log_total[v, h : h + 1] = top + jnp.log(total)
        for core in range(2):
            weights[core].append(w[core] / total)
    cols = jnp.transpose(jnp.concatenate(weights[0] + weights[1] + [jnp.zeros((112, 128), F32)], axis=0))
    for i in range(HEADS // 2):
        whole = []
        for h in (2 * i, 2 * i + 1):
            got = [spread(r.o_in[v, 2 * h + k, 0:64].astype(F32), h % 2 == 1) for k in range(2)]
            whole.append(got[0] * cols[:, h : h + 1] + got[1] * cols[:, 8 + h : 9 + h])
        pair = jnp.where(low, whole[0], whole[1])
        r.att[v, :, 128 * i : 128 * i + 128] = pair
        r.att_low[v, :, 128 * i : 128 * i + 128] = pair.astype(BF)
    mixed = r.hid[v].astype(F32) + nn(r.att_low[v], r.w_out[...])
    n_one, f_one = norm(mixed)
    first = n_one * r.gain_one[...] + r.shift_one[...]
    first_low = first.astype(BF)
    r.n_one[v] = n_one
    r.f_one[v] = jnp.broadcast_to(f_one, (ROWS, 128))
    r.first_low[v] = first_low
    r.work[...] = first

    @pl.loop(0, 4)
    def _(j):
        cols = ds(j * 512, 512)
        pre = nn(r.first_low[v], r.w_up[:, cols])
        r.pre[v, :, cols] = pre
        act = gelu(pre).astype(BF)
        r.act[v, :, cols] = act
        r.work[...] += nn(act, r.w_down[cols, :])

    n_two, f_two = norm(r.work[...])
    r.n_two[v] = n_two
    r.f_two[v] = jnp.broadcast_to(f_two, (ROWS, 128))
    r.hid[v + 1] = (n_two * r.gain_two[...] + r.shift_two[...]).astype(BF)


def before_attention_back(v, r):
    dy = r.dy[...]
    n_two = r.n_two[v]
    r.vec_own[2:3, :] += jnp.sum(dy * n_two, axis=0, keepdims=True)
    r.vec_own[3:4, :] += jnp.sum(dy, axis=0, keepdims=True)
    grad_two = norm_back(dy, n_two, r.f_two[v][:, 0:1], r.gain_two[...])
    r.down_low[v] = grad_two.astype(BF)
    r.work[...] = grad_two

    @pl.loop(0, 4)
    def _(j):
        cols = ds(j * 512, 512)
        grad = nt(r.down_low[v], r.w_down[cols, :])
        up = (grad * gelu_slope(r.pre[v, :, cols])).astype(BF)
        r.up_low[v, :, cols] = up
        r.work[...] += nt(up, r.w_up[:, cols])

    dz = r.work[...]
    n_one = r.n_one[v]
    r.vec_own[0:1, :] += jnp.sum(dz * n_one, axis=0, keepdims=True)
    r.vec_own[1:2, :] += jnp.sum(dz, axis=0, keepdims=True)
    grad_one = norm_back(dz, n_one, r.f_one[v][:, 0:1], r.gain_one[...])
    out_low = grad_one.astype(BF)
    r.out_low[v] = out_low
    r.work[...] = grad_one
    grad_att = nt(out_low, r.w_out[...]).astype(BF).astype(F32)
    ln = lanes((ROWS, 128))
    low = ln < 64
    deltas = jnp.zeros((ROWS, 128), F32)
    for h in range(HEADS):
        cols = slice(128 * (h // 2), 128 * (h // 2) + 128)
        product = grad_att[:, cols] * r.att[v, :, cols]
        mine = jnp.where(low, product, 0.0) if h % 2 == 0 else jnp.where(low, 0.0, product)
        deltas = jnp.where(ln == h, jnp.sum(mine, axis=1, keepdims=True), deltas)
    deltas = jnp.transpose(deltas)
    for h in range(HEADS):
        tile = grad_att[:, 128 * (h // 2) : 128 * (h // 2) + 128]
        r.do_out[v, h, 0:64] = pack(tile, h % 2 == 1).astype(BF)
        rows = split3(-deltas[h : h + 1]) + split3(-r.log_total[v, h : h + 1])
        r.do_out[v, h, 64:80] = parts_in_rows(rows)


def send_do(v, r, place):
    to_queries(
        lambda h: r.do_out.at[v, h], r.do_in.at[v], r.sems.at[6, v], r.sems.at[7, v], place
    )


def prepare_back(v, r):
    low = lanes((ROWS, 128)) < 64

    @pl.loop(0, 16)
    def _(n):
        rows = ds(n * 128, 128)
        do = spread(r.do_in[v, n, 0:64].astype(F32), True)
        r.ld[rows, :] = jnp.where(low, 0.0, do).astype(BF)
        r.qz[rows, :] = jnp.where(low, r.lq[v, rows, :].astype(F32), 0.0).astype(BF)
        x = r.do_in[v, n, 64:80].astype(F32)
        r.neg_delta[n] = jnp.broadcast_to(x[0:1] + x[1:2] + x[2:3], (8, 128))
        r.neg_log[n] = jnp.broadcast_to(x[3:4] + x[4:5] + x[5:6], (8, 128))

    @pl.loop(0, 8)
    def _(i):
        rows = ds(i * 512, 512)
        r.kat[:, rows] = jnp.transpose(r.ka[v, rows, :].astype(F32))[:64].astype(BF)

    r.dqt[...] = jnp.zeros_like(r.dqt)


def bwd_body(v, c, tiles, masked, r, place):
    rows = ds(c * 512, 512)
    probs, grads = [], []
    for i in tiles:
        mine = ds(i * 256, 256)
        x = nt(r.ka[v, rows, :], r.lq[v, mine, :])
        x = x + jnp.concatenate([r.neg_log[2 * i][0:1], r.neg_log[2 * i + 1][0:1]], axis=1)
        if masked:
            row, col = subs((512, 256)), lanes((512, 256))
            shift = 1024 * c + 128 * place.s - 256 * tile_of(i, place.t)
            x = jnp.where(256 * (row // 128) + row % 128 + shift <= col, x, -BIG)
        p = jnp.exp(x)
        dp = nt(r.va[v, rows, :], r.ld[mine, :])
        dp = dp + jnp.concatenate([r.neg_delta[2 * i][0:1], r.neg_delta[2 * i + 1][0:1]], axis=1)
        probs.append(p.astype(BF))
        grads.append((p * dp).astype(BF))
    size = 256 * len(tiles)
    queries = pl.ds(pl.multiple_of(tiles[0] * 256, 256), size)
    r.dkv_acc[...] += nn(jnp.concatenate(grads, axis=1), r.qz[queries, :]) + nn(
        jnp.concatenate(probs, axis=1), r.ld[queries, :]
    )
    for i, dsc in zip(tiles, grads):
        r.dqt[i] += nn(r.kat[:, rows], dsc)


def bwd_finish(v, i, r, place):
    dq = jnp.transpose(jnp.concatenate([r.dqt[i], jnp.zeros((64, 256), F32)], axis=0))
    for k in range(2):
        r.dq_out[v, 2 * i + k] = pack(dq[128 * k : 128 * k + 128], False).astype(BF)
    for turn in range(2):
        half = (turn + place.s) % 2
        place.send(
            r.dq_out.at[v, 2 * i + half],
            r.dq_in.at[v, 2 * place.head + place.s],
            r.sems.at[8, v],
            r.sems.at[9, v],
            place.micro,
            2 * tile_of(i, place.t) + half,
        )


def attention_back(v, r, place):
    prepare_back(v, r)

    @pl.when(v == 0)
    def _():
        wait_sent(r.dkv_in.at[1], r.sems.at[10, 1], place.self_kv, 32)

    @pl.loop(0, 8)
    def _(a):
        first = (a // 2 + place.head) % 4
        c = jnp.where(a % 2 == 0, first, 7 - first)
        r.dkv_acc[...] = jnp.zeros_like(r.dkv_acc)

        @pl.when(c % 2 == 0)
        def _():
            bwd_body(v, c, [c, c + 1], True, r, place)

        @pl.when(c % 2 == 1)
        def _():
            bwd_body(v, c, [c], True, r, place)

        @pl.loop(c // 2 + 1, 4)
        def _(m):
            bwd_body(v, c, [2 * m, 2 * m + 1], False, r, place)

        for b in range(4):
            k = (b + place.t) % 4
            n = 4 * c + k
            r.dkv_out[n] = r.dkv_acc[ds(k * 128, 128), :].astype(BF)
            place.send(
                r.dkv_out.at[n],
                r.dkv_in.at[v, 4 * place.head + place.t],
                r.sems.at[10, v],
                r.sems.at[11, v],
                place.micro,
                2 * n + place.s,
            )
        for after, step in SUM_DURING_BACK:

            @pl.when((v == 0) & (a == after))
            def _():
                SUM_STEPS[step](0, r, place)

    @pl.loop(0, 8)
    def _(k):
        bwd_finish(v, (k + place.head) % 8, r, place)


def after_attention_back(v, r):
    ln = lanes((ROWS, 128))
    low = ln < 64
    for i in range(HEADS // 2):
        cols = slice(128 * i, 128 * i + 128)
        dq, dkv = [], []
        for h in (2 * i, 2 * i + 1):
            both = r.dq_in[v, 2 * h].astype(F32) + r.dq_in[v, 2 * h + 1].astype(F32)
            dq.append(spread(both * 0.125, h % 2 == 1))
            four = [r.dkv_in[v, 4 * h + t].astype(F32) for t in range(4)]
            dkv.append((four[0] + four[1]) + (four[2] + four[3]))
        r.dq[v, :, cols] = jnp.where(low, dq[0], dq[1]).astype(BF)
        r.dk[v, :, cols] = jnp.where(low, dkv[0], pltpu.roll(dkv[1], 64, 1)).astype(BF)
        r.dv[v, :, cols] = jnp.where(low, pltpu.roll(dkv[0], 64, 1), dkv[1]).astype(BF)
    r.work[...] += (
        nt(r.dq[v], r.w_query[...]) + nt(r.dk[v], r.w_key[...]) + nt(r.dv[v], r.w_value[...])
    )


def both(ref):
    return jnp.concatenate([ref[0], ref[1]], axis=0)


def put(ref, unit, tile):
    ref[ds(unit * 512, 512), :] = tile.astype(BF)


def weight_grads_early(r):
    @pl.loop(0, 4)
    def _(j):
        cols = ds(j * 512, 512)
        up = jnp.concatenate([r.up_low[0, :, cols], r.up_low[1, :, cols]], axis=0)
        grad = tn(both(r.first_low), up)
        for k in range(4):
            put(r.sum_in0, 4 * j + k, grad[:, 128 * k : 128 * k + 128])
        act = jnp.concatenate([r.act[0, :, cols], r.act[1, :, cols]], axis=0)
        grad = tn(act, both(r.down_low))
        for k in range(4):
            put(r.sum_in0, 16 + 4 * k + j, grad[:, 128 * k : 128 * k + 128])

    grad = tn(both(r.att_low), both(r.out_low))
    for k in range(4):
        put(r.sum_in0, 32 + k, grad[:, 128 * k : 128 * k + 128])


def weight_grads_late(r):
    hid = jnp.concatenate([r.hid[0], r.hid[1]], axis=0)
    for i, ref in enumerate((r.dq, r.dk, r.dv)):
        grad = tn(hid, both(ref))
        for k in range(4):
            put(r.sum_in1, 4 * i + k, grad[:, 128 * k : 128 * k + 128])


SUM_ROWS = (3072, 1024)
ORDERS = ((0, 1, 2), (1, 2, 0), (2, 0, 1))


def sum_refs(g, r):
    names = ("in", "x", "r0", "r1", "r2", "s0", "s1", "t", "sems")
    return SimpleNamespace(**{n: getattr(r, "sum_" + n + str(g)) for n in names})


def remote(src, dst, send_sem, recv_sem, section, dp):
    pltpu.make_async_remote_copy(
        src_ref=src,
        dst_ref=dst,
        send_sem=send_sem,
        recv_sem=recv_sem,
        device_id=(section, dp),
        device_id_type=MESH,
    ).start()


def offsets(p, rows, place):
    out, at = [], 0
    for k in range(3):
        at = at + place.coords[ORDERS[p][k]] * (rows // 4 ** (k + 1))
        out.append(at)
    return out


def exchange_start(g, r, place):
    q, rows = sum_refs(g, r), SUM_ROWS[g]
    for p in range(3):
        remote(
            q.__dict__["in"].at[ds((1 - place.s) * 3 * rows + p * rows, rows)],
            q.x.at[pl.ds(p * rows, rows)],
            q.sems.at[0, 0, p],
            q.sems.at[1, 0, p],
            1 - place.s,
            place.me,
        )


def scatter_send(g, p, k, src, base, q, place):
    size = SUM_ROWS[g] // 4 ** (k + 1)
    dst = (q.r0, q.r1, q.r2)[k]
    axis = ORDERS[p][k]
    for d in (2, 1, 3):
        c = (place.coords[axis] + d) % 4
        remote(
            src.at[ds(base + c * size, size)],
            dst.at[p, d - 1],
            q.sems.at[0, 1 + k, p],
            q.sems.at[1, 1 + k, p],
            place.s,
            place.along(axis, d),
        )


def exchange_done(g, r, place):
    q, rows = sum_refs(g, r), SUM_ROWS[g]
    src = q.__dict__["in"]
    for p in range(3):
        base = place.s * 3 * rows + p * rows
        wait_all(q.x.at[pl.ds(p * rows, rows)], q.sems.at[1, 0, p])

        @pl.loop(0, rows // 512)
        def _(k):
            at = ds(base + k * 512, 512)
            other = q.x[ds(p * rows + k * 512, 512), :]
            src[at, :] = (src[at, :].astype(F32) + other.astype(F32)).astype(BF)

        scatter_send(g, p, 0, src, base, q, place)


def scatter_done(k, g, r, place):
    q, rows = sum_refs(g, r), SUM_ROWS[g]
    size = rows // 4 ** (k + 1)
    got = (q.r0, q.r1, q.r2)[k]
    for p in range(3):
        wait_all(got.at[p], q.sems.at[1, 1 + k, p])
        c = place.coords[ORDERS[p][k]]
        if k == 0:
            own = q.__dict__["in"][ds(place.s * 3 * rows + p * rows + c * size, size), :]
        else:
            own = (q.s0, q.s1)[k - 1][p, ds(c * size, size), :]
        total = own.astype(F32)
        for d in range(3):
            total = total + got[p, d].astype(F32)
        if k < 2:
            dst = (q.s0, q.s1)[k]
            dst[p] = total.astype(BF)
            scatter_send(g, p, k + 1, dst.at[p], 0, q, place)
        else:
            q.t[place.s, p, ds(offsets(p, rows, place)[2], size), :] = total.astype(BF)
            gather_send(g, p, 2, q, place)


def gather_send(g, p, k, q, place):
    rows = SUM_ROWS[g]
    size = rows // 4 ** (k + 1)
    block = q.t.at[place.s, p, ds(offsets(p, rows, place)[k], size)]
    axis = ORDERS[p][k]
    for d in (2, 1, 3):
        sem = 4 + k if k else 6 + d
        remote(
            block, block, q.sems.at[0, sem, p], q.sems.at[1, sem, p], place.s, place.along(axis, d)
        )


def cross_send(p, start, size, q, place):
    block = q.t.at[place.s, p, ds(start, size)]
    remote(block, block, q.sems.at[0, 4, p], q.sems.at[1, 4, p], 1 - place.s, place.me)


def gather_done(k, g, r, place):
    q, rows = sum_refs(g, r), SUM_ROWS[g]
    for p in range(3):
        wait_all(
            q.t.at[0, p, pl.ds(0, 3 * rows // 4 ** (k + 1))],
            q.sems.at[1, 4 + k, p],
        )
        gather_send(g, p, k - 1, q, place)
        if k == 1:
            cross_send(p, offsets(p, rows, place)[0], rows // 4, q, place)


def gather_last(g, r, place):
    q, rows = sum_refs(g, r), SUM_ROWS[g]
    size = rows // 4
    for d in (1, 3, 2):
        for p in range(3):
            wait_all(q.t.at[0, p, pl.ds(0, size)], q.sems.at[1, 6 + d, p])
            c = (place.coords[ORDERS[p][0]] - d + 4) % 4
            cross_send(p, c * size, size, q, place)


def sum_out(g, r, place):
    q = sum_refs(g, r)
    for p in range(3):
        wait_all(q.t.at[0, p], q.sems.at[1, 4, p])
    pltpu.make_async_copy(q.t, (r.sums0, r.sums1)[g], r.vsems.at[2, g]).start()


def sum_drain(g, r, place):
    q, rows = sum_refs(g, r), SUM_ROWS[g]
    for p in range(3):
        wait_all(q.x.at[pl.ds(0, rows)], q.sems.at[0, 0, p])
        for k in range(3):
            wait_all(q.t.at[0, p, pl.ds(0, 3 * rows // 4 ** (k + 1))], q.sems.at[0, 1 + k, p])
        for k in (1, 2):
            wait_all(q.t.at[0, p, pl.ds(0, 3 * rows // 4 ** (k + 1))], q.sems.at[0, 4 + k, p])
        for d in range(1, 4):
            wait_all(q.t.at[0, p, pl.ds(0, rows // 4)], q.sems.at[0, 6 + d, p])
        wait_all(q.t.at[0, p], q.sems.at[0, 4, p])
    pltpu.make_async_copy(q.t, (r.sums0, r.sums1)[g], r.vsems.at[2, g]).wait()


def vec_exchange(r, place):
    remote(r.vec_own, r.vec_x, r.vsems.at[0, 0], r.vsems.at[1, 0], 1 - place.s, place.me)


def vec_send(axis, r, place):
    c = place.coords[axis]
    for d in (1, 2, 3):
        remote(
            r.vec_in.at[axis, c],
            r.vec_in.at[axis, c],
            r.vsems.at[0, 1 + axis],
            r.vsems.at[1, 1 + axis],
            place.s,
            place.along(axis, d),
        )


def vec_step(axis, r, place):
    if axis == 0:
        wait_all(r.vec_x, r.vsems.at[1, 0])
        total = r.vec_own[...] + r.vec_x[...]
    else:
        wait_all(r.vec_in.at[axis - 1, pl.ds(0, 3)], r.vsems.at[1, axis])
        total = (r.vec_in[axis - 1, 0] + r.vec_in[axis - 1, 1]) + (
            r.vec_in[axis - 1, 2] + r.vec_in[axis - 1, 3]
        )
    if axis < 3:
        r.vec_in[axis, place.coords[axis]] = total
        vec_send(axis, r, place)
    else:
        r.vec[...] = total


def vec_drain(r):
    wait_all(r.vec_x, r.vsems.at[0, 0])
    for axis in range(3):
        wait_all(r.vec_in.at[axis, pl.ds(0, 3)], r.vsems.at[0, 1 + axis])


def step_exchange(g, r, place):
    exchange_start(g, r, place)
    if g == 0:
        vec_exchange(r, place)


def step_scatter(g, r, place):
    exchange_done(g, r, place)
    if g == 0:
        vec_step(0, r, place)


def step_between(k, g, r, place):
    scatter_done(k, g, r, place)
    if g == 0:
        vec_step(k + 1, r, place)


SUM_STEPS = (
    step_exchange,
    step_scatter,
    lambda *a: step_between(0, *a),
    lambda *a: step_between(1, *a),
    lambda *a: step_between(2, *a),
    lambda *a: gather_done(2, *a),
    lambda *a: gather_done(1, *a),
    gather_last,
    sum_out,
)
SUM_DURING_BACK = ((3, 2), (4, 3), (5, 4), (6, 5))


WEIGHTS = ["w_query", "w_key", "w_value", "w_out", "w_up", "w_down"]
INPUTS = ["inputs", "groups", "cotangent"] + [name + "_hbm" for name in WEIGHTS]
INPUTS += ["gain_one", "shift_one", "gain_two", "shift_two"]
OUTPUTS = {
    "output": ((1, ROWS, D), BF),
    "input_grad": ((1, ROWS, D), BF),
    "sums0": ((2, 3, 3072, 128), BF),
    "sums1": ((2, 3, 1024, 128), BF),
    "vec": ((8, D), F32),
}
SCRATCH = {
    "w_query": ((D, D), BF),
    "w_key": ((D, D), BF),
    "w_value": ((D, D), BF),
    "w_out": ((D, D), BF),
    "w_up": ((D, FF), BF),
    "w_down": ((FF, D), BF),
    "cot": ((ROWS, D), BF),
    "hid": ((3, ROWS, D), BF),
    "q_out": ((2, 8, 64, 128), BF),
    "q_in": ((2, 16, 64, 128), BF),
    "o_out": ((2, 16, 80, 128), BF),
    "o_in": ((2, 16, 80, 128), BF),
    "do_out": ((2, 8, 80, 128), BF),
    "do_in": ((2, 16, 80, 128), BF),
    "dq_out": ((2, 16, 64, 128), BF),
    "dq_in": ((2, 16, 64, 128), BF),
    "dkv_acc": ((512, 128), F32),
    "dqt": ((8, 64, 256), F32),
    "lq": ((2, 2048, 128), BF),
    "qz": ((2048, 128), BF),
    "ld": ((2048, 128), BF),
    "neg_log": ((16, 8, 128), F32),
    "neg_delta": ((16, 8, 128), F32),
    "f_acc": ((4, 512, 128), F32),
    "f_top": ((4, 512, 128), F32),
    "att": ((2, ROWS, D), F32),
    "log_total": ((2, 8, 128), F32),
    "grp_q": ((16, 8, 128), jnp.int32),
    "kv_out": ((2, 8, ROWS, 128), BF),
    "kv_in": ((2, 32, ROWS, 128), BF),
    "grp_out": ((1, 8, 128), jnp.int32),
    "grp_in": ((32, 8, 128), jnp.int32),
    "ka": ((2, 4096, 128), BF),
    "va": ((2, 4096, 128), BF),
    "kat": ((64, 4096), BF),
    "att_low": ((2, ROWS, D), BF),
    "n_one": ((2, ROWS, D), F32),
    "f_one": ((2, ROWS, 128), F32),
    "first_low": ((2, ROWS, D), BF),
    "pre": ((2, ROWS, FF), F32),
    "act": ((2, ROWS, FF), BF),
    "n_two": ((2, ROWS, D), F32),
    "f_two": ((2, ROWS, 128), F32),
    "work": ((ROWS, D), F32),
    "dy": ((ROWS, D), F32),
    "down_low": ((2, ROWS, D), BF),
    "up_low": ((2, ROWS, FF), BF),
    "out_low": ((2, ROWS, D), BF),
    "dkv_out": ((32, ROWS, 128), BF),
    "dkv_in": ((2, 32, ROWS, 128), BF),
    "dq": ((2, ROWS, D), BF),
    "dk": ((2, ROWS, D), BF),
    "dv": ((2, ROWS, D), BF),
    "vec_own": ((8, D), F32),
    "vec_x": ((8, D), F32),
    "vec_in": ((3, 4, 8, D), F32),
}
for g, rows in enumerate(SUM_ROWS):
    SCRATCH |= {
        f"sum_in{g}": ((6 * rows, 128), BF),
        f"sum_x{g}": ((3 * rows, 128), BF),
        f"sum_r0{g}": ((3, 3, rows // 4, 128), BF),
        f"sum_r1{g}": ((3, 3, rows // 16, 128), BF),
        f"sum_r2{g}": ((3, 3, rows // 64, 128), BF),
        f"sum_s0{g}": ((3, rows // 4, 128), BF),
        f"sum_s1{g}": ((3, rows // 16, 128), BF),
        f"sum_t{g}": ((2, 3, rows, 128), BF),
    }
SEMS = {"sems": (12, 2), "gsems": (4,), "load_sems": (8,), "kv_sems": (2, 4), "sum_sems0": (2, 10, 3), "sum_sems1": (2, 10, 3), "vsems": (3, 4)}


def kernel(*refs):
    names = INPUTS + list(OUTPUTS) + list(SCRATCH) + list(SEMS)
    r = SimpleNamespace(**dict(zip(names, refs)))
    place = Place()
    for name in LOADED:
        load(name, r, place).start()
    greet(place)
    r.vec_own[...] = jnp.zeros_like(r.vec_own)

    @pl.loop(0, 2)
    def _(v):
        @pl.when(v == 0)
        def _():
            for name in LOADED[:4]:
                load(name, r, place).wait()

        project_queries(v, r)
        project_keys_values(v, r)

        @pl.when(v == 0)
        def _():
            all_here()
            send_groups(r, place)

        send_queries(v, r, place)
        send_keys_values(v, r, place)

        @pl.when(v == 0)
        def _():
            wait_all(r.grp_in, r.gsems.at[1])
            wait_all(r.grp_q, r.gsems.at[3])
            make_aug(r)

        wait_all(r.q_in.at[v], r.sems.at[3, v])
        make_queries(v, r)
        attention(v, r, place)

        @pl.when(v == 0)
        def _():
            for name in LOADED[4:7]:
                load(name, r, place).wait()

        wait_all(r.o_in.at[v], r.sems.at[5, v])
        after_attention(v, r)

    r.output[0] = r.hid[2]
    load("cot", r, place).wait()
    r.dy[...] = r.cot[...].astype(F32)

    @pl.loop(0, 2)
    def _(step):
        v = 1 - step
        before_attention_back(v, r)
        send_do(v, r, place)

        @pl.when(v == 0)
        def _():
            weight_grads_early(r)
            SUM_STEPS[0](0, r, place)

        wait_all(r.do_in.at[v], r.sems.at[7, v])

        @pl.when(v == 0)
        def _():
            SUM_STEPS[1](0, r, place)

        attention_back(v, r, place)

        @pl.when(v == 0)
        def _():
            SUM_STEPS[6](0, r, place)

        wait_all(r.dq_in.at[v], r.sems.at[9, v])
        wait_all(r.dkv_in.at[v], r.sems.at[11, v])
        after_attention_back(v, r)
        r.dy[...] = r.work[...].astype(BF).astype(F32)

    r.input_grad[0] = r.dy[...].astype(BF)
    weight_grads_late(r)
    SUM_STEPS[0](1, r, place)
    SUM_STEPS[7](0, r, place)
    for step in SUM_STEPS[1:5]:
        step(1, r, place)
    SUM_STEPS[8](0, r, place)
    for step in SUM_STEPS[5:]:
        step(1, r, place)

    vec_drain(r)
    for g in range(2):
        sum_drain(g, r, place)
    wait_sent(r.grp_in, r.gsems.at[0], place.self_kv, 32)
    wait_sent(r.grp_q, r.gsems.at[2], place.self_q, 16)

    @pl.loop(0, 2)
    def _(v):
        wait_sent(r.kv_in.at[v], r.sems.at[0, v], place.self_kv, 32)
        wait_sent(r.q_in.at[v], r.sems.at[2, v], place.self_q, 16)
        wait_sent(r.o_in.at[v], r.sems.at[4, v], place.self_q, 16)
        wait_sent(r.do_in.at[v], r.sems.at[6, v], place.self_q, 16)
        wait_sent(r.dq_in.at[v], r.sems.at[8, v], place.self_q, 16)

    wait_sent(r.dkv_in.at[0], r.sems.at[10, 0], place.self_kv, 32)


def unpack(output, input_grad, early, late, vec):
    def body(*refs):
        output, input_grad, early, late, vec, output_to, input_grad_to = refs[:7]
        query, key, value, out, up, down = refs[7:13]
        got, small, up_f, down_f, sin, sout = refs[17:]
        loads = []
        for j in range(12):
            src = late.at[pl.ds(4 * j, 4)] if j < 3 else early.at[pl.ds(4 * (j - 3), 4)]
            loads.append(pltpu.make_async_copy(src, got.at[pl.ds(4 * j, 4)], sin.at[j]))
        order = [0, 1, 2, 11, 3, 4, 5, 6, 7, 8, 9, 10]
        for j in order:
            loads[j].start()
        for i in range(4):
            refs[13 + i][...] = vec[i]
        stores = [
            pltpu.make_async_copy(output, output_to, sout.at[12]),
            pltpu.make_async_copy(input_grad, input_grad_to, sout.at[13]),
        ]
        for copy in stores:
            copy.start()

        def store(j, src, dst):
            stores.append(pltpu.make_async_copy(src, dst, sout.at[j]))
            stores[-1].start()

        for j in order:
            loads[j].wait()
            tiles = [got[4 * j + k].astype(F32) for k in range(4)]
            cols = [slice(128 * k, 128 * k + 128) for k in range(4)]
            if j < 3 or j == 11:
                i = min(j, 3)
                for k in range(4):
                    small[i, :, cols[k]] = tiles[k]
                store(j, small.at[i], (query, key, value, out)[i])
            elif j < 7:
                at = 512 * (j - 3)
                for k in range(4):
                    up_f[:, at + 128 * k : at + 128 * k + 128] = tiles[k]
                store(j, up_f.at[:, pl.ds(at, 512)], up.at[:, pl.ds(at, 512)])
            else:
                for k in range(4):
                    down_f[512 * k : 512 * k + 512, cols[j - 7]] = tiles[k]
        store(7, down_f, down)
        for copy in stores:
            copy.wait()

    square, hbm = jax.ShapeDtypeStruct((D, D), F32), pl.BlockSpec(memory_space=pl.ANY)
    vmem = pl.BlockSpec(memory_space=pltpu.VMEM)
    rows = jax.ShapeDtypeStruct((1, ROWS, D), BF)
    shapes = [rows] * 2 + [square] * 4
    shapes += [jax.ShapeDtypeStruct((D, FF), F32), jax.ShapeDtypeStruct((FF, D), F32)]
    return pl.pallas_call(
        body,
        out_shape=shapes + [jax.ShapeDtypeStruct((D,), F32)] * 4,
        in_specs=[hbm] * 4 + [vmem],
        out_specs=[hbm] * 8 + [vmem] * 4,
        scratch_shapes=[
            pltpu.VMEM((48, 512, 128), BF),
            pltpu.VMEM((4, D, D), F32),
            pltpu.VMEM((D, FF), F32),
            pltpu.VMEM((FF, D), F32),
            pltpu.SemaphoreType.DMA((12,)),
            pltpu.SemaphoreType.DMA((14,)),
        ],
        compiler_params=pltpu.CompilerParams(vmem_limit_bytes=60 * 2**20),
        name="unpack",
    )(output, input_grad, early, late, vec)


def on_device(inputs, groups, cotangent, *params):
    vectors = [x.reshape(1, D) for x in params[6:]]
    vmem = pl.BlockSpec(memory_space=pltpu.VMEM)
    out = pl.pallas_call(
        kernel,
        out_shape=[jax.ShapeDtypeStruct(shape, kind) for shape, kind in OUTPUTS.values()],
        in_specs=[
            pl.BlockSpec(memory_space=pl.ANY) if n.endswith("_hbm") or n in ("inputs", "cotangent") else vmem
            for n in INPUTS
        ],
        out_specs=[
            pl.BlockSpec(memory_space=pl.ANY) if n.startswith("sums") else vmem for n in OUTPUTS
        ],
        scratch_shapes=[pltpu.VMEM(shape, kind) for shape, kind in SCRATCH.values()]
        + [pltpu.SemaphoreType.DMA(shape) for shape in SEMS.values()],
        compiler_params=pltpu.CompilerParams(
            collective_id=0, has_side_effects=True, vmem_limit_bytes=62 * 2**20
        ),
        name="visits",
    )(inputs, groups, cotangent, *params[:6], *vectors)
    return unpack(*out[:2], out[2].reshape(36, 512, 128), out[3].reshape(12, 512, 128), out[4])


def solution(mesh):
    rows = P(None, "dp", None)
    return jax.shard_map(
        on_device,
        mesh=mesh,
        in_specs=(rows, P(None, "dp"), rows) + (P(),) * 10,
        out_specs=(P("section", "dp", None),) * 2 + (P(),) * 10,
        check_vma=False,
    )
```

```python
from types import SimpleNamespace

import jax
import jax.numpy as jnp
from jax import lax
from jax.experimental import pallas as pl
from jax.experimental.pallas import tpu as pltpu
from jax.sharding import PartitionSpec as P

F32, BF = jnp.float32, jnp.bfloat16
BIG = 1e30
ROWS, D, FF, HEADS = 128, 512, 2048, 8
MESH = pl.DeviceIdType.MESH


def nt(a, b):
    return lax.dot_general(a, b, (((1,), (1,)), ((), ())), preferred_element_type=F32)


def nn(a, b):
    return lax.dot_general(a, b, (((1,), (0,)), ((), ())), preferred_element_type=F32)


def tn(a, b):
    return lax.dot_general(a, b, (((0,), (0,)), ((), ())), preferred_element_type=F32)


def lanes(shape):
    return lax.broadcasted_iota(jnp.int32, shape, len(shape) - 1)


def subs(shape):
    return lax.broadcasted_iota(jnp.int32, shape, len(shape) - 2)


def ds(start, size):
    if isinstance(start, int):
        return pl.ds(start, size)
    return pl.ds(pl.multiple_of(start, size), size)


def split3(x):
    a = x.astype(BF).astype(F32)
    b = (x - a).astype(BF).astype(F32)
    return a, b, (x - a - b).astype(BF).astype(F32)


def tile_of(r, t):
    return 4 * r + (r + t) % 4


def mean(x):
    return jnp.mean(x, axis=-1, keepdims=True)


def norm(x):
    centred = x - mean(x)
    factor = lax.rsqrt(mean(centred * centred) + 1e-05)
    return centred * factor, factor


def norm_back(dy, n, factor, gain):
    u = dy * gain
    return factor * (u - mean(u) - n * mean(u * n))


GELU_C = 0.7978845608028654


def gelu(x):
    return 0.5 * x * (1.0 + jnp.tanh(GELU_C * (x + 0.044715 * x * x * x)))


def gelu_slope(x):
    sq = x * x
    th = jnp.tanh(GELU_C * x * (1.0 + 0.044715 * sq))
    return 0.5 * (1.0 + th) + 0.5 * x * (1.0 - th * th) * (GELU_C * (1.0 + 3 * 0.044715 * sq))


class Place:
    def __init__(self):
        self.me = lax.axis_index("dp")
        self.s = lax.axis_index("section")
        me = self.me
        self.coords = (me % 4, me // 16, (me // 4) % 4)
        x, y, z = self.coords
        self.t = (x + y + z) % 4
        self.head = 4 * (y % 2) + x
        self.micro = y // 2
        self.own_t = ((me // 2) % 4 - me // 8 + 32) % 4
        self.own_slot = 2 * (me // 8) + me % 2
        mine = self.micro == self.s
        self.self_kv = mine & (me % 2 == self.s)
        self.self_q = mine & (self.own_t == self.t)

    def along(self, axis, d):
        c = self.coords[axis]
        return self.me + ((c + d) % 4 - c) * (1, 16, 4)[axis]

    def chip_in_plane(self, h):
        return 16 * (2 * self.s + h // 4) + 4 * self.coords[2] + h % 4

    def chip(self, h, t):
        x, y = h % 4, 2 * self.s + h // 4
        return 16 * y + 4 * ((t - x - y + 8) % 4) + x

    def send(self, src, dst, send_sem, recv_sem, section, dp):
        to_self = (section == self.s) & (dp == self.me)

        @pl.when(jnp.logical_not(to_self))
        def _():
            pltpu.make_async_remote_copy(
                src_ref=src,
                dst_ref=dst,
                send_sem=send_sem,
                recv_sem=recv_sem,
                device_id=(section, dp),
                device_id_type=MESH,
            ).start()

        @pl.when(to_self)
        def _():
            pltpu.make_async_copy(src, dst, recv_sem).start()


def remote(src, dst, send_sem, recv_sem, section, dp):
    pltpu.make_async_remote_copy(
        src_ref=src,
        dst_ref=dst,
        send_sem=send_sem,
        recv_sem=recv_sem,
        device_id=(section, dp),
        device_id_type=MESH,
    ).start()


def wait_all(ref, sem):
    pltpu.make_async_copy(ref, ref, sem).wait()


def wait_sent(ref, sem, to_self, count):
    @pl.when(to_self)
    def _():
        wait_all(ref.at[pl.ds(0, count - 1)], sem)

    @pl.when(jnp.logical_not(to_self))
    def _():
        wait_all(ref.at[pl.ds(0, count)], sem)


def greet(place):
    sem = pltpu.get_barrier_semaphore()

    @pl.loop(1, 128)
    def _(k):
        other = (place.s * 64 + place.me + k) % 128
        pl.semaphore_signal(sem, inc=1, device_id=(other // 64, other % 64), device_id_type=MESH)


def all_here():
    pl.semaphore_wait(pltpu.get_barrier_semaphore(), 127)


LOADED = ["hid", "w_query", "w_key", "w_value", "w_out", "w_up", "w_down", "cot"]


def load(name, r, place):
    if name == "hid":
        return pltpu.make_async_copy(r.inputs.at[place.s], r.hid.at[0], r.load_sems.at[0])
    if name == "cot":
        return pltpu.make_async_copy(r.cotangent.at[place.s], r.cot, r.load_sems.at[7])
    return pltpu.make_async_copy(
        getattr(r, name + "_hbm"), getattr(r, name), r.load_sems.at[LOADED.index(name)]
    )


def pack(tile, odd):
    low = lanes((64, 128)) < 64
    if odd:
        return jnp.where(low, pltpu.roll(tile[:64], 64, 1), tile[64:])
    return jnp.where(low, tile[:64], pltpu.roll(tile[64:], 64, 1))


def spread(packed, odd):
    turned = pltpu.roll(packed, 64, 1)
    return jnp.concatenate([turned, packed] if odd else [packed, turned], axis=0)


def parts_in_rows(rows):
    at = subs((16, 128))
    out = jnp.zeros((16, 128), F32)
    for i, part in enumerate(rows):
        out = jnp.where(at == i, part, out)
    return out.astype(BF)


def project_queries(v, r):
    q = nn(r.hid[v], r.w_query[...]).astype(BF).astype(F32) * 0.125
    for h in range(HEADS):
        tile = q[:, 128 * (h // 2) : 128 * (h // 2) + 128]
        r.q_out[v, h] = pack(tile, h % 2 == 1).astype(BF)


def project_keys_values(v, r):
    hid = r.hid[v]
    k = nn(hid, r.w_key[...]).astype(BF).astype(F32)
    w = nn(hid, r.w_value[...]).astype(BF).astype(F32)
    low = lanes((ROWS, 128)) < 64
    for h in range(HEADS):
        cols = slice(128 * (h // 2), 128 * (h // 2) + 128)
        kt, vt = k[:, cols], w[:, cols]
        if h % 2 == 0:
            vt = pltpu.roll(vt, 64, 1)
        else:
            kt = pltpu.roll(kt, 64, 1)
        r.kv_out[v, h] = jnp.where(low, kt, vt).astype(BF)


def to_queries(src, dst, send_sem, recv_sem, place):
    @pl.loop(0, HEADS)
    def _(a):
        h = (place.me // 4 + a) % 8
        for b in range(2):
            core, chip = (place.me + b) % 2, place.chip(h, place.own_t)
            place.send(src(h), dst.at[place.own_slot], send_sem, recv_sem, core, chip)


def to_keys(src, dst, send_sem, recv_sem, place):
    n = place.me // 2

    @pl.loop(0, HEADS)
    def _(a):
        h = 2 * ((n // 8 + a // 2) % 4) + (n // 4 + a) % 2
        for b in range(4):
            chip = place.chip(h, (n + b) % 4)
            place.send(src(h), dst.at[n], send_sem, recv_sem, place.me % 2, chip)


def send_queries(v, r, place):
    to_queries(
        lambda h: r.q_out.at[v, h], r.q_in.at[v], r.sems.at[2, v], r.sems.at[3, v], place
    )


def send_keys_values(v, r, place):
    x, y, _ = place.coords
    n = place.me // 2

    @pl.loop(0, HEADS)
    def _(a):
        h = 2 * ((n // 8 + a // 2) % 4) + (n // 4 + a) % 2
        place.send(
            r.kv_out.at[v, h],
            r.kv_in.at[v, n],
            r.sems.at[0, v],
            r.plane_sems.at[v, 2 * y + x // 2],
            x % 2,
            place.chip_in_plane(h),
        )


def pass_on(v, r, place):
    z = place.coords[2]

    @pl.loop(0, 4)
    def _(y):
        for b in range(2):
            block = r.kv_in.at[v, 8 * y + 2 * z + b]
            wait_all(block, r.plane_sems.at[v, 2 * y + b])
            for d in (2, 1, 3):
                to = place.along(2, d)
                remote(block, block, r.sems.at[1, v], r.kv_sems.at[v, y], place.s, to)


def send_groups(r, place):
    r.grp_out[0] = jnp.broadcast_to(r.groups[pl.ds(place.s, 1), :], (8, 128))
    to_queries(lambda h: r.grp_out.at[0], r.grp_q, r.gsems.at[2], r.gsems.at[3], place)
    to_keys(lambda h: r.grp_out.at[0], r.grp_in, r.gsems.at[0], r.gsems.at[1], place)


def column_of(row):
    return jnp.transpose(jnp.broadcast_to(row.astype(F32), (128, 128)))


def make_aug(r):
    ln = lanes((ROWS, 128))
    inside = (ln >= 64) & (ln < 68)

    @pl.loop(0, 32)
    def _(n):
        g = column_of(r.grp_in[n][0:1, :]).astype(jnp.int32)
        aug = jnp.where(inside & (ln - 64 != g), -BIG, 0.0).astype(BF)
        for v in range(2):
            r.ka[v, ds(n * 128, 128), :] = aug

    @pl.loop(0, 16)
    def _(n):
        g = column_of(r.grp_q[n][0:1, :]).astype(jnp.int32)
        aug = jnp.where(ln - 64 == g, 1.0, 0.0).astype(BF)
        for v in range(2):
            r.lq[v, ds(n * 128, 128), :] = aug


def make_queries(v, r):
    low = lanes((ROWS, 128)) < 64

    @pl.loop(0, 16)
    def _(n):
        rows = ds(n * 128, 128)
        q = spread(r.q_in[v, n].astype(F32), False)
        r.lq[v, rows, :] = jnp.where(low, q, r.lq[v, rows, :].astype(F32)).astype(BF)


def make_kv(v, c, r):
    ln = lanes((ROWS, 128))
    low = ln < 64
    ones = jnp.where(ln < 1, 1.0, 0.0)

    @pl.loop(0, 8)
    def _(k):
        n = 8 * c + k
        rows = ds(n * 128, 128)
        kv = r.kv_in[v, n].astype(F32)
        r.ka[v, rows, :] = jnp.where(low, kv, r.ka[v, rows, :].astype(F32)).astype(BF)
        r.va[v, rows, :] = jnp.where(low, ones, kv).astype(BF)


def fwd_body(v, c, j, masked, r, place):
    width = 1024
    rows = ds(c * width, width)
    sc = nt(r.lq[v, ds(512 * j, 512), :], r.ka[v, rows, :])
    if masked:
        col, row = lanes((512, width)), subs((512, width))
        tiles = [tile_of(2 * j + k, place.t) for k in range(2)]
        at = 256 * (col // 128) + col % 128 + (2048 * c + 128 * place.s)
        limit = row % 256 + 256 * jnp.where(row < 256, tiles[0], tiles[1])
        sc = jnp.where(at <= limit, sc, -BIG)
    top = r.f_top[j][:, 0:1]
    new = jnp.maximum(top, jnp.max(sc, axis=1, keepdims=True))
    p = jnp.exp(sc - new).astype(BF)
    r.f_acc[j] = r.f_acc[j] * jnp.exp(top - new) + nn(p, r.va[v, rows, :])
    r.f_top[j] = jnp.broadcast_to(new, (512, 128))


def fwd_finish(v, j, r, place):
    acc = r.f_acc[j]
    total = acc[:, 0:1]
    out = acc / total
    logs = jnp.broadcast_to(r.f_top[j][:, 0:1] + jnp.log(total), (512, 128))
    for k in range(4):
        rows = slice(128 * k, 128 * k + 128)
        r.o_out[v, 4 * j + k, 0:64] = pack(out[rows], True).astype(BF)
        row = jnp.transpose(logs[rows])[0:1]
        r.o_out[v, 4 * j + k, 64:80] = parts_in_rows(split3(row))
    for k in range(2):
        for turn in range(2):
            half = (turn + place.s) % 2
            place.send(
                r.o_out.at[v, 4 * j + 2 * k + half],
                r.o_in.at[v, 2 * place.head + place.s],
                r.sems.at[4, v],
                r.sems.at[5, v],
                place.micro,
                2 * tile_of(2 * j + k, place.t) + half,
            )


def attention(v, r, place):
    r.f_acc[...] = jnp.zeros_like(r.f_acc)
    r.f_top[...] = jnp.full_like(r.f_top, -2 * BIG)

    @pl.loop(0, 4)
    def _(c):
        wait_all(r.kv_in.at[v, pl.ds(0, 6)], r.kv_sems.at[v, c])
        make_kv(v, c, r)
        fwd_body(v, c, c, True, r, place)
        fwd_finish(v, c, r, place)

        @pl.loop(c + 1, 4)
        def _(j):
            fwd_body(v, c, j, False, r, place)


def after_attention(v, r):
    low = lanes((ROWS, 128)) < 64
    weights = [[], []]
    for h in range(HEADS):
        logs = []
        for core in range(2):
            x = r.o_in[v, 2 * h + core, 64:80].astype(F32)
            logs.append(x[0:1] + x[1:2] + x[2:3])
        top = jnp.maximum(logs[0], logs[1])
        w = [jnp.exp(x - top) for x in logs]
        total = w[0] + w[1]
        r.log_total[v, h : h + 1] = top + jnp.log(total)
        for core in range(2):
            weights[core].append(w[core] / total)
    cols = jnp.transpose(jnp.concatenate(weights[0] + weights[1] + [jnp.zeros((112, 128), F32)], axis=0))
    for i in range(HEADS // 2):
        whole = []
        for h in (2 * i, 2 * i + 1):
            got = [spread(r.o_in[v, 2 * h + k, 0:64].astype(F32), h % 2 == 1) for k in range(2)]
            whole.append(got[0] * cols[:, h : h + 1] + got[1] * cols[:, 8 + h : 9 + h])
        pair = jnp.where(low, whole[0], whole[1])
        r.att[v, :, 128 * i : 128 * i + 128] = pair
        r.att_low[v, :, 128 * i : 128 * i + 128] = pair.astype(BF)
    mixed = r.hid[v].astype(F32) + nn(r.att_low[v], r.w_out[...])
    n_one, f_one = norm(mixed)
    first = n_one * r.gain_one[...] + r.shift_one[...]
    first_low = first.astype(BF)
    r.n_one[v] = n_one
    r.f_one[v] = jnp.broadcast_to(f_one, (ROWS, 128))
    r.first_low[v] = first_low
    r.work[...] = first

    @pl.loop(0, 4)
    def _(j):
        cols = ds(j * 512, 512)
        pre = nn(r.first_low[v], r.w_up[:, cols])
        r.pre[v, :, cols] = pre
        act = gelu(pre).astype(BF)
        r.act[v, :, cols] = act
        r.work[...] += nn(act, r.w_down[cols, :])

    n_two, f_two = norm(r.work[...])
    r.n_two[v] = n_two
    r.f_two[v] = jnp.broadcast_to(f_two, (ROWS, 128))
    r.hid[v + 1] = (n_two * r.gain_two[...] + r.shift_two[...]).astype(BF)


def before_attention_back(v, r):
    dy = r.dy[...]
    n_two = r.n_two[v]
    r.vec_own[2:3, :] += jnp.sum(dy * n_two, axis=0, keepdims=True)
    r.vec_own[3:4, :] += jnp.sum(dy, axis=0, keepdims=True)
    grad_two = norm_back(dy, n_two, r.f_two[v][:, 0:1], r.gain_two[...])
    r.down_low[v] = grad_two.astype(BF)
    r.work[...] = grad_two

    @pl.loop(0, 4)
    def _(j):
        cols = ds(j * 512, 512)
        grad = nt(r.down_low[v], r.w_down[cols, :])
        up = (grad * gelu_slope(r.pre[v, :, cols])).astype(BF)
        r.up_low[v, :, cols] = up
        r.work[...] += nt(up, r.w_up[:, cols])

    dz = r.work[...]
    n_one = r.n_one[v]
    r.vec_own[0:1, :] += jnp.sum(dz * n_one, axis=0, keepdims=True)
    r.vec_own[1:2, :] += jnp.sum(dz, axis=0, keepdims=True)
    grad_one = norm_back(dz, n_one, r.f_one[v][:, 0:1], r.gain_one[...])
    out_low = grad_one.astype(BF)
    r.out_low[v] = out_low
    r.work[...] = grad_one
    grad_att = nt(out_low, r.w_out[...]).astype(BF).astype(F32)
    ln = lanes((ROWS, 128))
    low = ln < 64
    deltas = jnp.zeros((ROWS, 128), F32)
    for h in range(HEADS):
        cols = slice(128 * (h // 2), 128 * (h // 2) + 128)
        product = grad_att[:, cols] * r.att[v, :, cols]
        mine = jnp.where(low, product, 0.0) if h % 2 == 0 else jnp.where(low, 0.0, product)
        deltas = jnp.where(ln == h, jnp.sum(mine, axis=1, keepdims=True), deltas)
    deltas = jnp.transpose(deltas)
    for h in range(HEADS):
        tile = grad_att[:, 128 * (h // 2) : 128 * (h // 2) + 128]
        r.do_out[v, h, 0:64] = pack(tile, h % 2 == 1).astype(BF)
        rows = split3(-deltas[h : h + 1]) + split3(-r.log_total[v, h : h + 1])
        r.do_out[v, h, 64:80] = parts_in_rows(rows)


def send_do(v, r, place):
    to_queries(
        lambda h: r.do_out.at[v, h], r.do_in.at[v], r.sems.at[6, v], r.sems.at[7, v], place
    )


def prepare_back(v, r):
    low = lanes((ROWS, 128)) < 64

    @pl.loop(0, 16)
    def _(n):
        rows = ds(n * 128, 128)
        r.qz[rows, :] = jnp.where(low, r.lq[v, rows, :].astype(F32), 0.0).astype(BF)

    @pl.loop(0, 8)
    def _(i):
        rows = ds(i * 512, 512)
        r.kat[:, rows] = jnp.transpose(r.ka[v, rows, :].astype(F32))[:64].astype(BF)

    r.dqt[...] = jnp.zeros_like(r.dqt)


def take_do(v, r):
    low = lanes((ROWS, 128)) < 64

    @pl.loop(0, 16)
    def _(n):
        do = spread(r.do_in[v, n, 0:64].astype(F32), True)
        r.ld[ds(n * 128, 128), :] = jnp.where(low, 0.0, do).astype(BF)
        x = r.do_in[v, n, 64:80].astype(F32)
        r.neg_delta[n] = jnp.broadcast_to(x[0:1] + x[1:2] + x[2:3], (8, 128))
        r.neg_log[n] = jnp.broadcast_to(x[3:4] + x[4:5] + x[5:6], (8, 128))


def bwd_body(v, c, tiles, masked, r, place):
    rows = ds(c * 512, 512)
    probs, grads = [], []
    for i in tiles:
        mine = ds(i * 256, 256)
        x = nt(r.ka[v, rows, :], r.lq[v, mine, :])
        x = x + jnp.concatenate([r.neg_log[2 * i][0:1], r.neg_log[2 * i + 1][0:1]], axis=1)
        if masked:
            row, col = subs((512, 256)), lanes((512, 256))
            shift = 1024 * c + 128 * place.s - 256 * tile_of(i, place.t)
            x = jnp.where(256 * (row // 128) + row % 128 + shift <= col, x, -BIG)
        p = jnp.exp(x)
        dp = nt(r.va[v, rows, :], r.ld[mine, :])
        dp = dp + jnp.concatenate([r.neg_delta[2 * i][0:1], r.neg_delta[2 * i + 1][0:1]], axis=1)
        probs.append(p.astype(BF))
        grads.append((p * dp).astype(BF))
    size = 256 * len(tiles)
    queries = pl.ds(pl.multiple_of(tiles[0] * 256, 256), size)
    r.dkv_acc[...] += nn(jnp.concatenate(grads, axis=1), r.qz[queries, :]) + nn(
        jnp.concatenate(probs, axis=1), r.ld[queries, :]
    )
    for i, dsc in zip(tiles, grads):
        r.dqt[i] += nn(r.kat[:, rows], dsc)


def bwd_finish(v, i, r, place):
    dq = jnp.transpose(jnp.concatenate([r.dqt[i], jnp.zeros((64, 256), F32)], axis=0))
    for k in range(2):
        r.dq_out[v, 2 * i + k] = pack(dq[128 * k : 128 * k + 128], False).astype(BF)
    for turn in range(2):
        half = (turn + place.s) % 2
        place.send(
            r.dq_out.at[v, 2 * i + half],
            r.dq_in.at[v, 2 * place.head + place.s],
            r.sems.at[8, v],
            r.sems.at[9, v],
            place.micro,
            2 * tile_of(i, place.t) + half,
        )


def chunk_at(a, place):
    first = (a // 2 + place.head) % 4
    return jnp.where(a % 2 == 0, first, 7 - first)


def attention_back(v, r, place):
    take_do(v, r)

    @pl.when(v == 0)
    def _():
        wait_sent(r.dkv_in.at[1], r.sems.at[10, 1], place.self_kv, 32)

    @pl.loop(0, 8)
    def _(a):
        first = (a // 2 + place.head) % 4
        c = jnp.where(a % 2 == 0, first, 7 - first)

        @pl.loop(0, jnp.where(a == 7, c, 0))
        def _(i):
            bwd_finish(v, i, r, place)

        r.dkv_acc[...] = jnp.zeros_like(r.dkv_acc)

        @pl.when(c % 2 == 0)
        def _():
            bwd_body(v, c, [c, c + 1], True, r, place)

        @pl.when(c % 2 == 1)
        def _():
            bwd_body(v, c, [c], True, r, place)

        @pl.loop(c // 2 + 1, 4)
        def _(m):
            bwd_body(v, c, [2 * m, 2 * m + 1], False, r, place)

        for b in range(4):
            k = (b + place.t) % 4
            n = 4 * c + k
            r.dkv_out[n] = r.dkv_acc[ds(k * 128, 128), :].astype(BF)
            place.send(
                r.dkv_out.at[n],
                r.dkv_in.at[v, 4 * place.head + place.t],
                r.sems.at[10, v],
                r.sems.at[11, v],
                place.micro,
                2 * n + place.s,
            )
        for after, step in SUM_DURING_BACK:

            @pl.when((v == 0) & (a == after))
            def _():
                SUM_STEPS[step](0, r, place)

    @pl.loop(7 - (3 + place.head) % 4, 8)
    def _(i):
        bwd_finish(v, i, r, place)


def take_gradients(v, r):
    low = lanes((ROWS, 128)) < 64
    for i in range(HEADS // 2):
        cols = slice(128 * i, 128 * i + 128)
        dq, dkv = [], []
        for h in (2 * i, 2 * i + 1):
            both = r.dq_in[v, 2 * h].astype(F32) + r.dq_in[v, 2 * h + 1].astype(F32)
            dq.append(spread(both * 0.125, h % 2 == 1))
            four = [r.dkv_in[v, 4 * h + t].astype(F32) for t in range(4)]
            dkv.append((four[0] + four[1]) + (four[2] + four[3]))
        r.dq[v, :, cols] = jnp.where(low, dq[0], dq[1]).astype(BF)
        r.dk[v, :, cols] = jnp.where(low, dkv[0], pltpu.roll(dkv[1], 64, 1)).astype(BF)
        r.dv[v, :, cols] = jnp.where(low, pltpu.roll(dkv[0], 64, 1), dkv[1]).astype(BF)


def input_gradient(v, r):
    return (
        r.work[...]
        + nt(r.dq[v], r.w_query[...])
        + nt(r.dk[v], r.w_key[...])
        + nt(r.dv[v], r.w_value[...])
    ).astype(BF)


def both(ref):
    return jnp.concatenate([ref[0], ref[1]], axis=0)


def put(ref, unit, tile):
    ref[ds(unit * 512, 512), :] = tile.astype(BF)


def weight_grads_early(r):
    @pl.loop(0, 4)
    def _(j):
        cols = ds(j * 512, 512)
        up = jnp.concatenate([r.up_low[0, :, cols], r.up_low[1, :, cols]], axis=0)
        grad = tn(both(r.first_low), up)
        for k in range(4):
            put(r.sum_in0, 4 * j + k, grad[:, 128 * k : 128 * k + 128])
        act = jnp.concatenate([r.act[0, :, cols], r.act[1, :, cols]], axis=0)
        grad = tn(act, both(r.down_low))
        for k in range(4):
            put(r.sum_in0, 16 + 4 * k + j, grad[:, 128 * k : 128 * k + 128])

    grad = tn(both(r.att_low), both(r.out_low))
    for k in range(4):
        put(r.sum_in0, 32 + k, grad[:, 128 * k : 128 * k + 128])


def weight_grads_late(r):
    hid = jnp.concatenate([r.hid[0], r.hid[1]], axis=0)
    for i, ref in enumerate((r.dq, r.dk, r.dv)):
        grad = tn(hid, both(ref))
        for k in range(4):
            put(r.sum_in1, 4 * i + k, grad[:, 128 * k : 128 * k + 128])


SUM_ROWS = (3072, 1024)
ORDERS = ((0, 1, 2), (1, 2, 0), (2, 0, 1))
PLANE = [(d, e) for d in range(4) for e in range(4) if (d, e) != (0, 0)]


def sum_refs(g, r):
    names = ("in", "x", "r0", "r1", "s0", "t", "sems")
    return SimpleNamespace(**{n: getattr(r, "sum_" + n + str(g)) for n in names})


def offsets(p, rows, place):
    first, second, third = [place.coords[axis] for axis in ORDERS[p]]
    at = first * (rows // 4)
    return at, at + (4 * second + third) * (rows // 64)


def exchange_start(g, r, place):
    q, rows = sum_refs(g, r), SUM_ROWS[g]
    for p in range(3):
        remote(
            q.__dict__["in"].at[ds((1 - place.s) * 3 * rows + p * rows, rows)],
            q.x.at[pl.ds(p * rows, rows)],
            q.sems.at[0, 0, p],
            q.sems.at[1, 0, p],
            1 - place.s,
            place.me,
        )


def axis_send(p, base, q, g, src, place):
    size = SUM_ROWS[g] // 4
    axis = ORDERS[p][0]
    for d in (2, 1, 3):
        c = (place.coords[axis] + d) % 4
        remote(
            src.at[ds(base + c * size, size)],
            q.r0.at[p, d - 1],
            q.sems.at[0, 1, p],
            q.sems.at[1, 1, p],
            place.s,
            place.along(axis, d),
        )


def plane_send(p, q, g, place):
    size = SUM_ROWS[g] // 64
    second, third = ORDERS[p][1:]
    for d, e in PLANE:
        block = 4 * ((place.coords[second] + d) % 4) + (place.coords[third] + e) % 4
        remote(
            q.s0.at[p, ds(block * size, size)],
            q.r1.at[p, 4 * d + e - 1],
            q.sems.at[0, 2, p],
            q.sems.at[1, 2, p],
            place.s,
            place.along(second, d) + place.along(third, e) - place.me,
        )


def exchange_done(g, r, place):
    q, rows = sum_refs(g, r), SUM_ROWS[g]
    src = q.__dict__["in"]
    for p in range(3):
        base = place.s * 3 * rows + p * rows
        wait_all(q.x.at[pl.ds(p * rows, rows)], q.sems.at[1, 0, p])

        @pl.loop(0, rows // 512)
        def _(k):
            at = ds(base + k * 512, 512)
            other = q.x[ds(p * rows + k * 512, 512), :]
            src[at, :] = (src[at, :].astype(F32) + other.astype(F32)).astype(BF)

        axis_send(p, base, q, g, src, place)


def axis_done(g, r, place):
    q, rows = sum_refs(g, r), SUM_ROWS[g]
    size = rows // 4
    for p in range(3):
        wait_all(q.r0.at[p], q.sems.at[1, 1, p])
        at = place.s * 3 * rows + p * rows + place.coords[ORDERS[p][0]] * size
        total = q.__dict__["in"][ds(at, size), :].astype(F32)
        for d in range(3):
            total = total + q.r0[p, d].astype(F32)
        q.s0[p] = total.astype(BF)
        plane_send(p, q, g, place)


def plane_done(g, r, place):
    q, rows = sum_refs(g, r), SUM_ROWS[g]
    size = rows // 64
    for p in range(3):
        wait_all(q.r1.at[p], q.sems.at[1, 2, p])
        second, third = [place.coords[axis] for axis in ORDERS[p][1:]]
        total = q.s0[p, ds((4 * second + third) * size, size), :].astype(F32)
        for d in range(15):
            total = total + q.r1[p, d].astype(F32)
        block = q.t.at[place.s, p, ds(offsets(p, rows, place)[1], size)]
        block[...] = total.astype(BF)
        for d, e in PLANE:
            to = place.along(ORDERS[p][1], d) + place.along(ORDERS[p][2], e) - place.me
            remote(block, block, q.sems.at[0, 3, p], q.sems.at[1, 3, p], place.s, to)


def cross_send(p, start, size, q, place):
    block = q.t.at[place.s, p, ds(start, size)]
    remote(block, block, q.sems.at[0, 4, p], q.sems.at[1, 4, p], 1 - place.s, place.me)


def plane_back(g, r, place):
    q, rows = sum_refs(g, r), SUM_ROWS[g]
    for p in range(3):
        wait_all(q.t.at[0, p, pl.ds(0, 15 * rows // 64)], q.sems.at[1, 3, p])
        at, axis = offsets(p, rows, place)[0], ORDERS[p][0]
        block = q.t.at[place.s, p, ds(at, rows // 4)]
        for d in (2, 1, 3):
            send_sem, recv_sem = q.sems.at[0, 4 + d, p], q.sems.at[1, 4 + d, p]
            remote(block, block, send_sem, recv_sem, place.s, place.along(axis, d))
        cross_send(p, at, rows // 4, q, place)


def gather_last(g, r, place):
    q, rows = sum_refs(g, r), SUM_ROWS[g]
    size = rows // 4
    for d in (1, 3, 2):
        for p in range(3):
            wait_all(q.t.at[0, p, pl.ds(0, size)], q.sems.at[1, 4 + d, p])
            c = (place.coords[ORDERS[p][0]] - d + 4) % 4
            cross_send(p, c * size, size, q, place)


def sum_out(g, r, place):
    q = sum_refs(g, r)
    for p in range(3):
        wait_all(q.t.at[0, p], q.sems.at[1, 4, p])
    pltpu.make_async_copy(q.t, (r.sums0, r.sums1)[g], r.vsems.at[2, g]).start()


def sum_drain(g, r, place):
    q, rows = sum_refs(g, r), SUM_ROWS[g]
    for p in range(3):
        wait_all(q.x.at[pl.ds(0, rows)], q.sems.at[0, 0, p])
        wait_all(q.r0.at[p], q.sems.at[0, 1, p])
        for k in (2, 3):
            wait_all(q.r1.at[p], q.sems.at[0, k, p])
        for d in range(1, 4):
            wait_all(q.t.at[0, p, pl.ds(0, rows // 4)], q.sems.at[0, 4 + d, p])
        wait_all(q.t.at[0, p], q.sems.at[0, 4, p])
    pltpu.make_async_copy(q.t, (r.sums0, r.sums1)[g], r.vsems.at[2, g]).wait()


def vec_exchange(r, place):
    remote(r.vec_own, r.vec_x, r.vsems.at[0, 0], r.vsems.at[1, 0], 1 - place.s, place.me)


def vec_send(axis, r, place):
    c = place.coords[axis]
    for d in (1, 2, 3):
        remote(
            r.vec_in.at[axis, c],
            r.vec_in.at[axis, c],
            r.vsems.at[0, 1 + axis],
            r.vsems.at[1, 1 + axis],
            place.s,
            place.along(axis, d),
        )


def vec_step(axis, r, place):
    if axis == 0:
        wait_all(r.vec_x, r.vsems.at[1, 0])
        total = r.vec_own[...] + r.vec_x[...]
    else:
        wait_all(r.vec_in.at[axis - 1, pl.ds(0, 3)], r.vsems.at[1, axis])
        total = (r.vec_in[axis - 1, 0] + r.vec_in[axis - 1, 1]) + (
            r.vec_in[axis - 1, 2] + r.vec_in[axis - 1, 3]
        )
    if axis < 3:
        r.vec_in[axis, place.coords[axis]] = total
        vec_send(axis, r, place)
    else:
        r.vec[...] = total


def vec_drain(r):
    wait_all(r.vec_x, r.vsems.at[0, 0])
    for axis in range(3):
        wait_all(r.vec_in.at[axis, pl.ds(0, 3)], r.vsems.at[0, 1 + axis])


def step_exchange(g, r, place):
    exchange_start(g, r, place)
    if g == 0:
        vec_exchange(r, place)


def step_scatter(g, r, place):
    exchange_done(g, r, place)
    if g == 0:
        vec_step(0, r, place)


def step_axis(g, r, place):
    axis_done(g, r, place)
    if g == 0:
        vec_step(1, r, place)


def step_plane(g, r, place):
    plane_done(g, r, place)
    if g == 0:
        vec_step(2, r, place)


def step_back(g, r, place):
    plane_back(g, r, place)
    if g == 0:
        vec_step(3, r, place)


SUM_STEPS = (
    step_exchange,
    step_scatter,
    step_axis,
    step_plane,
    step_back,
    gather_last,
    sum_out,
)
SUM_DURING_BACK = ((7, 2),)
SUM_AFTER_BACK = (3,)
SUM_TAIL = ((0, 4), (1, 1), (1, 2), (0, 5), (1, 3), (0, 6), (1, 4), (1, 5), (1, 6))


WEIGHTS = ["w_query", "w_key", "w_value", "w_out", "w_up", "w_down"]
INPUTS = ["inputs", "groups", "cotangent"] + [name + "_hbm" for name in WEIGHTS]
INPUTS += ["gain_one", "shift_one", "gain_two", "shift_two"]
OUTPUTS = {
    "output": ((1, ROWS, D), BF),
    "input_grad": ((1, ROWS, D), BF),
    "sums0": ((2, 3, 3072, 128), BF),
    "sums1": ((2, 3, 1024, 128), BF),
    "vec": ((8, D), F32),
}
SCRATCH = {
    "w_query": ((D, D), BF),
    "w_key": ((D, D), BF),
    "w_value": ((D, D), BF),
    "w_out": ((D, D), BF),
    "w_up": ((D, FF), BF),
    "w_down": ((FF, D), BF),
    "cot": ((ROWS, D), BF),
    "hid": ((3, ROWS, D), BF),
    "q_out": ((2, 8, 64, 128), BF),
    "q_in": ((2, 16, 64, 128), BF),
    "o_out": ((2, 16, 80, 128), BF),
    "o_in": ((2, 16, 80, 128), BF),
    "do_out": ((2, 8, 80, 128), BF),
    "do_in": ((2, 16, 80, 128), BF),
    "dq_out": ((2, 16, 64, 128), BF),
    "dq_in": ((2, 16, 64, 128), BF),
    "dkv_acc": ((512, 128), F32),
    "dqt": ((8, 64, 256), F32),
    "lq": ((2, 2048, 128), BF),
    "qz": ((2048, 128), BF),
    "ld": ((2048, 128), BF),
    "neg_log": ((16, 8, 128), F32),
    "neg_delta": ((16, 8, 128), F32),
    "f_acc": ((4, 512, 128), F32),
    "f_top": ((4, 512, 128), F32),
    "att": ((2, ROWS, D), F32),
    "log_total": ((2, 8, 128), F32),
    "grp_q": ((16, 8, 128), jnp.int32),
    "kv_out": ((2, 8, ROWS, 128), BF),
    "kv_in": ((2, 32, ROWS, 128), BF),
    "grp_out": ((1, 8, 128), jnp.int32),
    "grp_in": ((32, 8, 128), jnp.int32),
    "ka": ((2, 4096, 128), BF),
    "va": ((2, 4096, 128), BF),
    "kat": ((64, 4096), BF),
    "att_low": ((2, ROWS, D), BF),
    "n_one": ((2, ROWS, D), F32),
    "f_one": ((2, ROWS, 128), F32),
    "first_low": ((2, ROWS, D), BF),
    "pre": ((2, ROWS, FF), F32),
    "act": ((2, ROWS, FF), BF),
    "n_two": ((2, ROWS, D), F32),
    "f_two": ((2, ROWS, 128), F32),
    "work": ((ROWS, D), F32),
    "dy": ((ROWS, D), F32),
    "down_low": ((2, ROWS, D), BF),
    "up_low": ((2, ROWS, FF), BF),
    "out_low": ((2, ROWS, D), BF),
    "dkv_out": ((32, ROWS, 128), BF),
    "dkv_in": ((2, 32, ROWS, 128), BF),
    "dq": ((2, ROWS, D), BF),
    "dk": ((2, ROWS, D), BF),
    "dv": ((2, ROWS, D), BF),
    "vec_own": ((8, D), F32),
    "vec_x": ((8, D), F32),
    "vec_in": ((3, 4, 8, D), F32),
}
for g, rows in enumerate(SUM_ROWS):
    SCRATCH |= {
        f"sum_in{g}": ((6 * rows, 128), BF),
        f"sum_x{g}": ((3 * rows, 128), BF),
        f"sum_r0{g}": ((3, 3, rows // 4, 128), BF),
        f"sum_r1{g}": ((3, 15, rows // 64, 128), BF),
        f"sum_s0{g}": ((3, rows // 4, 128), BF),
        f"sum_t{g}": ((2, 3, rows, 128), BF),
    }
SEMS = {"sems": (12, 2), "gsems": (4,), "load_sems": (8,), "kv_sems": (2, 4), "plane_sems": (2, 8), "sum_sems0": (2, 8, 3), "sum_sems1": (2, 8, 3), "vsems": (3, 4)}


def kernel(*refs):
    names = INPUTS + list(OUTPUTS) + list(SCRATCH) + list(SEMS)
    r = SimpleNamespace(**dict(zip(names, refs)))
    place = Place()
    for name in LOADED:
        load(name, r, place).start()
    greet(place)
    r.vec_own[...] = jnp.zeros_like(r.vec_own)

    @pl.loop(0, 2)
    def _(v):
        @pl.when(v == 0)
        def _():
            for name in LOADED[:4]:
                load(name, r, place).wait()

        project_queries(v, r)
        project_keys_values(v, r)

        @pl.when(v == 0)
        def _():
            all_here()
            send_groups(r, place)

        send_queries(v, r, place)
        send_keys_values(v, r, place)
        pass_on(v, r, place)

        @pl.when(v == 0)
        def _():
            wait_all(r.grp_in, r.gsems.at[1])
            wait_all(r.grp_q, r.gsems.at[3])
            make_aug(r)

        wait_all(r.q_in.at[v], r.sems.at[3, v])
        make_queries(v, r)
        attention(v, r, place)

        @pl.when(v == 0)
        def _():
            for name in LOADED[4:7]:
                load(name, r, place).wait()

        wait_all(r.o_in.at[v], r.sems.at[5, v])
        after_attention(v, r)

    r.output[0] = r.hid[2]
    load("cot", r, place).wait()
    r.dy[...] = r.cot[...].astype(F32)

    @pl.loop(0, 2)
    def _(step):
        v = 1 - step
        before_attention_back(v, r)
        send_do(v, r, place)

        @pl.when(v == 0)
        def _():
            weight_grads_early(r)
            SUM_STEPS[0](0, r, place)

        prepare_back(v, r)
        wait_all(r.do_in.at[v], r.sems.at[7, v])

        @pl.when(v == 0)
        def _():
            SUM_STEPS[1](0, r, place)

        attention_back(v, r, place)

        @pl.when(v == 0)
        def _():
            for step in SUM_AFTER_BACK:
                SUM_STEPS[step](0, r, place)

        wait_all(r.dq_in.at[v], r.sems.at[9, v])
        wait_all(r.dkv_in.at[v], r.sems.at[11, v])
        take_gradients(v, r)

        @pl.when(v == 1)
        def _():
            r.dy[...] = input_gradient(v, r).astype(F32)

    weight_grads_late(r)
    SUM_STEPS[0](1, r, place)
    r.input_grad[0] = input_gradient(0, r)
    for g, step in SUM_TAIL:
        SUM_STEPS[step](g, r, place)

    vec_drain(r)
    for g in range(2):
        sum_drain(g, r, place)
    wait_sent(r.grp_in, r.gsems.at[0], place.self_kv, 32)
    wait_sent(r.grp_q, r.gsems.at[2], place.self_q, 16)

    @pl.loop(0, 2)
    def _(v):
        wait_sent(r.kv_in.at[v], r.sems.at[0, v], place.self_kv, 8)
        wait_all(r.kv_in.at[v, pl.ds(0, 24)], r.sems.at[1, v])
        wait_sent(r.q_in.at[v], r.sems.at[2, v], place.self_q, 16)
        wait_sent(r.o_in.at[v], r.sems.at[4, v], place.self_q, 16)
        wait_sent(r.do_in.at[v], r.sems.at[6, v], place.self_q, 16)
        wait_sent(r.dq_in.at[v], r.sems.at[8, v], place.self_q, 16)

    wait_sent(r.dkv_in.at[0], r.sems.at[10, 0], place.self_kv, 32)


def unpack(output, input_grad, early, late, vec):
    def body(*refs):
        output, input_grad, early, late, vec, output_to, input_grad_to = refs[:7]
        query, key, value, out, up, down = refs[7:13]
        got, small, up_f, down_f, vec_in, vec_out, sin, sout = refs[17:]
        loads = []
        for j in range(12):
            src = late.at[pl.ds(4 * j, 4)] if j < 3 else early.at[pl.ds(4 * (j - 3), 4)]
            loads.append(pltpu.make_async_copy(src, got.at[pl.ds(4 * j, 4)], sin.at[j]))
        order = [7, 8, 9, 10, 3, 4, 5, 6, 0, 1, 2, 11]
        for j in order:
            loads[j].start()
        get_vec = pltpu.make_async_copy(vec, vec_in, sin.at[12])
        get_vec.start()
        stores = [
            pltpu.make_async_copy(output, output_to, sout.at[12]),
            pltpu.make_async_copy(input_grad, input_grad_to, sout.at[13]),
        ]
        for copy in stores:
            copy.start()

        def store(j, src, dst):
            stores.append(pltpu.make_async_copy(src, dst, sout.at[j]))
            stores[-1].start()

        for j in order:
            loads[j].wait()
            tiles = [got[4 * j + k].astype(F32) for k in range(4)]
            cols = [slice(128 * k, 128 * k + 128) for k in range(4)]
            if j < 3 or j == 11:
                i = min(j, 3)
                for k in range(4):
                    small[i, :, cols[k]] = tiles[k]
                store(j, small.at[i], (query, key, value, out)[i])
            elif j < 7:
                at = 512 * (j - 3)
                for k in range(4):
                    up_f[:, at + 128 * k : at + 128 * k + 128] = tiles[k]
                store(j, up_f.at[:, pl.ds(at, 512)], up.at[:, pl.ds(at, 512)])
            else:
                for k in range(4):
                    down_f[512 * k : 512 * k + 512, cols[j - 7]] = tiles[k]
                if j == 10:
                    store(7, down_f, down)
        get_vec.wait()
        for i in range(4):
            vec_out[i, 0] = vec_in[i]
            copy = pltpu.make_async_copy(vec_out.at[i, 0], refs[13 + i], sout.at[14 + i])
            copy.start()
            stores.append(copy)
        for copy in stores:
            copy.wait()

    square, hbm = jax.ShapeDtypeStruct((D, D), F32), pl.BlockSpec(memory_space=pl.ANY)
    rows = jax.ShapeDtypeStruct((1, ROWS, D), BF)
    shapes = [rows] * 2 + [square] * 4
    shapes += [jax.ShapeDtypeStruct((D, FF), F32), jax.ShapeDtypeStruct((FF, D), F32)]
    return pl.pallas_call(
        body,
        out_shape=shapes + [jax.ShapeDtypeStruct((D,), F32)] * 4,
        in_specs=[hbm] * 5,
        out_specs=[hbm] * 12,
        scratch_shapes=[
            pltpu.VMEM((48, 512, 128), BF),
            pltpu.VMEM((4, D, D), F32),
            pltpu.VMEM((D, FF), F32),
            pltpu.VMEM((FF, D), F32),
            pltpu.VMEM((8, D), F32),
            pltpu.VMEM((4, 1, D), F32),
            pltpu.SemaphoreType.DMA((13,)),
            pltpu.SemaphoreType.DMA((18,)),
        ],
        compiler_params=pltpu.CompilerParams(vmem_limit_bytes=60 * 2**20),
        name="unpack",
    )(output, input_grad, early, late, vec)


def on_device(inputs, groups, cotangent, *params):
    vectors = [x.reshape(1, D) for x in params[6:]]
    vmem = pl.BlockSpec(memory_space=pltpu.VMEM)
    out = pl.pallas_call(
        kernel,
        out_shape=[jax.ShapeDtypeStruct(shape, kind) for shape, kind in OUTPUTS.values()],
        in_specs=[
            pl.BlockSpec(memory_space=pl.ANY) if n.endswith("_hbm") or n in ("inputs", "cotangent") else vmem
            for n in INPUTS
        ],
        out_specs=[
            pl.BlockSpec(memory_space=pl.ANY) if n.startswith("sums") else vmem for n in OUTPUTS
        ],
        scratch_shapes=[pltpu.VMEM(shape, kind) for shape, kind in SCRATCH.values()]
        + [pltpu.SemaphoreType.DMA(shape) for shape in SEMS.values()],
        compiler_params=pltpu.CompilerParams(
            collective_id=0, has_side_effects=True, vmem_limit_bytes=62 * 2**20
        ),
        name="visits",
    )(inputs, groups, cotangent, *params[:6], *vectors)
    return unpack(*out[:2], out[2].reshape(36, 512, 128), out[3].reshape(12, 512, 128), out[4])


def solution(mesh):
    rows = P(None, "dp", None)
    return jax.shard_map(
        on_device,
        mesh=mesh,
        in_specs=(rows, P(None, "dp"), rows) + (P(),) * 10,
        out_specs=(P("section", "dp", None),) * 2 + (P(),) * 10,
        check_vma=False,
    )
```

```python
from types import SimpleNamespace

import jax
import jax.numpy as jnp
from jax import lax
from jax.experimental import pallas as pl
from jax.experimental.pallas import tpu as pltpu
from jax.sharding import PartitionSpec as P

F32, BF = jnp.float32, jnp.bfloat16
BIG = 1e30
ROWS, D, FF, HEADS = 128, 512, 2048, 8
MESH = pl.DeviceIdType.MESH


def nt(a, b):
    return lax.dot_general(a, b, (((1,), (1,)), ((), ())), preferred_element_type=F32)


def nn(a, b):
    return lax.dot_general(a, b, (((1,), (0,)), ((), ())), preferred_element_type=F32)


def tn(a, b):
    return lax.dot_general(a, b, (((0,), (0,)), ((), ())), preferred_element_type=F32)


def lanes(shape):
    return lax.broadcasted_iota(jnp.int32, shape, len(shape) - 1)


def subs(shape):
    return lax.broadcasted_iota(jnp.int32, shape, len(shape) - 2)


def ds(start, size):
    if isinstance(start, int):
        return pl.ds(start, size)
    return pl.ds(pl.multiple_of(start, size), size)


def split3(x):
    a = x.astype(BF).astype(F32)
    b = (x - a).astype(BF).astype(F32)
    return a, b, (x - a - b).astype(BF).astype(F32)


def tile_of(r, t):
    return 4 * r + (r + t) % 4


def mean(x):
    return jnp.mean(x, axis=-1, keepdims=True)


def norm(x):
    centred = x - mean(x)
    factor = lax.rsqrt(mean(centred * centred) + 1e-05)
    return centred * factor, factor


def norm_back(dy, n, factor, gain):
    u = dy * gain
    return factor * (u - mean(u) - n * mean(u * n))


GELU_C = 0.7978845608028654


def gelu(x):
    return 0.5 * x * (1.0 + jnp.tanh(GELU_C * (x + 0.044715 * x * x * x)))


def gelu_slope(x):
    sq = x * x
    th = jnp.tanh(GELU_C * x * (1.0 + 0.044715 * sq))
    return 0.5 * (1.0 + th) + 0.5 * x * (1.0 - th * th) * (GELU_C * (1.0 + 3 * 0.044715 * sq))


class Place:
    def __init__(self):
        self.me = lax.axis_index("dp")
        self.s = lax.axis_index("section")
        me = self.me
        self.coords = (me % 4, me // 16, (me // 4) % 4)
        x, y, z = self.coords
        self.t = (x + y + z) % 4
        self.head = 4 * (y % 2) + x
        self.micro = y // 2
        self.own_t = ((me // 2) % 4 - me // 8 + 32) % 4
        self.own_slot = 2 * (me // 8) + me % 2
        mine = self.micro == self.s
        self.self_kv = mine & (me % 2 == self.s)
        self.self_q = mine & (self.own_t == self.t)

    def along(self, axis, d):
        c = self.coords[axis]
        return self.me + ((c + d) % 4 - c) * (1, 16, 4)[axis]

    def chip_in_plane(self, h):
        return 16 * (2 * self.s + h // 4) + 4 * self.coords[2] + h % 4

    def chip(self, h, t):
        x, y = h % 4, 2 * self.s + h // 4
        return 16 * y + 4 * ((t - x - y + 8) % 4) + x

    def send(self, src, dst, send_sem, recv_sem, section, dp):
        to_self = (section == self.s) & (dp == self.me)

        @pl.when(jnp.logical_not(to_self))
        def _():
            pltpu.make_async_remote_copy(
                src_ref=src,
                dst_ref=dst,
                send_sem=send_sem,
                recv_sem=recv_sem,
                device_id=(section, dp),
                device_id_type=MESH,
            ).start()

        @pl.when(to_self)
        def _():
            pltpu.make_async_copy(src, dst, recv_sem).start()


def remote(src, dst, send_sem, recv_sem, section, dp):
    pltpu.make_async_remote_copy(
        src_ref=src,
        dst_ref=dst,
        send_sem=send_sem,
        recv_sem=recv_sem,
        device_id=(section, dp),
        device_id_type=MESH,
    ).start()


def wait_all(ref, sem):
    pltpu.make_async_copy(ref, ref, sem).wait()


def wait_sent(ref, sem, to_self, count):
    @pl.when(to_self)
    def _():
        wait_all(ref.at[pl.ds(0, count - 1)], sem)

    @pl.when(jnp.logical_not(to_self))
    def _():
        wait_all(ref.at[pl.ds(0, count)], sem)


def greet(place):
    sem = pltpu.get_barrier_semaphore()

    @pl.loop(1, 128)
    def _(k):
        other = (place.s * 64 + place.me + k) % 128
        pl.semaphore_signal(sem, inc=1, device_id=(other // 64, other % 64), device_id_type=MESH)


def all_here():
    pl.semaphore_wait(pltpu.get_barrier_semaphore(), 127)


LOADED = ["hid", "w_query", "w_key", "w_value", "groups", "w_out", "w_up", "w_down", "gain_one"]
LOADED += ["shift_one", "gain_two", "shift_two", "cot"]


def load(name, r, place):
    sem = r.load_sems.at[LOADED.index(name)]
    if name == "hid":
        return pltpu.make_async_copy(r.inputs.at[place.s], r.hid.at[0], sem)
    if name == "cot":
        return pltpu.make_async_copy(r.cotangent.at[place.s], r.cot, sem)
    return pltpu.make_async_copy(getattr(r, name + "_hbm"), getattr(r, name), sem)


def pack(tile, odd):
    low = lanes((64, 128)) < 64
    if odd:
        return jnp.where(low, pltpu.roll(tile[:64], 64, 1), tile[64:])
    return jnp.where(low, tile[:64], pltpu.roll(tile[64:], 64, 1))


def spread(packed, odd):
    turned = pltpu.roll(packed, 64, 1)
    return jnp.concatenate([turned, packed] if odd else [packed, turned], axis=0)


def parts_in_rows(rows):
    at = subs((16, 128))
    out = jnp.zeros((16, 128), F32)
    for i, part in enumerate(rows):
        out = jnp.where(at == i, part, out)
    return out.astype(BF)


def project_queries(v, r):
    q = nn(r.hid[v], r.w_query[...]).astype(BF).astype(F32) * 0.125
    for h in range(HEADS):
        tile = q[:, 128 * (h // 2) : 128 * (h // 2) + 128]
        r.q_out[v, h] = pack(tile, h % 2 == 1).astype(BF)


def project_keys_values(v, r):
    hid = r.hid[v]
    k = nn(hid, r.w_key[...]).astype(BF).astype(F32)
    w = nn(hid, r.w_value[...]).astype(BF).astype(F32)
    low = lanes((ROWS, 128)) < 64
    for h in range(HEADS):
        cols = slice(128 * (h // 2), 128 * (h // 2) + 128)
        kt, vt = k[:, cols], w[:, cols]
        if h % 2 == 0:
            vt = pltpu.roll(vt, 64, 1)
        else:
            kt = pltpu.roll(kt, 64, 1)
        r.kv_out[v, h] = jnp.where(low, kt, vt).astype(BF)


def to_queries(src, dst, send_sem, recv_sem, place):
    @pl.loop(0, HEADS)
    def _(a):
        h = (place.me // 4 + a) % 8
        for b in range(2):
            core, chip = (place.me + b) % 2, place.chip(h, place.own_t)
            place.send(src(h), dst.at[place.own_slot], send_sem, recv_sem, core, chip)


def to_keys(src, dst, send_sem, recv_sem, place):
    n = place.me // 2

    @pl.loop(0, HEADS)
    def _(a):
        h = 2 * ((n // 8 + a // 2) % 4) + (n // 4 + a) % 2
        for b in range(4):
            chip = place.chip(h, (n + b) % 4)
            place.send(src(h), dst.at[n], send_sem, recv_sem, place.me % 2, chip)


def send_queries(v, r, place):
    to_queries(
        lambda h: r.q_out.at[v, h], r.q_in.at[v], r.sems.at[2, v], r.sems.at[3, v], place
    )


def send_keys_values(v, r, place):
    x, y, _ = place.coords
    n = place.me // 2

    @pl.loop(0, HEADS)
    def _(a):
        h = 2 * ((n // 8 + a // 2) % 4) + (n // 4 + a) % 2
        place.send(
            r.kv_out.at[v, h],
            r.kv_in.at[v, n],
            r.sems.at[0, v],
            r.plane_sems.at[v, 2 * y + x // 2],
            x % 2,
            place.chip_in_plane(h),
        )


def pass_on(v, r, place):
    z = place.coords[2]

    @pl.loop(0, 4)
    def _(y):
        for b in range(2):
            block = r.kv_in.at[v, 8 * y + 2 * z + b]
            wait_all(block, r.plane_sems.at[v, 2 * y + b])
            for d in (2, 1, 3):
                to = place.along(2, d)
                remote(block, block, r.sems.at[1, v], r.kv_sems.at[v, y], place.s, to)


def send_groups(r, place):
    r.grp_out[0] = jnp.broadcast_to(r.groups[pl.ds(place.s, 1), :], (8, 128))
    to_queries(lambda h: r.grp_out.at[0], r.grp_q, r.gsems.at[2], r.gsems.at[3], place)
    to_keys(lambda h: r.grp_out.at[0], r.grp_in, r.gsems.at[0], r.gsems.at[1], place)


def column_of(row):
    return jnp.transpose(jnp.broadcast_to(row.astype(F32), (128, 128)))


def make_aug(r):
    ln = lanes((ROWS, 128))
    inside = (ln >= 64) & (ln < 68)

    @pl.loop(0, 32)
    def _(n):
        g = column_of(r.grp_in[n][0:1, :]).astype(jnp.int32)
        aug = jnp.where(inside & (ln - 64 != g), -BIG, 0.0).astype(BF)
        for v in range(2):
            r.ka[v, ds(n * 128, 128), :] = aug

    @pl.loop(0, 16)
    def _(n):
        g = column_of(r.grp_q[n][0:1, :]).astype(jnp.int32)
        aug = jnp.where(ln - 64 == g, 1.0, 0.0).astype(BF)
        for v in range(2):
            r.lq[v, ds(n * 128, 128), :] = aug


def make_queries(v, r):
    low = lanes((ROWS, 128)) < 64

    @pl.loop(0, 16)
    def _(n):
        rows = ds(n * 128, 128)
        q = spread(r.q_in[v, n].astype(F32), False)
        r.lq[v, rows, :] = jnp.where(low, q, r.lq[v, rows, :].astype(F32)).astype(BF)


def make_kv(v, c, r):
    ln = lanes((ROWS, 128))
    low = ln < 64
    ones = jnp.where(ln < 1, 1.0, 0.0)

    @pl.loop(0, 8)
    def _(k):
        n = 8 * c + k
        rows = ds(n * 128, 128)
        kv = r.kv_in[v, n].astype(F32)
        r.ka[v, rows, :] = jnp.where(low, kv, r.ka[v, rows, :].astype(F32)).astype(BF)
        r.va[v, rows, :] = jnp.where(low, ones, kv).astype(BF)


def fwd_body(v, c, j, masked, r, place):
    width = 1024
    rows = ds(c * width, width)
    sc = nt(r.lq[v, ds(512 * j, 512), :], r.ka[v, rows, :])
    if masked:
        col, row = lanes((512, width)), subs((512, width))
        tiles = [tile_of(2 * j + k, place.t) for k in range(2)]
        at = 256 * (col // 128) + col % 128 + (2048 * c + 128 * place.s)
        limit = row % 256 + 256 * jnp.where(row < 256, tiles[0], tiles[1])
        sc = jnp.where(at <= limit, sc, -BIG)
    top = r.f_top[j][:, 0:1]
    new = jnp.maximum(top, jnp.max(sc, axis=1, keepdims=True))
    p = jnp.exp(sc - new).astype(BF)
    r.f_acc[j] = r.f_acc[j] * jnp.exp(top - new) + nn(p, r.va[v, rows, :])
    r.f_top[j] = jnp.broadcast_to(new, (512, 128))


def fwd_finish(v, j, r, place):
    acc = r.f_acc[j]
    total = acc[:, 0:1]
    out = acc / total
    logs = jnp.broadcast_to(r.f_top[j][:, 0:1] + jnp.log(total), (512, 128))
    for k in range(4):
        rows = slice(128 * k, 128 * k + 128)
        r.o_out[v, 4 * j + k, 0:64] = pack(out[rows], True).astype(BF)
        row = jnp.transpose(logs[rows])[0:1]
        r.o_out[v, 4 * j + k, 64:80] = parts_in_rows(split3(row))
    for k in range(2):
        for turn in range(2):
            half = (turn + place.s) % 2
            place.send(
                r.o_out.at[v, 4 * j + 2 * k + half],
                r.o_in.at[v, 2 * place.head + place.s],
                r.sems.at[4, v],
                r.sems.at[5, v],
                place.micro,
                2 * tile_of(2 * j + k, place.t) + half,
            )


def attention(v, r, place):
    r.f_acc[...] = jnp.zeros_like(r.f_acc)
    r.f_top[...] = jnp.full_like(r.f_top, -2 * BIG)

    @pl.loop(0, 4)
    def _(c):
        wait_all(r.kv_in.at[v, pl.ds(0, 6)], r.kv_sems.at[v, c])
        make_kv(v, c, r)
        fwd_body(v, c, c, True, r, place)
        fwd_finish(v, c, r, place)

        @pl.loop(c + 1, 4)
        def _(j):
            fwd_body(v, c, j, False, r, place)


def after_attention(v, r):
    low = lanes((ROWS, 128)) < 64
    weights = [[], []]
    for h in range(HEADS):
        logs = []
        for core in range(2):
            x = r.o_in[v, 2 * h + core, 64:80].astype(F32)
            logs.append(x[0:1] + x[1:2] + x[2:3])
        top = jnp.maximum(logs[0], logs[1])
        w = [jnp.exp(x - top) for x in logs]
        total = w[0] + w[1]
        r.log_total[v, h : h + 1] = top + jnp.log(total)
        for core in range(2):
            weights[core].append(w[core] / total)
    cols = jnp.transpose(jnp.concatenate(weights[0] + weights[1] + [jnp.zeros((112, 128), F32)], axis=0))
    for i in range(HEADS // 2):
        whole = []
        for h in (2 * i, 2 * i + 1):
            got = [spread(r.o_in[v, 2 * h + k, 0:64].astype(F32), h % 2 == 1) for k in range(2)]
            whole.append(got[0] * cols[:, h : h + 1] + got[1] * cols[:, 8 + h : 9 + h])
        pair = jnp.where(low, whole[0], whole[1])
        r.att[v, :, 128 * i : 128 * i + 128] = pair
        r.att_low[v, :, 128 * i : 128 * i + 128] = pair.astype(BF)
    mixed = r.hid[v].astype(F32) + nn(r.att_low[v], r.w_out[...])
    n_one, f_one = norm(mixed)
    first = n_one * r.gain_one[...] + r.shift_one[...]
    first_low = first.astype(BF)
    r.n_one[v] = n_one
    r.f_one[v] = jnp.broadcast_to(f_one, (ROWS, 128))
    r.first_low[v] = first_low
    r.work[...] = first

    @pl.loop(0, 4)
    def _(j):
        cols = ds(j * 512, 512)
        pre = nn(r.first_low[v], r.w_up[:, cols])
        r.pre[v, :, cols] = pre
        act = gelu(pre).astype(BF)
        r.act[v, :, cols] = act
        r.work[...] += nn(act, r.w_down[cols, :])

    n_two, f_two = norm(r.work[...])
    r.n_two[v] = n_two
    r.f_two[v] = jnp.broadcast_to(f_two, (ROWS, 128))
    r.hid[v + 1] = (n_two * r.gain_two[...] + r.shift_two[...]).astype(BF)


def before_attention_back(v, r):
    dy = r.dy[...]
    n_two = r.n_two[v]
    r.vec_own[2:3, :] += jnp.sum(dy * n_two, axis=0, keepdims=True)
    r.vec_own[3:4, :] += jnp.sum(dy, axis=0, keepdims=True)
    grad_two = norm_back(dy, n_two, r.f_two[v][:, 0:1], r.gain_two[...])
    r.down_low[v] = grad_two.astype(BF)
    r.work[...] = grad_two

    @pl.loop(0, 4)
    def _(j):
        cols = ds(j * 512, 512)
        grad = nt(r.down_low[v], r.w_down[cols, :])
        up = (grad * gelu_slope(r.pre[v, :, cols])).astype(BF)
        r.up_low[v, :, cols] = up
        r.work[...] += nt(up, r.w_up[:, cols])

    dz = r.work[...]
    n_one = r.n_one[v]
    r.vec_own[0:1, :] += jnp.sum(dz * n_one, axis=0, keepdims=True)
    r.vec_own[1:2, :] += jnp.sum(dz, axis=0, keepdims=True)
    grad_one = norm_back(dz, n_one, r.f_one[v][:, 0:1], r.gain_one[...])
    out_low = grad_one.astype(BF)
    r.out_low[v] = out_low
    r.work[...] = grad_one
    grad_att = nt(out_low, r.w_out[...]).astype(BF).astype(F32)
    ln = lanes((ROWS, 128))
    low = ln < 64
    deltas = jnp.zeros((ROWS, 128), F32)
    for h in range(HEADS):
        cols = slice(128 * (h // 2), 128 * (h // 2) + 128)
        product = grad_att[:, cols] * r.att[v, :, cols]
        mine = jnp.where(low, product, 0.0) if h % 2 == 0 else jnp.where(low, 0.0, product)
        deltas = jnp.where(ln == h, jnp.sum(mine, axis=1, keepdims=True), deltas)
    deltas = jnp.transpose(deltas)
    for h in range(HEADS):
        tile = grad_att[:, 128 * (h // 2) : 128 * (h // 2) + 128]
        r.do_out[v, h, 0:64] = pack(tile, h % 2 == 1).astype(BF)
        rows = split3(-deltas[h : h + 1]) + split3(-r.log_total[v, h : h + 1])
        r.do_out[v, h, 64:80] = parts_in_rows(rows)


def send_do(v, r, place):
    to_queries(
        lambda h: r.do_out.at[v, h], r.do_in.at[v], r.sems.at[6, v], r.sems.at[7, v], place
    )


def prepare_back(v, r):
    low = lanes((ROWS, 128)) < 64

    @pl.loop(0, 16)
    def _(n):
        rows = ds(n * 128, 128)
        r.qz[rows, :] = jnp.where(low, r.lq[v, rows, :].astype(F32), 0.0).astype(BF)

    @pl.loop(0, 8)
    def _(i):
        rows = ds(i * 512, 512)
        r.kat[:, rows] = jnp.transpose(r.ka[v, rows, :].astype(F32))[:64].astype(BF)

    r.dqt[...] = jnp.zeros_like(r.dqt)


def take_do(v, r):
    low = lanes((ROWS, 128)) < 64

    @pl.loop(0, 16)
    def _(n):
        do = spread(r.do_in[v, n, 0:64].astype(F32), True)
        r.ld[ds(n * 128, 128), :] = jnp.where(low, 0.0, do).astype(BF)
        x = r.do_in[v, n, 64:80].astype(F32)
        r.neg_delta[n] = jnp.broadcast_to(x[0:1] + x[1:2] + x[2:3], (8, 128))
        r.neg_log[n] = jnp.broadcast_to(x[3:4] + x[4:5] + x[5:6], (8, 128))


def bwd_body(v, c, tiles, masked, r, place):
    rows = ds(c * 512, 512)
    probs, grads = [], []
    for i in tiles:
        mine = ds(i * 256, 256)
        x = nt(r.ka[v, rows, :], r.lq[v, mine, :])
        x = x + jnp.concatenate([r.neg_log[2 * i][0:1], r.neg_log[2 * i + 1][0:1]], axis=1)
        if masked:
            row, col = subs((512, 256)), lanes((512, 256))
            shift = 1024 * c + 128 * place.s - 256 * tile_of(i, place.t)
            x = jnp.where(256 * (row // 128) + row % 128 + shift <= col, x, -BIG)
        p = jnp.exp(x)
        dp = nt(r.va[v, rows, :], r.ld[mine, :])
        dp = dp + jnp.concatenate([r.neg_delta[2 * i][0:1], r.neg_delta[2 * i + 1][0:1]], axis=1)
        probs.append(p.astype(BF))
        grads.append((p * dp).astype(BF))
    size = 256 * len(tiles)
    queries = pl.ds(pl.multiple_of(tiles[0] * 256, 256), size)
    r.dkv_acc[...] += nn(jnp.concatenate(grads, axis=1), r.qz[queries, :]) + nn(
        jnp.concatenate(probs, axis=1), r.ld[queries, :]
    )
    for i, dsc in zip(tiles, grads):
        r.dqt[i] += nn(r.kat[:, rows], dsc)


def bwd_finish(v, i, r, place):
    dq = jnp.transpose(jnp.concatenate([r.dqt[i], jnp.zeros((64, 256), F32)], axis=0))
    for k in range(2):
        r.dq_out[v, 2 * i + k] = pack(dq[128 * k : 128 * k + 128], False).astype(BF)
    for turn in range(2):
        half = (turn + place.s) % 2
        place.send(
            r.dq_out.at[v, 2 * i + half],
            r.dq_in.at[v, 2 * place.head + place.s],
            r.sems.at[8, v],
            r.sems.at[9, v],
            place.micro,
            2 * tile_of(i, place.t) + half,
        )


def chunk_at(a, place):
    first = (a // 2 + place.head) % 4
    return jnp.where(a % 2 == 0, first, 7 - first)


def chunk_at(a, place):
    first = (a // 2 + place.coords[0] + place.t) % 4
    return jnp.where((a + place.coords[1]) % 2 == 0, first, 7 - first)


def attention_back(v, r, place):
    take_do(v, r)

    @pl.when(v == 0)
    def _():
        wait_sent(r.dkv_in.at[1], r.sems.at[10, 1], place.self_kv, 32)

    @pl.loop(0, 8)
    def _(a):
        c = chunk_at(a, place)

        @pl.loop(0, jnp.where(a == 7, c, 0))
        def _(i):
            bwd_finish(v, i, r, place)

        r.dkv_acc[...] = jnp.zeros_like(r.dkv_acc)

        @pl.when(c % 2 == 0)
        def _():
            bwd_body(v, c, [c, c + 1], True, r, place)

        @pl.when(c % 2 == 1)
        def _():
            bwd_body(v, c, [c], True, r, place)

        @pl.loop(c // 2 + 1, 4)
        def _(m):
            bwd_body(v, c, [2 * m, 2 * m + 1], False, r, place)

        for b in range(4):
            k = (b + place.t) % 4
            n = 4 * c + k
            r.dkv_out[n] = r.dkv_acc[ds(k * 128, 128), :].astype(BF)
            place.send(
                r.dkv_out.at[n],
                r.dkv_in.at[v, 4 * place.head + place.t],
                r.sems.at[10, v],
                r.sems.at[11, v],
                place.micro,
                2 * n + place.s,
            )
        for after, step in SUM_DURING_BACK:

            @pl.when((v == 0) & (a == after))
            def _():
                SUM_STEPS[step](0, r, place)

    @pl.loop(chunk_at(7, place), 8)
    def _(i):
        bwd_finish(v, i, r, place)


def take_gradients(v, r):
    low = lanes((ROWS, 128)) < 64
    for i in range(HEADS // 2):
        cols = slice(128 * i, 128 * i + 128)
        dq, dkv = [], []
        for h in (2 * i, 2 * i + 1):
            both = r.dq_in[v, 2 * h].astype(F32) + r.dq_in[v, 2 * h + 1].astype(F32)
            dq.append(spread(both * 0.125, h % 2 == 1))
            four = [r.dkv_in[v, 4 * h + t].astype(F32) for t in range(4)]
            dkv.append((four[0] + four[1]) + (four[2] + four[3]))
        r.dq[v, :, cols] = jnp.where(low, dq[0], dq[1]).astype(BF)
        r.dk[v, :, cols] = jnp.where(low, dkv[0], pltpu.roll(dkv[1], 64, 1)).astype(BF)
        r.dv[v, :, cols] = jnp.where(low, pltpu.roll(dkv[0], 64, 1), dkv[1]).astype(BF)


def input_gradient(v, r):
    return (
        r.work[...]
        + nt(r.dq[v], r.w_query[...])
        + nt(r.dk[v], r.w_key[...])
        + nt(r.dv[v], r.w_value[...])
    ).astype(BF)


def both(ref):
    return jnp.concatenate([ref[0], ref[1]], axis=0)


def put(ref, unit, tile):
    ref[ds(unit * 512, 512), :] = tile.astype(BF)


def weight_grads_early(r):
    @pl.loop(0, 4)
    def _(j):
        cols = ds(j * 512, 512)
        up = jnp.concatenate([r.up_low[0, :, cols], r.up_low[1, :, cols]], axis=0)
        grad = tn(both(r.first_low), up)
        for k in range(4):
            put(r.sum_in0, 4 * j + k, grad[:, 128 * k : 128 * k + 128])
        act = jnp.concatenate([r.act[0, :, cols], r.act[1, :, cols]], axis=0)
        grad = tn(act, both(r.down_low))
        for k in range(4):
            put(r.sum_in0, 16 + 4 * k + j, grad[:, 128 * k : 128 * k + 128])

    grad = tn(both(r.att_low), both(r.out_low))
    for k in range(4):
        put(r.sum_in0, 32 + k, grad[:, 128 * k : 128 * k + 128])


def weight_grads_late(r):
    hid = jnp.concatenate([r.hid[0], r.hid[1]], axis=0)
    for i, ref in enumerate((r.dq, r.dk, r.dv)):
        grad = tn(hid, both(ref))
        for k in range(4):
            put(r.sum_in1, 4 * i + k, grad[:, 128 * k : 128 * k + 128])


SUM_ROWS = (3072, 1024)
ORDERS = ((0, 1, 2), (1, 2, 0), (2, 0, 1))
PLANE = [(d, e) for d in range(4) for e in range(4) if (d, e) != (0, 0)]


def sum_refs(g, r):
    names = ("in", "x", "r0", "r1", "s0", "t", "sems")
    return SimpleNamespace(**{n: getattr(r, "sum_" + n + str(g)) for n in names})


def offsets(p, rows, place):
    first, second, third = [place.coords[axis] for axis in ORDERS[p]]
    at = first * (rows // 4)
    return at, at + (4 * second + third) * (rows // 64)


def exchange_start(g, r, place):
    q, rows = sum_refs(g, r), SUM_ROWS[g]
    for p in range(3):
        remote(
            q.__dict__["in"].at[ds((1 - place.s) * 3 * rows + p * rows, rows)],
            q.x.at[pl.ds(p * rows, rows)],
            q.sems.at[0, 0, p],
            q.sems.at[1, 0, p],
            1 - place.s,
            place.me,
        )


def axis_send(p, base, q, g, src, place):
    size = SUM_ROWS[g] // 4
    axis = ORDERS[p][0]
    for d in (2, 1, 3):
        c = (place.coords[axis] + d) % 4
        remote(
            src.at[ds(base + c * size, size)],
            q.r0.at[p, d - 1],
            q.sems.at[0, 1, p],
            q.sems.at[1, 1, p],
            place.s,
            place.along(axis, d),
        )


def plane_send(p, q, g, place):
    size = SUM_ROWS[g] // 64
    second, third = ORDERS[p][1:]
    for d, e in PLANE:
        block = 4 * ((place.coords[second] + d) % 4) + (place.coords[third] + e) % 4
        remote(
            q.s0.at[p, ds(block * size, size)],
            q.r1.at[p, 4 * d + e - 1],
            q.sems.at[0, 2, p],
            q.sems.at[1, 2, p],
            place.s,
            place.along(second, d) + place.along(third, e) - place.me,
        )


def exchange_done(g, r, place):
    q, rows = sum_refs(g, r), SUM_ROWS[g]
    src = q.__dict__["in"]
    for p in range(3):
        base = place.s * 3 * rows + p * rows
        wait_all(q.x.at[pl.ds(p * rows, rows)], q.sems.at[1, 0, p])

        @pl.loop(0, rows // 512)
        def _(k):
            at = ds(base + k * 512, 512)
            other = q.x[ds(p * rows + k * 512, 512), :]
            src[at, :] = (src[at, :].astype(F32) + other.astype(F32)).astype(BF)

        axis_send(p, base, q, g, src, place)


def axis_done(g, r, place):
    q, rows = sum_refs(g, r), SUM_ROWS[g]
    size = rows // 4
    for p in range(3):
        wait_all(q.r0.at[p], q.sems.at[1, 1, p])
        at = place.s * 3 * rows + p * rows + place.coords[ORDERS[p][0]] * size
        total = q.__dict__["in"][ds(at, size), :].astype(F32)
        for d in range(3):
            total = total + q.r0[p, d].astype(F32)
        q.s0[p] = total.astype(BF)
        plane_send(p, q, g, place)


def plane_done(g, r, place):
    q, rows = sum_refs(g, r), SUM_ROWS[g]
    size = rows // 64
    for p in range(3):
        wait_all(q.r1.at[p], q.sems.at[1, 2, p])
        second, third = [place.coords[axis] for axis in ORDERS[p][1:]]
        total = q.s0[p, ds((4 * second + third) * size, size), :].astype(F32)
        for d in range(15):
            total = total + q.r1[p, d].astype(F32)
        block = q.t.at[place.s, p, ds(offsets(p, rows, place)[1], size)]
        block[...] = total.astype(BF)
        for d, e in PLANE:
            to = place.along(ORDERS[p][1], d) + place.along(ORDERS[p][2], e) - place.me
            remote(block, block, q.sems.at[0, 3, p], q.sems.at[1, 3, p], place.s, to)


def cross_send(p, start, size, q, place):
    block = q.t.at[place.s, p, ds(start, size)]
    remote(block, block, q.sems.at[0, 4, p], q.sems.at[1, 4, p], 1 - place.s, place.me)


def plane_back(g, r, place):
    q, rows = sum_refs(g, r), SUM_ROWS[g]
    for p in range(3):
        wait_all(q.t.at[0, p, pl.ds(0, 15 * rows // 64)], q.sems.at[1, 3, p])
        at, axis = offsets(p, rows, place)[0], ORDERS[p][0]
        block = q.t.at[place.s, p, ds(at, rows // 4)]
        for d in (2, 1, 3):
            send_sem, recv_sem = q.sems.at[0, 4 + d, p], q.sems.at[1, 4 + d, p]
            remote(block, block, send_sem, recv_sem, place.s, place.along(axis, d))
        cross_send(p, at, rows // 4, q, place)


def gather_last(g, r, place):
    q, rows = sum_refs(g, r), SUM_ROWS[g]
    size = rows // 4
    for d in (1, 3, 2):
        for p in range(3):
            wait_all(q.t.at[0, p, pl.ds(0, size)], q.sems.at[1, 4 + d, p])
            c = (place.coords[ORDERS[p][0]] - d + 4) % 4
            cross_send(p, c * size, size, q, place)


def half_out(half, sem, g, r):
    q = sum_refs(g, r)
    return pltpu.make_async_copy(q.t.at[half], (r.sums0, r.sums1)[g].at[half], r.vsems.at[2, sem])


def sum_out(g, r, place):
    q = sum_refs(g, r)
    for p in range(3):
        wait_all(q.t.at[0, p], q.sems.at[1, 4, p])
    half_out(1 - place.s, g, g, r).start()
    half_out(place.s, 2 + g, g, r).start()


def sum_drain(g, r, place):
    q, rows = sum_refs(g, r), SUM_ROWS[g]
    for p in range(3):
        wait_all(q.x.at[pl.ds(0, rows)], q.sems.at[0, 0, p])
        wait_all(q.r0.at[p], q.sems.at[0, 1, p])
        for k in (2, 3):
            wait_all(q.r1.at[p], q.sems.at[0, k, p])
        for d in range(1, 4):
            wait_all(q.t.at[0, p, pl.ds(0, rows // 4)], q.sems.at[0, 4 + d, p])
        wait_all(q.t.at[0, p], q.sems.at[0, 4, p])
    half_out(1 - place.s, g, g, r).wait()
    half_out(place.s, 2 + g, g, r).wait()


def vec_exchange(r, place):
    remote(r.vec_own, r.vec_x, r.vsems.at[0, 0], r.vsems.at[1, 0], 1 - place.s, place.me)


def vec_send(axis, r, place):
    c = place.coords[axis]
    for d in (1, 2, 3):
        remote(
            r.vec_in.at[axis, c],
            r.vec_in.at[axis, c],
            r.vsems.at[0, 1 + axis],
            r.vsems.at[1, 1 + axis],
            place.s,
            place.along(axis, d),
        )


def vec_step(axis, r, place):
    if axis == 0:
        wait_all(r.vec_x, r.vsems.at[1, 0])
        total = r.vec_own[...] + r.vec_x[...]
    else:
        wait_all(r.vec_in.at[axis - 1, pl.ds(0, 3)], r.vsems.at[1, axis])
        total = (r.vec_in[axis - 1, 0] + r.vec_in[axis - 1, 1]) + (
            r.vec_in[axis - 1, 2] + r.vec_in[axis - 1, 3]
        )
    if axis < 3:
        r.vec_in[axis, place.coords[axis]] = total
        vec_send(axis, r, place)
    else:
        r.vec[...] = total


def vec_drain(r):
    wait_all(r.vec_x, r.vsems.at[0, 0])
    for axis in range(3):
        wait_all(r.vec_in.at[axis, pl.ds(0, 3)], r.vsems.at[0, 1 + axis])


def step_exchange(g, r, place):
    exchange_start(g, r, place)
    if g == 0:
        vec_exchange(r, place)


def step_scatter(g, r, place):
    exchange_done(g, r, place)
    if g == 0:
        vec_step(0, r, place)


def step_axis(g, r, place):
    axis_done(g, r, place)
    if g == 0:
        vec_step(1, r, place)


def step_plane(g, r, place):
    plane_done(g, r, place)
    if g == 0:
        vec_step(2, r, place)


def step_back(g, r, place):
    plane_back(g, r, place)
    if g == 0:
        vec_step(3, r, place)


SUM_STEPS = (
    step_exchange,
    step_scatter,
    step_axis,
    step_plane,
    step_back,
    gather_last,
    sum_out,
)
SUM_DURING_BACK = ((7, 2),)
SUM_AFTER_BACK = (3,)
SUM_TAIL = ((1, 1), (0, 4), (1, 2), (1, 3), (0, 5), (1, 4), (0, 6), (1, 5), (1, 6))


WEIGHTS = ["w_query", "w_key", "w_value", "w_out", "w_up", "w_down"]
INPUTS = ["inputs", "groups_hbm", "cotangent"] + [name + "_hbm" for name in WEIGHTS]
INPUTS += [name + "_hbm" for name in ("gain_one", "shift_one", "gain_two", "shift_two")]
OUTPUTS = {
    "output": ((1, ROWS, D), BF),
    "input_grad": ((1, ROWS, D), BF),
    "sums0": ((2, 3, 3072, 128), BF),
    "sums1": ((2, 3, 1024, 128), BF),
    "vec_hbm": ((8, D), F32),
}
SCRATCH = {
    "w_query": ((D, D), BF),
    "w_key": ((D, D), BF),
    "w_value": ((D, D), BF),
    "w_out": ((D, D), BF),
    "w_up": ((D, FF), BF),
    "w_down": ((FF, D), BF),
    "cot": ((ROWS, D), BF),
    "groups": ((2, ROWS), jnp.int32),
    "gain_one": ((1, D), F32),
    "shift_one": ((1, D), F32),
    "gain_two": ((1, D), F32),
    "shift_two": ((1, D), F32),
    "last_grad": ((ROWS, D), BF),
    "vec": ((8, D), F32),
    "hid": ((3, ROWS, D), BF),
    "q_out": ((2, 8, 64, 128), BF),
    "q_in": ((2, 16, 64, 128), BF),
    "o_out": ((2, 16, 80, 128), BF),
    "o_in": ((2, 16, 80, 128), BF),
    "do_out": ((2, 8, 80, 128), BF),
    "do_in": ((2, 16, 80, 128), BF),
    "dq_out": ((2, 16, 64, 128), BF),
    "dq_in": ((2, 16, 64, 128), BF),
    "dkv_acc": ((512, 128), F32),
    "dqt": ((8, 64, 256), F32),
    "lq": ((2, 2048, 128), BF),
    "qz": ((2048, 128), BF),
    "ld": ((2048, 128), BF),
    "neg_log": ((16, 8, 128), F32),
    "neg_delta": ((16, 8, 128), F32),
    "f_acc": ((4, 512, 128), F32),
    "f_top": ((4, 512, 128), F32),
    "att": ((2, ROWS, D), F32),
    "log_total": ((2, 8, 128), F32),
    "grp_q": ((16, 8, 128), jnp.int32),
    "kv_out": ((2, 8, ROWS, 128), BF),
    "kv_in": ((2, 32, ROWS, 128), BF),
    "grp_out": ((1, 8, 128), jnp.int32),
    "grp_in": ((32, 8, 128), jnp.int32),
    "ka": ((2, 4096, 128), BF),
    "va": ((2, 4096, 128), BF),
    "kat": ((64, 4096), BF),
    "att_low": ((2, ROWS, D), BF),
    "n_one": ((2, ROWS, D), F32),
    "f_one": ((2, ROWS, 128), F32),
    "first_low": ((2, ROWS, D), BF),
    "pre": ((2, ROWS, FF), F32),
    "act": ((2, ROWS, FF), BF),
    "n_two": ((2, ROWS, D), F32),
    "f_two": ((2, ROWS, 128), F32),
    "work": ((ROWS, D), F32),
    "dy": ((ROWS, D), F32),
    "down_low": ((2, ROWS, D), BF),
    "up_low": ((2, ROWS, FF), BF),
    "out_low": ((2, ROWS, D), BF),
    "dkv_out": ((32, ROWS, 128), BF),
    "dkv_in": ((2, 32, ROWS, 128), BF),
    "dq": ((2, ROWS, D), BF),
    "dk": ((2, ROWS, D), BF),
    "dv": ((2, ROWS, D), BF),
    "vec_own": ((8, D), F32),
    "vec_x": ((8, D), F32),
    "vec_in": ((3, 4, 8, D), F32),
}
for g, rows in enumerate(SUM_ROWS):
    SCRATCH |= {
        f"sum_in{g}": ((6 * rows, 128), BF),
        f"sum_x{g}": ((3 * rows, 128), BF),
        f"sum_r0{g}": ((3, 3, rows // 4, 128), BF),
        f"sum_r1{g}": ((3, 15, rows // 64, 128), BF),
        f"sum_s0{g}": ((3, rows // 4, 128), BF),
        f"sum_t{g}": ((2, 3, rows, 128), BF),
    }
SEMS = {"sems": (12, 2), "gsems": (4,), "load_sems": (13,), "out_sems": (3,), "kv_sems": (2, 4), "plane_sems": (2, 8), "sum_sems0": (2, 8, 3), "sum_sems1": (2, 8, 3), "vsems": (3, 4)}


def kernel(*refs):
    names = INPUTS + list(OUTPUTS) + list(SCRATCH) + list(SEMS)
    r = SimpleNamespace(**dict(zip(names, refs)))
    place = Place()
    for name in LOADED[:5]:
        load(name, r, place).start()
    greet(place)
    for name in LOADED[5:]:
        load(name, r, place).start()
    r.vec_own[...] = jnp.zeros_like(r.vec_own)

    @pl.loop(0, 2)
    def _(v):
        @pl.when(v == 0)
        def _():
            for name in LOADED[:5]:
                load(name, r, place).wait()

        project_queries(v, r)
        project_keys_values(v, r)

        @pl.when(v == 0)
        def _():
            all_here()
            send_groups(r, place)

        send_queries(v, r, place)
        send_keys_values(v, r, place)
        pass_on(v, r, place)

        @pl.when(v == 0)
        def _():
            wait_all(r.grp_in, r.gsems.at[1])
            wait_all(r.grp_q, r.gsems.at[3])
            make_aug(r)

        wait_all(r.q_in.at[v], r.sems.at[3, v])
        make_queries(v, r)
        attention(v, r, place)

        @pl.when(v == 0)
        def _():
            for name in LOADED[5:12]:
                load(name, r, place).wait()

        wait_all(r.o_in.at[v], r.sems.at[5, v])
        after_attention(v, r)

    finals = [
        pltpu.make_async_copy(r.hid.at[2], r.output.at[0], r.out_sems.at[0]),
        pltpu.make_async_copy(r.last_grad, r.input_grad.at[0], r.out_sems.at[1]),
        pltpu.make_async_copy(r.vec, r.vec_hbm, r.out_sems.at[2]),
    ]
    finals[0].start()
    load("cot", r, place).wait()
    r.dy[...] = r.cot[...].astype(F32)

    @pl.loop(0, 2)
    def _(step):
        v = 1 - step
        before_attention_back(v, r)
        send_do(v, r, place)

        @pl.when(v == 0)
        def _():
            weight_grads_early(r)
            SUM_STEPS[0](0, r, place)

        prepare_back(v, r)
        wait_all(r.do_in.at[v], r.sems.at[7, v])

        @pl.when(v == 0)
        def _():
            SUM_STEPS[1](0, r, place)

        attention_back(v, r, place)

        @pl.when(v == 0)
        def _():
            for step in SUM_AFTER_BACK:
                SUM_STEPS[step](0, r, place)

        wait_all(r.dq_in.at[v], r.sems.at[9, v])
        wait_all(r.dkv_in.at[v], r.sems.at[11, v])
        take_gradients(v, r)

        @pl.when(v == 1)
        def _():
            r.dy[...] = input_gradient(v, r).astype(F32)

    weight_grads_late(r)
    SUM_STEPS[0](1, r, place)
    r.last_grad[...] = input_gradient(0, r)
    finals[1].start()
    for g, step in SUM_TAIL:
        SUM_STEPS[step](g, r, place)

    finals[2].start()
    for copy in finals:
        copy.wait()
    vec_drain(r)
    for g in range(2):
        sum_drain(g, r, place)
    wait_sent(r.grp_in, r.gsems.at[0], place.self_kv, 32)
    wait_sent(r.grp_q, r.gsems.at[2], place.self_q, 16)

    @pl.loop(0, 2)
    def _(v):
        wait_sent(r.kv_in.at[v], r.sems.at[0, v], place.self_kv, 8)
        wait_all(r.kv_in.at[v, pl.ds(0, 24)], r.sems.at[1, v])
        wait_sent(r.q_in.at[v], r.sems.at[2, v], place.self_q, 16)
        wait_sent(r.o_in.at[v], r.sems.at[4, v], place.self_q, 16)
        wait_sent(r.do_in.at[v], r.sems.at[6, v], place.self_q, 16)
        wait_sent(r.dq_in.at[v], r.sems.at[8, v], place.self_q, 16)

    wait_sent(r.dkv_in.at[0], r.sems.at[10, 0], place.self_kv, 32)


def unpack(output, input_grad, early, late, vec):
    def body(*refs):
        output, input_grad, early, late, vec, output_to, input_grad_to = refs[:7]
        query, key, value, out, up, down = refs[7:13]
        got, small, up_f, down_f, vec_in, vec_out, sin, sout = refs[17:]
        loads = []
        for j in range(12):
            src = late.at[pl.ds(4 * j, 4)] if j < 3 else early.at[pl.ds(4 * (j - 3), 4)]
            loads.append(pltpu.make_async_copy(src, got.at[pl.ds(4 * j, 4)], sin.at[j]))
        order = [7, 8, 9, 10, 3, 4, 5, 6, 0, 1, 2, 11]
        for j in order:
            loads[j].start()
        get_vec = pltpu.make_async_copy(vec, vec_in, sin.at[12])
        get_vec.start()
        stores = [
            pltpu.make_async_copy(output, output_to, sout.at[12]),
            pltpu.make_async_copy(input_grad, input_grad_to, sout.at[13]),
        ]
        for copy in stores:
            copy.start()

        def store(j, src, dst):
            stores.append(pltpu.make_async_copy(src, dst, sout.at[j]))
            stores[-1].start()

        for j in order:
            loads[j].wait()
            tiles = [got[4 * j + k].astype(F32) for k in range(4)]
            cols = [slice(128 * k, 128 * k + 128) for k in range(4)]
            if j < 3 or j == 11:
                i = min(j, 3)
                for k in range(4):
                    small[i, :, cols[k]] = tiles[k]
                store(j, small.at[i], (query, key, value, out)[i])
            elif j < 7:
                at = 512 * (j - 3)
                for k in range(4):
                    up_f[:, at + 128 * k : at + 128 * k + 128] = tiles[k]
                store(j, up_f.at[:, pl.ds(at, 512)], up.at[:, pl.ds(at, 512)])
            else:
                for k in range(4):
                    down_f[512 * k : 512 * k + 512, cols[j - 7]] = tiles[k]
                if j == 10:
                    for k in range(4):
                        rows = pl.ds(512 * k, 512)
                        store(7 + k, down_f.at[rows], down.at[rows])
        get_vec.wait()
        for i in range(4):
            vec_out[i, 0] = vec_in[i]
            copy = pltpu.make_async_copy(vec_out.at[i, 0], refs[13 + i], sout.at[14 + i])
            copy.start()
            stores.append(copy)
        for copy in stores:
            copy.wait()

    square, hbm = jax.ShapeDtypeStruct((D, D), F32), pl.BlockSpec(memory_space=pl.ANY)
    rows = jax.ShapeDtypeStruct((1, ROWS, D), BF)
    shapes = [rows] * 2 + [square] * 4
    shapes += [jax.ShapeDtypeStruct((D, FF), F32), jax.ShapeDtypeStruct((FF, D), F32)]
    return pl.pallas_call(
        body,
        out_shape=shapes + [jax.ShapeDtypeStruct((D,), F32)] * 4,
        in_specs=[hbm] * 5,
        out_specs=[hbm] * 12,
        scratch_shapes=[
            pltpu.VMEM((48, 512, 128), BF),
            pltpu.VMEM((4, D, D), F32),
            pltpu.VMEM((D, FF), F32),
            pltpu.VMEM((FF, D), F32),
            pltpu.VMEM((8, D), F32),
            pltpu.VMEM((4, 1, D), F32),
            pltpu.SemaphoreType.DMA((13,)),
            pltpu.SemaphoreType.DMA((18,)),
        ],
        compiler_params=pltpu.CompilerParams(vmem_limit_bytes=60 * 2**20),
        name="unpack",
    )(output, input_grad, early, late, vec)


def on_device(inputs, groups, cotangent, *params):
    vectors = [x.reshape(1, D) for x in params[6:]]
    hbm = pl.BlockSpec(memory_space=pl.ANY)
    out = pl.pallas_call(
        kernel,
        out_shape=[jax.ShapeDtypeStruct(shape, kind) for shape, kind in OUTPUTS.values()],
        in_specs=[hbm] * len(INPUTS),
        out_specs=[hbm] * len(OUTPUTS),
        scratch_shapes=[pltpu.VMEM(shape, kind) for shape, kind in SCRATCH.values()]
        + [pltpu.SemaphoreType.DMA(shape) for shape in SEMS.values()],
        compiler_params=pltpu.CompilerParams(
            collective_id=0, has_side_effects=True, vmem_limit_bytes=62 * 2**20
        ),
        name="visits",
    )(inputs, groups, cotangent, *params[:6], *vectors)
    return unpack(*out[:2], out[2].reshape(36, 512, 128), out[3].reshape(12, 512, 128), out[4])


def solution(mesh):
    rows = P(None, "dp", None)
    return jax.shard_map(
        on_device,
        mesh=mesh,
        in_specs=(rows, P(None, "dp"), rows) + (P(),) * 10,
        out_specs=(P("section", "dp", None),) * 2 + (P(),) * 10,
        check_vma=False,
    )
```

```python
from types import SimpleNamespace

import jax
import jax.numpy as jnp
from jax import lax
from jax.experimental import pallas as pl
from jax.experimental.pallas import tpu as pltpu
from jax.sharding import PartitionSpec as P

F32, BF = jnp.float32, jnp.bfloat16
BIG = 1e30
ROWS, D, FF, HEADS = 128, 512, 2048, 8
MESH = pl.DeviceIdType.MESH


def nt(a, b):
    return lax.dot_general(a, b, (((1,), (1,)), ((), ())), preferred_element_type=F32)


def nn(a, b):
    return lax.dot_general(a, b, (((1,), (0,)), ((), ())), preferred_element_type=F32)


def tn(a, b):
    return lax.dot_general(a, b, (((0,), (0,)), ((), ())), preferred_element_type=F32)


def lanes(shape):
    return lax.broadcasted_iota(jnp.int32, shape, len(shape) - 1)


def subs(shape):
    return lax.broadcasted_iota(jnp.int32, shape, len(shape) - 2)


def ds(start, size):
    if isinstance(start, int):
        return pl.ds(start, size)
    return pl.ds(pl.multiple_of(start, size), size)


def split3(x):
    a = x.astype(BF).astype(F32)
    b = (x - a).astype(BF).astype(F32)
    return a, b, (x - a - b).astype(BF).astype(F32)


def tile_of(r, t):
    return 4 * r + (r + t) % 4


def mean(x):
    return jnp.mean(x, axis=-1, keepdims=True)


def norm(x):
    centred = x - mean(x)
    factor = lax.rsqrt(mean(centred * centred) + 1e-05)
    return centred * factor, factor


def norm_back(dy, n, factor, gain):
    u = dy * gain
    return factor * (u - mean(u) - n * mean(u * n))


GELU_C = 0.7978845608028654


def gelu(x):
    return 0.5 * x * (1.0 + jnp.tanh(GELU_C * (x + 0.044715 * x * x * x)))


def gelu_slope(x):
    sq = x * x
    th = jnp.tanh(GELU_C * x * (1.0 + 0.044715 * sq))
    return 0.5 * (1.0 + th) + 0.5 * x * (1.0 - th * th) * (GELU_C * (1.0 + 3 * 0.044715 * sq))


class Place:
    def __init__(self):
        self.me = lax.axis_index("dp")
        self.s = lax.axis_index("section")
        me = self.me
        self.coords = (me % 4, me // 16, (me // 4) % 4)
        x, y, z = self.coords
        self.t = (x + y + z) % 4
        self.head = 4 * (y % 2) + x
        self.micro = y // 2
        self.own_t = ((me // 2) % 4 - me // 8 + 32) % 4
        self.own_slot = 2 * (me // 8) + me % 2
        mine = self.micro == self.s
        self.self_kv = mine & (me % 2 == self.s)
        self.self_q = mine & (self.own_t == self.t)

    def along(self, axis, d):
        c = self.coords[axis]
        return self.me + ((c + d) % 4 - c) * (1, 16, 4)[axis]

    def chip_in_plane(self, h):
        return 16 * (2 * self.s + h // 4) + 4 * self.coords[2] + h % 4

    def chip(self, h, t):
        x, y = h % 4, 2 * self.s + h // 4
        return 16 * y + 4 * ((t - x - y + 8) % 4) + x

    def send(self, src, dst, send_sem, recv_sem, section, dp):
        to_self = (section == self.s) & (dp == self.me)

        @pl.when(jnp.logical_not(to_self))
        def _():
            pltpu.make_async_remote_copy(
                src_ref=src,
                dst_ref=dst,
                send_sem=send_sem,
                recv_sem=recv_sem,
                device_id=(section, dp),
                device_id_type=MESH,
            ).start()

        @pl.when(to_self)
        def _():
            pltpu.make_async_copy(src, dst, recv_sem).start()


def remote(src, dst, send_sem, recv_sem, section, dp):
    pltpu.make_async_remote_copy(
        src_ref=src,
        dst_ref=dst,
        send_sem=send_sem,
        recv_sem=recv_sem,
        device_id=(section, dp),
        device_id_type=MESH,
    ).start()


def wait_all(ref, sem):
    pltpu.make_async_copy(ref, ref, sem).wait()


def wait_sent(ref, sem, to_self, count):
    @pl.when(to_self)
    def _():
        wait_all(ref.at[pl.ds(0, count - 1)], sem)

    @pl.when(jnp.logical_not(to_self))
    def _():
        wait_all(ref.at[pl.ds(0, count)], sem)


def greet(place):
    sem = pltpu.get_barrier_semaphore()

    @pl.loop(1, 128)
    def _(k):
        other = (place.s * 64 + place.me + k) % 128
        pl.semaphore_signal(sem, inc=1, device_id=(other // 64, other % 64), device_id_type=MESH)


def all_here():
    pl.semaphore_wait(pltpu.get_barrier_semaphore(), 127)


LOADED = ["hid", "w_query", "w_key", "w_value", "groups", "w_out", "w_up", "w_down", "gain_one"]
LOADED += ["shift_one", "gain_two", "shift_two", "cot"]


def load(name, r, place):
    sem = r.load_sems.at[LOADED.index(name)]
    if name == "hid":
        return pltpu.make_async_copy(r.inputs.at[place.s], r.hid.at[0], sem)
    if name == "cot":
        return pltpu.make_async_copy(r.cotangent.at[place.s], r.cot, sem)
    return pltpu.make_async_copy(getattr(r, name + "_hbm"), getattr(r, name), sem)


def pack(tile, odd):
    low = lanes((64, 128)) < 64
    if odd:
        return jnp.where(low, pltpu.roll(tile[:64], 64, 1), tile[64:])
    return jnp.where(low, tile[:64], pltpu.roll(tile[64:], 64, 1))


def spread(packed, odd):
    turned = pltpu.roll(packed, 64, 1)
    return jnp.concatenate([turned, packed] if odd else [packed, turned], axis=0)


def parts_in_rows(rows):
    at = subs((16, 128))
    out = jnp.zeros((16, 128), F32)
    for i, part in enumerate(rows):
        out = jnp.where(at == i, part, out)
    return out.astype(BF)


def project_queries(v, r):
    q = nn(r.hid[v], r.w_query[...]).astype(BF).astype(F32) * 0.125
    for h in range(HEADS):
        tile = q[:, 128 * (h // 2) : 128 * (h // 2) + 128]
        r.q_out[v, h] = pack(tile, h % 2 == 1).astype(BF)


def project_keys_values(v, r):
    hid = r.hid[v]
    k = nn(hid, r.w_key[...]).astype(BF).astype(F32)
    w = nn(hid, r.w_value[...]).astype(BF).astype(F32)
    low = lanes((ROWS, 128)) < 64
    for h in range(HEADS):
        cols = slice(128 * (h // 2), 128 * (h // 2) + 128)
        kt, vt = k[:, cols], w[:, cols]
        if h % 2 == 0:
            vt = pltpu.roll(vt, 64, 1)
        else:
            kt = pltpu.roll(kt, 64, 1)
        r.kv_out[v, h] = jnp.where(low, kt, vt).astype(BF)


def to_queries(src, dst, send_sem, recv_sem, place):
    @pl.loop(0, HEADS)
    def _(a):
        h = (place.me // 4 + a) % 8
        for b in range(2):
            core, chip = (place.me + b) % 2, place.chip(h, place.own_t)
            place.send(src(h), dst.at[place.own_slot], send_sem, recv_sem, core, chip)


def to_keys(src, dst, send_sem, recv_sem, place):
    n = place.me // 2

    @pl.loop(0, HEADS)
    def _(a):
        h = 2 * ((n // 8 + a // 2) % 4) + (n // 4 + a) % 2
        for b in range(4):
            chip = place.chip(h, (n + b) % 4)
            place.send(src(h), dst.at[n], send_sem, recv_sem, place.me % 2, chip)


def send_queries(v, r, place):
    to_queries(
        lambda h: r.q_out.at[v, h], r.q_in.at[v], r.sems.at[2, v], r.sems.at[3, v], place
    )


def send_keys_values(v, r, place):
    x, y, _ = place.coords
    n = place.me // 2

    @pl.loop(0, HEADS)
    def _(a):
        h = 2 * ((n // 8 + a // 2) % 4) + (n // 4 + a) % 2
        place.send(
            r.kv_out.at[v, h],
            r.kv_in.at[v, n],
            r.sems.at[0, v],
            r.plane_sems.at[v, 2 * y + x // 2],
            x % 2,
            place.chip_in_plane(h),
        )


def pass_on(v, r, place):
    z = place.coords[2]

    @pl.loop(0, 4)
    def _(y):
        for b in range(2):
            block = r.kv_in.at[v, 8 * y + 2 * z + b]
            wait_all(block, r.plane_sems.at[v, 2 * y + b])
            for d in (2, 1, 3):
                to = place.along(2, d)
                remote(block, block, r.sems.at[1, v], r.kv_sems.at[v, y], place.s, to)


def send_groups(r, place):
    r.grp_out[0] = jnp.broadcast_to(r.groups[pl.ds(place.s, 1), :], (8, 128))
    to_queries(lambda h: r.grp_out.at[0], r.grp_q, r.gsems.at[2], r.gsems.at[3], place)
    to_keys(lambda h: r.grp_out.at[0], r.grp_in, r.gsems.at[0], r.gsems.at[1], place)


def column_of(row):
    return jnp.transpose(jnp.broadcast_to(row.astype(F32), (128, 128)))


def make_aug(r):
    ln = lanes((ROWS, 128))
    inside = (ln >= 64) & (ln < 68)

    @pl.loop(0, 32)
    def _(n):
        g = column_of(r.grp_in[n][0:1, :]).astype(jnp.int32)
        aug = jnp.where(inside & (ln - 64 != g), -BIG, 0.0).astype(BF)
        for v in range(2):
            r.ka[v, ds(n * 128, 128), :] = aug

    @pl.loop(0, 16)
    def _(n):
        g = column_of(r.grp_q[n][0:1, :]).astype(jnp.int32)
        aug = jnp.where(ln - 64 == g, 1.0, 0.0).astype(BF)
        for v in range(2):
            r.lq[v, ds(n * 128, 128), :] = aug


def make_queries(v, r):
    low = lanes((ROWS, 128)) < 64

    @pl.loop(0, 16)
    def _(n):
        rows = ds(n * 128, 128)
        q = spread(r.q_in[v, n].astype(F32), False)
        r.lq[v, rows, :] = jnp.where(low, q, r.lq[v, rows, :].astype(F32)).astype(BF)


def make_kv(v, c, r):
    ln = lanes((ROWS, 128))
    low = ln < 64
    ones = jnp.where(ln < 1, 1.0, 0.0)

    @pl.loop(0, 8)
    def _(k):
        n = 8 * c + k
        rows = ds(n * 128, 128)
        kv = r.kv_in[v, n].astype(F32)
        r.ka[v, rows, :] = jnp.where(low, kv, r.ka[v, rows, :].astype(F32)).astype(BF)
        r.va[v, rows, :] = jnp.where(low, ones, kv).astype(BF)


def fwd_body(v, c, j, masked, r, place):
    width = 1024
    rows = ds(c * width, width)
    sc = nt(r.lq[v, ds(512 * j, 512), :], r.ka[v, rows, :])
    if masked:
        col, row = lanes((512, width)), subs((512, width))
        tiles = [tile_of(2 * j + k, place.t) for k in range(2)]
        at = 256 * (col // 128) + col % 128 + (2048 * c + 128 * place.s)
        limit = row % 256 + 256 * jnp.where(row < 256, tiles[0], tiles[1])
        sc = jnp.where(at <= limit, sc, -BIG)
    top = r.f_top[j][:, 0:1]
    new = jnp.maximum(top, jnp.max(sc, axis=1, keepdims=True))
    p = jnp.exp(sc - new).astype(BF)
    r.f_acc[j] = r.f_acc[j] * jnp.exp(top - new) + nn(p, r.va[v, rows, :])
    r.f_top[j] = jnp.broadcast_to(new, (512, 128))


def fwd_finish(v, j, r, place):
    acc = r.f_acc[j]
    total = acc[:, 0:1]
    out = acc / total
    logs = jnp.broadcast_to(r.f_top[j][:, 0:1] + jnp.log(total), (512, 128))
    for k in range(4):
        rows = slice(128 * k, 128 * k + 128)
        r.o_out[v, 4 * j + k, 0:64] = pack(out[rows], True).astype(BF)
        row = jnp.transpose(logs[rows])[0:1]
        r.o_out[v, 4 * j + k, 64:80] = parts_in_rows(split3(row))
    for k in range(2):
        for turn in range(2):
            half = (turn + place.s) % 2
            place.send(
                r.o_out.at[v, 4 * j + 2 * k + half],
                r.o_in.at[v, 2 * place.head + place.s],
                r.sems.at[4, v],
                r.sems.at[5, v],
                place.micro,
                2 * tile_of(2 * j + k, place.t) + half,
            )


def attention(v, r, place):
    r.f_acc[...] = jnp.zeros_like(r.f_acc)
    r.f_top[...] = jnp.full_like(r.f_top, -2 * BIG)

    @pl.loop(0, 4)
    def _(c):
        wait_all(r.kv_in.at[v, pl.ds(0, 6)], r.kv_sems.at[v, c])
        make_kv(v, c, r)
        fwd_body(v, c, c, True, r, place)
        fwd_finish(v, c, r, place)

        @pl.loop(c + 1, 4)
        def _(j):
            fwd_body(v, c, j, False, r, place)


def after_attention(v, r):
    low = lanes((ROWS, 128)) < 64
    weights = [[], []]
    for h in range(HEADS):
        logs = []
        for core in range(2):
            x = r.o_in[v, 2 * h + core, 64:80].astype(F32)
            logs.append(x[0:1] + x[1:2] + x[2:3])
        top = jnp.maximum(logs[0], logs[1])
        w = [jnp.exp(x - top) for x in logs]
        total = w[0] + w[1]
        r.log_total[v, h : h + 1] = top + jnp.log(total)
        for core in range(2):
            weights[core].append(w[core] / total)
    cols = jnp.transpose(jnp.concatenate(weights[0] + weights[1] + [jnp.zeros((112, 128), F32)], axis=0))
    for i in range(HEADS // 2):
        whole = []
        for h in (2 * i, 2 * i + 1):
            got = [spread(r.o_in[v, 2 * h + k, 0:64].astype(F32), h % 2 == 1) for k in range(2)]
            whole.append(got[0] * cols[:, h : h + 1] + got[1] * cols[:, 8 + h : 9 + h])
        pair = jnp.where(low, whole[0], whole[1])
        r.att[v, :, 128 * i : 128 * i + 128] = pair
        r.att_low[v, :, 128 * i : 128 * i + 128] = pair.astype(BF)
    mixed = r.hid[v].astype(F32) + nn(r.att_low[v], r.w_out[...])
    n_one, f_one = norm(mixed)
    first = n_one * r.gain_one[...] + r.shift_one[...]
    first_low = first.astype(BF)
    r.n_one[v] = n_one
    r.f_one[v] = jnp.broadcast_to(f_one, (ROWS, 128))
    r.first_low[v] = first_low
    r.work[...] = first

    @pl.loop(0, 4)
    def _(j):
        cols = ds(j * 512, 512)
        pre = nn(r.first_low[v], r.w_up[:, cols])
        r.pre[v, :, cols] = pre
        act = gelu(pre).astype(BF)
        r.act[v, :, cols] = act
        r.work[...] += nn(act, r.w_down[cols, :])

    n_two, f_two = norm(r.work[...])
    r.n_two[v] = n_two
    r.f_two[v] = jnp.broadcast_to(f_two, (ROWS, 128))
    r.hid[v + 1] = (n_two * r.gain_two[...] + r.shift_two[...]).astype(BF)


def before_attention_back(v, r):
    dy = r.dy[...]
    n_two = r.n_two[v]
    r.vec_own[2:3, :] += jnp.sum(dy * n_two, axis=0, keepdims=True)
    r.vec_own[3:4, :] += jnp.sum(dy, axis=0, keepdims=True)
    grad_two = norm_back(dy, n_two, r.f_two[v][:, 0:1], r.gain_two[...])
    r.down_low[v] = grad_two.astype(BF)
    r.work[...] = grad_two

    @pl.loop(0, 4)
    def _(j):
        cols = ds(j * 512, 512)
        grad = nt(r.down_low[v], r.w_down[cols, :])
        up = (grad * gelu_slope(r.pre[v, :, cols])).astype(BF)
        r.up_low[v, :, cols] = up
        r.work[...] += nt(up, r.w_up[:, cols])

    dz = r.work[...]
    n_one = r.n_one[v]
    r.vec_own[0:1, :] += jnp.sum(dz * n_one, axis=0, keepdims=True)
    r.vec_own[1:2, :] += jnp.sum(dz, axis=0, keepdims=True)
    grad_one = norm_back(dz, n_one, r.f_one[v][:, 0:1], r.gain_one[...])
    out_low = grad_one.astype(BF)
    r.out_low[v] = out_low
    r.work[...] = grad_one
    grad_att = nt(out_low, r.w_out[...]).astype(BF).astype(F32)
    ln = lanes((ROWS, 128))
    low = ln < 64
    deltas = jnp.zeros((ROWS, 128), F32)
    for h in range(HEADS):
        cols = slice(128 * (h // 2), 128 * (h // 2) + 128)
        product = grad_att[:, cols] * r.att[v, :, cols]
        mine = jnp.where(low, product, 0.0) if h % 2 == 0 else jnp.where(low, 0.0, product)
        deltas = jnp.where(ln == h, jnp.sum(mine, axis=1, keepdims=True), deltas)
    deltas = jnp.transpose(deltas)
    for h in range(HEADS):
        tile = grad_att[:, 128 * (h // 2) : 128 * (h // 2) + 128]
        r.do_out[v, h, 0:64] = pack(tile, h % 2 == 1).astype(BF)
        rows = split3(-deltas[h : h + 1]) + split3(-r.log_total[v, h : h + 1])
        r.do_out[v, h, 64:80] = parts_in_rows(rows)


def send_do(v, r, place):
    to_queries(
        lambda h: r.do_out.at[v, h], r.do_in.at[v], r.sems.at[6, v], r.sems.at[7, v], place
    )


def prepare_back(v, r):
    low = lanes((ROWS, 128)) < 64

    @pl.loop(0, 16)
    def _(n):
        rows = ds(n * 128, 128)
        r.qz[rows, :] = jnp.where(low, r.lq[v, rows, :].astype(F32), 0.0).astype(BF)

    @pl.loop(0, 8)
    def _(i):
        rows = ds(i * 512, 512)
        r.kat[:, rows] = jnp.transpose(r.ka[v, rows, :].astype(F32))[:64].astype(BF)

    r.dqt[...] = jnp.zeros_like(r.dqt)


def take_do(v, r):
    low = lanes((ROWS, 128)) < 64

    @pl.loop(0, 16)
    def _(n):
        do = spread(r.do_in[v, n, 0:64].astype(F32), True)
        r.ld[ds(n * 128, 128), :] = jnp.where(low, 0.0, do).astype(BF)
        x = r.do_in[v, n, 64:80].astype(F32)
        r.neg_delta[n] = jnp.broadcast_to(x[0:1] + x[1:2] + x[2:3], (8, 128))
        r.neg_log[n] = jnp.broadcast_to(x[3:4] + x[4:5] + x[5:6], (8, 128))


def bwd_body(v, c, tiles, masked, r, place):
    rows = ds(c * 512, 512)
    probs, grads = [], []
    for i in tiles:
        mine = ds(i * 256, 256)
        x = nt(r.ka[v, rows, :], r.lq[v, mine, :])
        x = x + jnp.concatenate([r.neg_log[2 * i][0:1], r.neg_log[2 * i + 1][0:1]], axis=1)
        if masked:
            row, col = subs((512, 256)), lanes((512, 256))
            shift = 1024 * c + 128 * place.s - 256 * tile_of(i, place.t)
            x = jnp.where(256 * (row // 128) + row % 128 + shift <= col, x, -BIG)
        p = jnp.exp(x)
        dp = nt(r.va[v, rows, :], r.ld[mine, :])
        dp = dp + jnp.concatenate([r.neg_delta[2 * i][0:1], r.neg_delta[2 * i + 1][0:1]], axis=1)
        probs.append(p.astype(BF))
        grads.append((p * dp).astype(BF))
    size = 256 * len(tiles)
    queries = pl.ds(pl.multiple_of(tiles[0] * 256, 256), size)
    r.dkv_acc[...] += nn(jnp.concatenate(grads, axis=1), r.qz[queries, :]) + nn(
        jnp.concatenate(probs, axis=1), r.ld[queries, :]
    )
    for i, dsc in zip(tiles, grads):
        r.dqt[i] += nn(r.kat[:, rows], dsc)


def bwd_finish(v, i, r, place):
    dq = jnp.transpose(jnp.concatenate([r.dqt[i], jnp.zeros((64, 256), F32)], axis=0))
    for k in range(2):
        r.dq_out[v, 2 * i + k] = pack(dq[128 * k : 128 * k + 128], False).astype(BF)
    for turn in range(2):
        half = (turn + place.s) % 2
        place.send(
            r.dq_out.at[v, 2 * i + half],
            r.dq_in.at[v, 2 * place.head + place.s],
            r.sems.at[8, v],
            r.sems.at[9, v],
            place.micro,
            2 * tile_of(i, place.t) + half,
        )


def chunk_at(a, place):
    first = (a // 2 + place.head) % 4
    return jnp.where(a % 2 == 0, first, 7 - first)


def chunk_at(a, place):
    first = (a // 2 + place.coords[0] + place.t) % 4
    return jnp.where((a + place.coords[1]) % 2 == 0, first, 7 - first)


def attention_back(v, r, place):
    take_do(v, r)

    @pl.when(v == 0)
    def _():
        wait_sent(r.dkv_in.at[1], r.sems.at[10, 1], place.self_kv, 32)

    @pl.loop(0, 8)
    def _(a):
        c = chunk_at(a, place)

        @pl.loop(0, jnp.where(a == 7, c, 0))
        def _(i):
            bwd_finish(v, i, r, place)

        r.dkv_acc[...] = jnp.zeros_like(r.dkv_acc)

        @pl.when(c % 2 == 0)
        def _():
            bwd_body(v, c, [c, c + 1], True, r, place)

        @pl.when(c % 2 == 1)
        def _():
            bwd_body(v, c, [c], True, r, place)

        @pl.loop(c // 2 + 1, 4)
        def _(m):
            bwd_body(v, c, [2 * m, 2 * m + 1], False, r, place)

        for b in range(4):
            k = (b + place.t) % 4
            n = 4 * c + k
            r.dkv_out[n] = r.dkv_acc[ds(k * 128, 128), :].astype(BF)
            place.send(
                r.dkv_out.at[n],
                r.dkv_in.at[v, 4 * place.head + place.t],
                r.sems.at[10, v],
                r.sems.at[11, v],
                place.micro,
                2 * n + place.s,
            )
        for after, step in SUM_DURING_BACK:

            @pl.when((v == 0) & (a == after))
            def _():
                SUM_STEPS[step](0, r, place)

    @pl.loop(chunk_at(7, place), 8)
    def _(i):
        bwd_finish(v, i, r, place)


def take_gradients(v, r):
    low = lanes((ROWS, 128)) < 64
    for i in range(HEADS // 2):
        cols = slice(128 * i, 128 * i + 128)
        dq, dkv = [], []
        for h in (2 * i, 2 * i + 1):
            both = r.dq_in[v, 2 * h].astype(F32) + r.dq_in[v, 2 * h + 1].astype(F32)
            dq.append(spread(both * 0.125, h % 2 == 1))
            four = [r.dkv_in[v, 4 * h + t].astype(F32) for t in range(4)]
            dkv.append((four[0] + four[1]) + (four[2] + four[3]))
        r.dq[v, :, cols] = jnp.where(low, dq[0], dq[1]).astype(BF)
        r.dk[v, :, cols] = jnp.where(low, dkv[0], pltpu.roll(dkv[1], 64, 1)).astype(BF)
        r.dv[v, :, cols] = jnp.where(low, pltpu.roll(dkv[0], 64, 1), dkv[1]).astype(BF)


def input_gradient(v, r):
    return (
        r.work[...]
        + nt(r.dq[v], r.w_query[...])
        + nt(r.dk[v], r.w_key[...])
        + nt(r.dv[v], r.w_value[...])
    ).astype(BF)


def both(ref):
    return jnp.concatenate([ref[0], ref[1]], axis=0)


def put(ref, unit, tile):
    ref[ds(unit * 512, 512), :] = tile.astype(BF)


def weight_grads_early(r):
    @pl.loop(0, 4)
    def _(j):
        cols = ds(j * 512, 512)
        up = jnp.concatenate([r.up_low[0, :, cols], r.up_low[1, :, cols]], axis=0)
        grad = tn(both(r.first_low), up)
        for k in range(4):
            put(r.sum_in0, 4 * j + k, grad[:, 128 * k : 128 * k + 128])
        act = jnp.concatenate([r.act[0, :, cols], r.act[1, :, cols]], axis=0)
        grad = tn(act, both(r.down_low))
        for k in range(4):
            put(r.sum_in0, 16 + 4 * k + j, grad[:, 128 * k : 128 * k + 128])

    grad = tn(both(r.att_low), both(r.out_low))
    for k in range(4):
        put(r.sum_in0, 32 + k, grad[:, 128 * k : 128 * k + 128])


def weight_grads_late(r):
    hid = jnp.concatenate([r.hid[0], r.hid[1]], axis=0)
    for i, ref in enumerate((r.dq, r.dk, r.dv)):
        grad = tn(hid, both(ref))
        for k in range(4):
            put(r.sum_in1, 4 * i + k, grad[:, 128 * k : 128 * k + 128])


SUM_ROWS = (3072, 1024)
ORDERS = ((0, 1, 2), (1, 2, 0), (2, 0, 1))
PLANE = [(d, e) for d in range(4) for e in range(4) if (d, e) != (0, 0)]


def sum_refs(g, r):
    names = ("in", "x", "r0", "r1", "s0", "t", "sems")
    return SimpleNamespace(**{n: getattr(r, "sum_" + n + str(g)) for n in names})


def offsets(p, rows, place):
    first, second, third = [place.coords[axis] for axis in ORDERS[p]]
    at = first * (rows // 4)
    return at, at + (4 * second + third) * (rows // 64)


def exchange_start(g, r, place):
    q, rows = sum_refs(g, r), SUM_ROWS[g]
    for p in range(3):
        remote(
            q.__dict__["in"].at[ds((1 - place.s) * 3 * rows + p * rows, rows)],
            q.x.at[pl.ds(p * rows, rows)],
            q.sems.at[0, 0, p],
            q.sems.at[1, 0, p],
            1 - place.s,
            place.me,
        )


def axis_send(p, base, q, g, src, place):
    size = SUM_ROWS[g] // 4
    axis = ORDERS[p][0]
    for d in (2, 1, 3):
        c = (place.coords[axis] + d) % 4
        remote(
            src.at[ds(base + c * size, size)],
            q.r0.at[p, d - 1],
            q.sems.at[0, 1, p],
            q.sems.at[1, 1, p],
            place.s,
            place.along(axis, d),
        )


def plane_send(p, q, g, place):
    size = SUM_ROWS[g] // 64
    second, third = ORDERS[p][1:]
    for d, e in PLANE:
        block = 4 * ((place.coords[second] + d) % 4) + (place.coords[third] + e) % 4
        remote(
            q.s0.at[p, ds(block * size, size)],
            q.r1.at[p, 4 * d + e - 1],
            q.sems.at[0, 2, p],
            q.sems.at[1, 2, p],
            place.s,
            place.along(second, d) + place.along(third, e) - place.me,
        )


def exchange_done(g, r, place):
    q, rows = sum_refs(g, r), SUM_ROWS[g]
    src = q.__dict__["in"]
    for p in range(3):
        base = place.s * 3 * rows + p * rows
        wait_all(q.x.at[pl.ds(p * rows, rows)], q.sems.at[1, 0, p])

        @pl.loop(0, rows // 512)
        def _(k):
            at = ds(base + k * 512, 512)
            other = q.x[ds(p * rows + k * 512, 512), :]
            src[at, :] = (src[at, :].astype(F32) + other.astype(F32)).astype(BF)

        axis_send(p, base, q, g, src, place)


def axis_done(g, r, place):
    q, rows = sum_refs(g, r), SUM_ROWS[g]
    size = rows // 4
    for p in range(3):
        wait_all(q.r0.at[p], q.sems.at[1, 1, p])
        at = place.s * 3 * rows + p * rows + place.coords[ORDERS[p][0]] * size
        total = q.__dict__["in"][ds(at, size), :].astype(F32)
        for d in range(3):
            total = total + q.r0[p, d].astype(F32)
        q.s0[p] = total.astype(BF)
        plane_send(p, q, g, place)


def plane_done(g, r, place):
    q, rows = sum_refs(g, r), SUM_ROWS[g]
    size = rows // 64
    for p in range(3):
        wait_all(q.r1.at[p], q.sems.at[1, 2, p])
        second, third = [place.coords[axis] for axis in ORDERS[p][1:]]
        total = q.s0[p, ds((4 * second + third) * size, size), :].astype(F32)
        for d in range(15):
            total = total + q.r1[p, d].astype(F32)
        block = q.t.at[place.s, p, ds(offsets(p, rows, place)[1], size)]
        block[...] = total.astype(BF)
        for d, e in PLANE:
            to = place.along(ORDERS[p][1], d) + place.along(ORDERS[p][2], e) - place.me
            remote(block, block, q.sems.at[0, 3, p], q.sems.at[1, 3, p], place.s, to)


def cross_send(p, start, size, q, place):
    block = q.t.at[place.s, p, ds(start, size)]
    remote(block, block, q.sems.at[0, 4, p], q.sems.at[1, 4, p], 1 - place.s, place.me)


def plane_back(g, r, place):
    q, rows = sum_refs(g, r), SUM_ROWS[g]
    for p in range(3):
        wait_all(q.t.at[0, p, pl.ds(0, 15 * rows // 64)], q.sems.at[1, 3, p])
        at, axis = offsets(p, rows, place)[0], ORDERS[p][0]
        block = q.t.at[place.s, p, ds(at, rows // 4)]
        for d in (2, 1, 3):
            send_sem, recv_sem = q.sems.at[0, 4 + d, p], q.sems.at[1, 4 + d, p]
            remote(block, block, send_sem, recv_sem, place.s, place.along(axis, d))
        cross_send(p, at, rows // 4, q, place)


def gather_last(g, r, place):
    q, rows = sum_refs(g, r), SUM_ROWS[g]
    size = rows // 4
    for d in (1, 3, 2):
        for p in range(3):
            wait_all(q.t.at[0, p, pl.ds(0, size)], q.sems.at[1, 4 + d, p])
            c = (place.coords[ORDERS[p][0]] - d + 4) % 4
            cross_send(p, c * size, size, q, place)


def half_out(half, sem, g, r):
    q = sum_refs(g, r)
    return pltpu.make_async_copy(q.t.at[half], (r.sums0, r.sums1)[g].at[half], r.vsems.at[2, sem])


def sum_out(g, r, place):
    q = sum_refs(g, r)
    for p in range(3):
        wait_all(q.t.at[0, p], q.sems.at[1, 4, p])
    half_out(1 - place.s, g, g, r).start()
    half_out(place.s, 2 + g, g, r).start()


def sum_drain(g, r, place):
    q, rows = sum_refs(g, r), SUM_ROWS[g]
    for p in range(3):
        wait_all(q.x.at[pl.ds(0, rows)], q.sems.at[0, 0, p])
        wait_all(q.r0.at[p], q.sems.at[0, 1, p])
        for k in (2, 3):
            wait_all(q.r1.at[p], q.sems.at[0, k, p])
        for d in range(1, 4):
            wait_all(q.t.at[0, p, pl.ds(0, rows // 4)], q.sems.at[0, 4 + d, p])
        wait_all(q.t.at[0, p], q.sems.at[0, 4, p])
    half_out(1 - place.s, g, g, r).wait()
    half_out(place.s, 2 + g, g, r).wait()


def vec_exchange(r, place):
    remote(r.vec_own, r.vec_x, r.vsems.at[0, 0], r.vsems.at[1, 0], 1 - place.s, place.me)


def vec_send(axis, r, place):
    c = place.coords[axis]
    for d in (1, 2, 3):
        remote(
            r.vec_in.at[axis, c],
            r.vec_in.at[axis, c],
            r.vsems.at[0, 1 + axis],
            r.vsems.at[1, 1 + axis],
            place.s,
            place.along(axis, d),
        )


def vec_step(axis, r, place):
    if axis == 0:
        wait_all(r.vec_x, r.vsems.at[1, 0])
        total = r.vec_own[...] + r.vec_x[...]
    else:
        wait_all(r.vec_in.at[axis - 1, pl.ds(0, 3)], r.vsems.at[1, axis])
        total = (r.vec_in[axis - 1, 0] + r.vec_in[axis - 1, 1]) + (
            r.vec_in[axis - 1, 2] + r.vec_in[axis - 1, 3]
        )
    if axis < 3:
        r.vec_in[axis, place.coords[axis]] = total
        vec_send(axis, r, place)
    else:
        r.vec[...] = total


def vec_drain(r):
    wait_all(r.vec_x, r.vsems.at[0, 0])
    for axis in range(3):
        wait_all(r.vec_in.at[axis, pl.ds(0, 3)], r.vsems.at[0, 1 + axis])


def step_exchange(g, r, place):
    exchange_start(g, r, place)
    if g == 0:
        vec_exchange(r, place)


def step_scatter(g, r, place):
    exchange_done(g, r, place)
    if g == 0:
        vec_step(0, r, place)


def step_axis(g, r, place):
    axis_done(g, r, place)
    if g == 0:
        vec_step(1, r, place)


def step_plane(g, r, place):
    plane_done(g, r, place)
    if g == 0:
        vec_step(2, r, place)


def step_back(g, r, place):
    plane_back(g, r, place)
    if g == 0:
        vec_step(3, r, place)


SUM_STEPS = (
    step_exchange,
    step_scatter,
    step_axis,
    step_plane,
    step_back,
    gather_last,
    sum_out,
)
SUM_DURING_BACK = ((7, 2),)
SUM_AFTER_BACK = (3,)
SUM_TAIL = ((1, 1), (1, 2), (0, 4), (1, 3), (1, 4), (0, 5), (1, 5), (0, 6), (1, 6))


WEIGHTS = ["w_query", "w_key", "w_value", "w_out", "w_up", "w_down"]
INPUTS = ["inputs", "groups_hbm", "cotangent"] + [name + "_hbm" for name in WEIGHTS]
INPUTS += [name + "_hbm" for name in ("gain_one", "shift_one", "gain_two", "shift_two")]
OUTPUTS = {
    "output": ((1, ROWS, D), BF),
    "input_grad": ((1, ROWS, D), BF),
    "sums0": ((2, 3, 3072, 128), BF),
    "sums1": ((2, 3, 1024, 128), BF),
    "vec_hbm": ((8, D), F32),
}
SCRATCH = {
    "w_query": ((D, D), BF),
    "w_key": ((D, D), BF),
    "w_value": ((D, D), BF),
    "w_out": ((D, D), BF),
    "w_up": ((D, FF), BF),
    "w_down": ((FF, D), BF),
    "cot": ((ROWS, D), BF),
    "groups": ((2, ROWS), jnp.int32),
    "gain_one": ((1, D), F32),
    "shift_one": ((1, D), F32),
    "gain_two": ((1, D), F32),
    "shift_two": ((1, D), F32),
    "last_grad": ((ROWS, D), BF),
    "vec": ((8, D), F32),
    "hid": ((3, ROWS, D), BF),
    "q_out": ((2, 8, 64, 128), BF),
    "q_in": ((2, 16, 64, 128), BF),
    "o_out": ((2, 16, 80, 128), BF),
    "o_in": ((2, 16, 80, 128), BF),
    "do_out": ((2, 8, 80, 128), BF),
    "do_in": ((2, 16, 80, 128), BF),
    "dq_out": ((2, 16, 64, 128), BF),
    "dq_in": ((2, 16, 64, 128), BF),
    "dkv_acc": ((512, 128), F32),
    "dqt": ((8, 64, 256), F32),
    "lq": ((2, 2048, 128), BF),
    "qz": ((2048, 128), BF),
    "ld": ((2048, 128), BF),
    "neg_log": ((16, 8, 128), F32),
    "neg_delta": ((16, 8, 128), F32),
    "f_acc": ((4, 512, 128), F32),
    "f_top": ((4, 512, 128), F32),
    "att": ((2, ROWS, D), F32),
    "log_total": ((2, 8, 128), F32),
    "grp_q": ((16, 8, 128), jnp.int32),
    "kv_out": ((2, 8, ROWS, 128), BF),
    "kv_in": ((2, 32, ROWS, 128), BF),
    "grp_out": ((1, 8, 128), jnp.int32),
    "grp_in": ((32, 8, 128), jnp.int32),
    "ka": ((2, 4096, 128), BF),
    "va": ((2, 4096, 128), BF),
    "kat": ((64, 4096), BF),
    "att_low": ((2, ROWS, D), BF),
    "n_one": ((2, ROWS, D), F32),
    "f_one": ((2, ROWS, 128), F32),
    "first_low": ((2, ROWS, D), BF),
    "pre": ((2, ROWS, FF), F32),
    "act": ((2, ROWS, FF), BF),
    "n_two": ((2, ROWS, D), F32),
    "f_two": ((2, ROWS, 128), F32),
    "work": ((ROWS, D), F32),
    "dy": ((ROWS, D), F32),
    "down_low": ((2, ROWS, D), BF),
    "up_low": ((2, ROWS, FF), BF),
    "out_low": ((2, ROWS, D), BF),
    "dkv_out": ((32, ROWS, 128), BF),
    "dkv_in": ((2, 32, ROWS, 128), BF),
    "dq": ((2, ROWS, D), BF),
    "dk": ((2, ROWS, D), BF),
    "dv": ((2, ROWS, D), BF),
    "vec_own": ((8, D), F32),
    "vec_x": ((8, D), F32),
    "vec_in": ((3, 4, 8, D), F32),
}
for g, rows in enumerate(SUM_ROWS):
    SCRATCH |= {
        f"sum_in{g}": ((6 * rows, 128), BF),
        f"sum_x{g}": ((3 * rows, 128), BF),
        f"sum_r0{g}": ((3, 3, rows // 4, 128), BF),
        f"sum_r1{g}": ((3, 15, rows // 64, 128), BF),
        f"sum_s0{g}": ((3, rows // 4, 128), BF),
        f"sum_t{g}": ((2, 3, rows, 128), BF),
    }
SEMS = {"sems": (12, 2), "gsems": (4,), "load_sems": (13,), "out_sems": (3,), "kv_sems": (2, 4), "plane_sems": (2, 8), "sum_sems0": (2, 8, 3), "sum_sems1": (2, 8, 3), "vsems": (3, 4)}


def kernel(*refs):
    names = INPUTS + list(OUTPUTS) + list(SCRATCH) + list(SEMS)
    r = SimpleNamespace(**dict(zip(names, refs)))
    place = Place()
    for name in LOADED[:5]:
        load(name, r, place).start()
    greet(place)
    for name in LOADED[5:]:
        load(name, r, place).start()
    r.vec_own[...] = jnp.zeros_like(r.vec_own)

    @pl.loop(0, 2)
    def _(v):
        @pl.when(v == 0)
        def _():
            for name in LOADED[:5]:
                load(name, r, place).wait()

        project_queries(v, r)
        project_keys_values(v, r)

        @pl.when(v == 0)
        def _():
            all_here()
            send_groups(r, place)

        send_queries(v, r, place)
        send_keys_values(v, r, place)
        pass_on(v, r, place)

        @pl.when(v == 0)
        def _():
            wait_all(r.grp_in, r.gsems.at[1])
            wait_all(r.grp_q, r.gsems.at[3])
            make_aug(r)

        wait_all(r.q_in.at[v], r.sems.at[3, v])
        make_queries(v, r)
        attention(v, r, place)

        @pl.when(v == 0)
        def _():
            for name in LOADED[5:12]:
                load(name, r, place).wait()

        wait_all(r.o_in.at[v], r.sems.at[5, v])
        after_attention(v, r)

    finals = [
        pltpu.make_async_copy(r.hid.at[2], r.output.at[0], r.out_sems.at[0]),
        pltpu.make_async_copy(r.last_grad, r.input_grad.at[0], r.out_sems.at[1]),
        pltpu.make_async_copy(r.vec, r.vec_hbm, r.out_sems.at[2]),
    ]
    finals[0].start()
    load("cot", r, place).wait()
    r.dy[...] = r.cot[...].astype(F32)

    @pl.loop(0, 2)
    def _(step):
        v = 1 - step
        before_attention_back(v, r)
        send_do(v, r, place)

        @pl.when(v == 0)
        def _():
            weight_grads_early(r)
            SUM_STEPS[0](0, r, place)

        prepare_back(v, r)

        @pl.when(v == 0)
        def _():
            SUM_STEPS[1](0, r, place)

        wait_all(r.do_in.at[v], r.sems.at[7, v])

        attention_back(v, r, place)

        @pl.when(v == 0)
        def _():
            for step in SUM_AFTER_BACK:
                SUM_STEPS[step](0, r, place)

        wait_all(r.dq_in.at[v], r.sems.at[9, v])
        wait_all(r.dkv_in.at[v], r.sems.at[11, v])
        take_gradients(v, r)

        @pl.when(v == 1)
        def _():
            r.dy[...] = input_gradient(v, r).astype(F32)

    weight_grads_late(r)
    SUM_STEPS[0](1, r, place)
    r.last_grad[...] = input_gradient(0, r)
    finals[1].start()
    for g, step in SUM_TAIL:
        SUM_STEPS[step](g, r, place)

    finals[2].start()
    for copy in finals:
        copy.wait()
    vec_drain(r)
    for g in range(2):
        sum_drain(g, r, place)
    wait_sent(r.grp_in, r.gsems.at[0], place.self_kv, 32)
    wait_sent(r.grp_q, r.gsems.at[2], place.self_q, 16)

    @pl.loop(0, 2)
    def _(v):
        wait_sent(r.kv_in.at[v], r.sems.at[0, v], place.self_kv, 8)
        wait_all(r.kv_in.at[v, pl.ds(0, 24)], r.sems.at[1, v])
        wait_sent(r.q_in.at[v], r.sems.at[2, v], place.self_q, 16)
        wait_sent(r.o_in.at[v], r.sems.at[4, v], place.self_q, 16)
        wait_sent(r.do_in.at[v], r.sems.at[6, v], place.self_q, 16)
        wait_sent(r.dq_in.at[v], r.sems.at[8, v], place.self_q, 16)

    wait_sent(r.dkv_in.at[0], r.sems.at[10, 0], place.self_kv, 32)


def unpack(output, input_grad, early, late, vec):
    def body(*refs):
        output, input_grad, early, late, vec, output_to, input_grad_to = refs[:7]
        query, key, value, out, up, down = refs[7:13]
        got, small, up_f, down_f, vec_in, vec_out, sin, sout = refs[17:]
        loads = []
        for j in range(12):
            src = late.at[pl.ds(4 * j, 4)] if j < 3 else early.at[pl.ds(4 * (j - 3), 4)]
            loads.append(pltpu.make_async_copy(src, got.at[pl.ds(4 * j, 4)], sin.at[j]))
        order = [7, 8, 9, 10, 3, 4, 5, 6, 0, 1, 2, 11]
        for j in order:
            loads[j].start()
        get_vec = pltpu.make_async_copy(vec, vec_in, sin.at[12])
        get_vec.start()
        stores = [
            pltpu.make_async_copy(output, output_to, sout.at[12]),
            pltpu.make_async_copy(input_grad, input_grad_to, sout.at[13]),
        ]
        for copy in stores:
            copy.start()

        def store(j, src, dst):
            stores.append(pltpu.make_async_copy(src, dst, sout.at[j]))
            stores[-1].start()

        for j in order:
            loads[j].wait()
            tiles = [got[4 * j + k].astype(F32) for k in range(4)]
            cols = [slice(128 * k, 128 * k + 128) for k in range(4)]
            if j < 3 or j == 11:
                i = min(j, 3)
                for k in range(4):
                    small[i, :, cols[k]] = tiles[k]
                store(j, small.at[i], (query, key, value, out)[i])
            elif j < 7:
                at = 512 * (j - 3)
                for k in range(4):
                    up_f[:, at + 128 * k : at + 128 * k + 128] = tiles[k]
                store(j, up_f.at[:, pl.ds(at, 512)], up.at[:, pl.ds(at, 512)])
            else:
                for k in range(4):
                    down_f[512 * k : 512 * k + 512, cols[j - 7]] = tiles[k]
                if j == 10:
                    for k in range(4):
                        rows = pl.ds(512 * k, 512)
                        store(7 + k, down_f.at[rows], down.at[rows])
        get_vec.wait()
        for i in range(4):
            vec_out[i, 0] = vec_in[i]
            copy = pltpu.make_async_copy(vec_out.at[i, 0], refs[13 + i], sout.at[14 + i])
            copy.start()
            stores.append(copy)
        for copy in stores:
            copy.wait()

    square, hbm = jax.ShapeDtypeStruct((D, D), F32), pl.BlockSpec(memory_space=pl.ANY)
    rows = jax.ShapeDtypeStruct((1, ROWS, D), BF)
    shapes = [rows] * 2 + [square] * 4
    shapes += [jax.ShapeDtypeStruct((D, FF), F32), jax.ShapeDtypeStruct((FF, D), F32)]
    return pl.pallas_call(
        body,
        out_shape=shapes + [jax.ShapeDtypeStruct((D,), F32)] * 4,
        in_specs=[hbm] * 5,
        out_specs=[hbm] * 12,
        scratch_shapes=[
            pltpu.VMEM((48, 512, 128), BF),
            pltpu.VMEM((4, D, D), F32),
            pltpu.VMEM((D, FF), F32),
            pltpu.VMEM((FF, D), F32),
            pltpu.VMEM((8, D), F32),
            pltpu.VMEM((4, 1, D), F32),
            pltpu.SemaphoreType.DMA((13,)),
            pltpu.SemaphoreType.DMA((18,)),
        ],
        compiler_params=pltpu.CompilerParams(vmem_limit_bytes=60 * 2**20),
        name="unpack",
    )(output, input_grad, early, late, vec)


def on_device(inputs, groups, cotangent, *params):
    vectors = [x.reshape(1, D) for x in params[6:]]
    hbm = pl.BlockSpec(memory_space=pl.ANY)
    out = pl.pallas_call(
        kernel,
        out_shape=[jax.ShapeDtypeStruct(shape, kind) for shape, kind in OUTPUTS.values()],
        in_specs=[hbm] * len(INPUTS),
        out_specs=[hbm] * len(OUTPUTS),
        scratch_shapes=[pltpu.VMEM(shape, kind) for shape, kind in SCRATCH.values()]
        + [pltpu.SemaphoreType.DMA(shape) for shape in SEMS.values()],
        compiler_params=pltpu.CompilerParams(
            collective_id=0, has_side_effects=True, vmem_limit_bytes=62 * 2**20
        ),
        name="visits",
    )(inputs, groups, cotangent, *params[:6], *vectors)
    return unpack(*out[:2], out[2].reshape(36, 512, 128), out[3].reshape(12, 512, 128), out[4])


def solution(mesh):
    rows = P(None, "dp", None)
    return jax.shard_map(
        on_device,
        mesh=mesh,
        in_specs=(rows, P(None, "dp"), rows) + (P(),) * 10,
        out_specs=(P("section", "dp", None),) * 2 + (P(),) * 10,
        check_vma=False,
    )
```

```python
from types import SimpleNamespace

import jax
import jax.numpy as jnp
from jax import lax
from jax.experimental import pallas as pl
from jax.experimental.pallas import tpu as pltpu
from jax.sharding import PartitionSpec as P

F32, BF = jnp.float32, jnp.bfloat16
BIG = 1e30
ROWS, D, FF, HEADS = 128, 512, 2048, 8
MESH = pl.DeviceIdType.MESH


def nt(a, b):
    return lax.dot_general(a, b, (((1,), (1,)), ((), ())), preferred_element_type=F32)


def nn(a, b):
    return lax.dot_general(a, b, (((1,), (0,)), ((), ())), preferred_element_type=F32)


def tn(a, b):
    return lax.dot_general(a, b, (((0,), (0,)), ((), ())), preferred_element_type=F32)


def lanes(shape):
    return lax.broadcasted_iota(jnp.int32, shape, len(shape) - 1)


def subs(shape):
    return lax.broadcasted_iota(jnp.int32, shape, len(shape) - 2)


def ds(start, size):
    if isinstance(start, int):
        return pl.ds(start, size)
    return pl.ds(pl.multiple_of(start, size), size)


def split3(x):
    a = x.astype(BF).astype(F32)
    b = (x - a).astype(BF).astype(F32)
    return a, b, (x - a - b).astype(BF).astype(F32)


def tile_of(r, t):
    return 4 * r + (r + t) % 4


def mean(x):
    return jnp.mean(x, axis=-1, keepdims=True)


def norm(x):
    centred = x - mean(x)
    factor = lax.rsqrt(mean(centred * centred) + 1e-05)
    return centred * factor, factor


def norm_back(dy, n, factor, gain):
    u = dy * gain
    return factor * (u - mean(u) - n * mean(u * n))


GELU_C = 0.7978845608028654


def gelu(x):
    return 0.5 * x * (1.0 + jnp.tanh(GELU_C * (x + 0.044715 * x * x * x)))


def gelu_slope(x):
    sq = x * x
    th = jnp.tanh(GELU_C * x * (1.0 + 0.044715 * sq))
    return 0.5 * (1.0 + th) + 0.5 * x * (1.0 - th * th) * (GELU_C * (1.0 + 3 * 0.044715 * sq))


class Place:
    def __init__(self):
        self.me = lax.axis_index("dp")
        self.s = lax.axis_index("section")
        me = self.me
        self.coords = (me % 4, me // 16, (me // 4) % 4)
        x, y, z = self.coords
        self.t = (x + y + z) % 4
        self.head = 4 * (y % 2) + x
        self.micro = y // 2
        self.own_t = ((me // 2) % 4 - me // 8 + 32) % 4
        self.own_slot = 2 * (me // 8) + me % 2
        mine = self.micro == self.s
        self.self_kv = mine & (me % 2 == self.s)
        self.self_q = mine & (self.own_t == self.t)

    def along(self, axis, d):
        c = self.coords[axis]
        return self.me + ((c + d) % 4 - c) * (1, 16, 4)[axis]

    def chip_in_plane(self, h):
        return 16 * (2 * self.s + h // 4) + 4 * self.coords[2] + h % 4

    def chip(self, h, t):
        x, y = h % 4, 2 * self.s + h // 4
        return 16 * y + 4 * ((t - x - y + 8) % 4) + x

    def send(self, src, dst, send_sem, recv_sem, section, dp):
        to_self = (section == self.s) & (dp == self.me)

        @pl.when(jnp.logical_not(to_self))
        def _():
            pltpu.make_async_remote_copy(
                src_ref=src,
                dst_ref=dst,
                send_sem=send_sem,
                recv_sem=recv_sem,
                device_id=(section, dp),
                device_id_type=MESH,
            ).start()

        @pl.when(to_self)
        def _():
            pltpu.make_async_copy(src, dst, recv_sem).start()


def remote(src, dst, send_sem, recv_sem, section, dp):
    pltpu.make_async_remote_copy(
        src_ref=src,
        dst_ref=dst,
        send_sem=send_sem,
        recv_sem=recv_sem,
        device_id=(section, dp),
        device_id_type=MESH,
    ).start()


def wait_all(ref, sem):
    pltpu.make_async_copy(ref, ref, sem).wait()


def wait_sent(ref, sem, to_self, count):
    @pl.when(to_self)
    def _():
        wait_all(ref.at[pl.ds(0, count - 1)], sem)

    @pl.when(jnp.logical_not(to_self))
    def _():
        wait_all(ref.at[pl.ds(0, count)], sem)


def greet(place):
    sem = pltpu.get_barrier_semaphore()

    @pl.loop(1, 128)
    def _(k):
        other = (place.s * 64 + place.me + k) % 128
        pl.semaphore_signal(sem, inc=1, device_id=(other // 64, other % 64), device_id_type=MESH)


def all_here():
    pl.semaphore_wait(pltpu.get_barrier_semaphore(), 127)


LOADED = ["hid", "w_query", "w_key", "w_value", "groups", "w_out", "w_up", "w_down", "gain_one"]
LOADED += ["shift_one", "gain_two", "shift_two", "cot"]


def load(name, r, place):
    sem = r.load_sems.at[LOADED.index(name)]
    if name == "hid":
        return pltpu.make_async_copy(r.inputs.at[place.s], r.hid.at[0], sem)
    if name == "cot":
        return pltpu.make_async_copy(r.cotangent.at[place.s], r.cot, sem)
    return pltpu.make_async_copy(getattr(r, name + "_hbm"), getattr(r, name), sem)


def pack(tile, odd):
    low = lanes((64, 128)) < 64
    if odd:
        return jnp.where(low, pltpu.roll(tile[:64], 64, 1), tile[64:])
    return jnp.where(low, tile[:64], pltpu.roll(tile[64:], 64, 1))


def spread(packed, odd):
    turned = pltpu.roll(packed, 64, 1)
    return jnp.concatenate([turned, packed] if odd else [packed, turned], axis=0)


def parts_in_rows(rows):
    at = subs((16, 128))
    out = jnp.zeros((16, 128), F32)
    for i, part in enumerate(rows):
        out = jnp.where(at == i, part, out)
    return out.astype(BF)


def project_queries(v, r):
    q = nn(r.hid[v], r.w_query[...]).astype(BF).astype(F32) * 0.125
    for h in range(HEADS):
        tile = q[:, 128 * (h // 2) : 128 * (h // 2) + 128]
        r.q_out[v, h] = pack(tile, h % 2 == 1).astype(BF)


def project_keys_values(v, r):
    hid = r.hid[v]
    k = nn(hid, r.w_key[...]).astype(BF).astype(F32)
    w = nn(hid, r.w_value[...]).astype(BF).astype(F32)
    low = lanes((ROWS, 128)) < 64
    for h in range(HEADS):
        cols = slice(128 * (h // 2), 128 * (h // 2) + 128)
        kt, vt = k[:, cols], w[:, cols]
        if h % 2 == 0:
            vt = pltpu.roll(vt, 64, 1)
        else:
            kt = pltpu.roll(kt, 64, 1)
        r.kv_out[v, h] = jnp.where(low, kt, vt).astype(BF)


def to_queries(src, dst, send_sem, recv_sem, place):
    @pl.loop(0, HEADS)
    def _(a):
        h = (place.me // 4 + a) % 8
        for b in range(2):
            core, chip = (place.me + b) % 2, place.chip(h, place.own_t)
            place.send(src(h), dst.at[place.own_slot], send_sem, recv_sem, core, chip)


def to_keys(src, dst, send_sem, recv_sem, place):
    n = place.me // 2

    @pl.loop(0, HEADS)
    def _(a):
        h = 2 * ((n // 8 + a // 2) % 4) + (n // 4 + a) % 2
        for b in range(4):
            chip = place.chip(h, (n + b) % 4)
            place.send(src(h), dst.at[n], send_sem, recv_sem, place.me % 2, chip)


def send_queries(v, r, place):
    to_queries(
        lambda h: r.q_out.at[v, h], r.q_in.at[v], r.sems.at[2, v], r.sems.at[3, v], place
    )


def send_keys_values(v, r, place):
    x, y, _ = place.coords
    n = place.me // 2

    @pl.loop(0, HEADS)
    def _(a):
        h = 2 * ((n // 8 + a // 2) % 4) + (n // 4 + a) % 2
        place.send(
            r.kv_out.at[v, h],
            r.kv_in.at[v, n],
            r.sems.at[0, v],
            r.plane_sems.at[v, 2 * y + x // 2],
            x % 2,
            place.chip_in_plane(h),
        )


def pass_on(v, r, place):
    z = place.coords[2]

    @pl.loop(0, 4)
    def _(y):
        for b in range(2):
            block = r.kv_in.at[v, 8 * y + 2 * z + b]
            wait_all(block, r.plane_sems.at[v, 2 * y + b])
            for d in (2, 1, 3):
                to = place.along(2, d)
                remote(block, block, r.sems.at[1, v], r.kv_sems.at[v, y], place.s, to)


def send_groups(r, place):
    r.grp_out[0] = jnp.broadcast_to(r.groups[pl.ds(place.s, 1), :], (8, 128))
    to_queries(lambda h: r.grp_out.at[0], r.grp_q, r.gsems.at[2], r.gsems.at[3], place)
    to_keys(lambda h: r.grp_out.at[0], r.grp_in, r.gsems.at[0], r.gsems.at[1], place)


def column_of(row):
    return jnp.transpose(jnp.broadcast_to(row.astype(F32), (128, 128)))


def make_aug(r):
    ln = lanes((ROWS, 128))
    inside = (ln >= 64) & (ln < 68)

    @pl.loop(0, 32)
    def _(n):
        g = column_of(r.grp_in[n][0:1, :]).astype(jnp.int32)
        aug = jnp.where(inside & (ln - 64 != g), -BIG, 0.0).astype(BF)
        for v in range(2):
            r.ka[v, ds(n * 128, 128), :] = aug

    @pl.loop(0, 16)
    def _(n):
        g = column_of(r.grp_q[n][0:1, :]).astype(jnp.int32)
        aug = jnp.where(ln - 64 == g, 1.0, 0.0).astype(BF)
        for v in range(2):
            r.lq[v, ds(n * 128, 128), :] = aug


def make_queries(v, r):
    low = lanes((ROWS, 128)) < 64

    @pl.loop(0, 16)
    def _(n):
        rows = ds(n * 128, 128)
        q = spread(r.q_in[v, n].astype(F32), False)
        r.lq[v, rows, :] = jnp.where(low, q, r.lq[v, rows, :].astype(F32)).astype(BF)


def make_kv(v, c, r):
    ln = lanes((ROWS, 128))
    low = ln < 64
    ones = jnp.where(ln < 1, 1.0, 0.0)

    @pl.loop(0, 8)
    def _(k):
        n = 8 * c + k
        rows = ds(n * 128, 128)
        kv = r.kv_in[v, n].astype(F32)
        r.ka[v, rows, :] = jnp.where(low, kv, r.ka[v, rows, :].astype(F32)).astype(BF)
        r.va[v, rows, :] = jnp.where(low, ones, kv).astype(BF)


def fwd_body(v, c, j, masked, r, place):
    width = 1024
    rows = ds(c * width, width)
    sc = nt(r.lq[v, ds(512 * j, 512), :], r.ka[v, rows, :])
    if masked:
        col, row = lanes((512, width)), subs((512, width))
        tiles = [tile_of(2 * j + k, place.t) for k in range(2)]
        at = 256 * (col // 128) + col % 128 + (2048 * c + 128 * place.s)
        limit = row % 256 + 256 * jnp.where(row < 256, tiles[0], tiles[1])
        sc = jnp.where(at <= limit, sc, -BIG)
    top = r.f_top[j][:, 0:1]
    new = jnp.maximum(top, jnp.max(sc, axis=1, keepdims=True))
    p = jnp.exp(sc - new).astype(BF)
    r.f_acc[j] = r.f_acc[j] * jnp.exp(top - new) + nn(p, r.va[v, rows, :])
    r.f_top[j] = jnp.broadcast_to(new, (512, 128))


def fwd_finish(v, j, r, place):
    acc = r.f_acc[j]
    total = acc[:, 0:1]
    out = acc / total
    logs = jnp.broadcast_to(r.f_top[j][:, 0:1] + jnp.log(total), (512, 128))
    for k in range(4):
        rows = slice(128 * k, 128 * k + 128)
        r.o_out[v, 4 * j + k, 0:64] = pack(out[rows], True).astype(BF)
        row = jnp.transpose(logs[rows])[0:1]
        r.o_out[v, 4 * j + k, 64:80] = parts_in_rows(split3(row))
    for k in range(2):
        for turn in range(2):
            half = (turn + place.s) % 2
            place.send(
                r.o_out.at[v, 4 * j + 2 * k + half],
                r.o_in.at[v, 2 * place.head + place.s],
                r.sems.at[4, v],
                r.sems.at[5, v],
                place.micro,
                2 * tile_of(2 * j + k, place.t) + half,
            )


def attention(v, r, place):
    r.f_acc[...] = jnp.zeros_like(r.f_acc)
    r.f_top[...] = jnp.full_like(r.f_top, -2 * BIG)

    @pl.loop(0, 4)
    def _(c):
        wait_all(r.kv_in.at[v, pl.ds(0, 6)], r.kv_sems.at[v, c])
        make_kv(v, c, r)
        fwd_body(v, c, c, True, r, place)
        fwd_finish(v, c, r, place)

        @pl.loop(c + 1, 4)
        def _(j):
            fwd_body(v, c, j, False, r, place)


def after_attention(v, r):
    low = lanes((ROWS, 128)) < 64
    weights = [[], []]
    for h in range(HEADS):
        logs = []
        for core in range(2):
            x = r.o_in[v, 2 * h + core, 64:80].astype(F32)
            logs.append(x[0:1] + x[1:2] + x[2:3])
        top = jnp.maximum(logs[0], logs[1])
        w = [jnp.exp(x - top) for x in logs]
        total = w[0] + w[1]
        r.log_total[v, h : h + 1] = top + jnp.log(total)
        for core in range(2):
            weights[core].append(w[core] / total)
    cols = jnp.transpose(jnp.concatenate(weights[0] + weights[1] + [jnp.zeros((112, 128), F32)], axis=0))
    for i in range(HEADS // 2):
        whole = []
        for h in (2 * i, 2 * i + 1):
            got = [spread(r.o_in[v, 2 * h + k, 0:64].astype(F32), h % 2 == 1) for k in range(2)]
            whole.append(got[0] * cols[:, h : h + 1] + got[1] * cols[:, 8 + h : 9 + h])
        pair = jnp.where(low, whole[0], whole[1])
        r.att[v, :, 128 * i : 128 * i + 128] = pair
        r.att_low[v, :, 128 * i : 128 * i + 128] = pair.astype(BF)
    mixed = r.hid[v].astype(F32) + nn(r.att_low[v], r.w_out[...])
    n_one, f_one = norm(mixed)
    first = n_one * r.gain_one[...] + r.shift_one[...]
    first_low = first.astype(BF)
    r.n_one[v] = n_one
    r.f_one[v] = jnp.broadcast_to(f_one, (ROWS, 128))
    r.first_low[v] = first_low
    r.work[...] = first

    @pl.loop(0, 4)
    def _(j):
        cols = ds(j * 512, 512)
        pre = nn(r.first_low[v], r.w_up[:, cols])
        r.pre[v, :, cols] = pre
        act = gelu(pre).astype(BF)
        r.act[v, :, cols] = act
        r.work[...] += nn(act, r.w_down[cols, :])

    n_two, f_two = norm(r.work[...])
    r.n_two[v] = n_two
    r.f_two[v] = jnp.broadcast_to(f_two, (ROWS, 128))
    r.hid[v + 1] = (n_two * r.gain_two[...] + r.shift_two[...]).astype(BF)


def before_attention_back(v, r):
    dy = r.dy[...]
    n_two = r.n_two[v]
    r.vec_own[2:3, :] += jnp.sum(dy * n_two, axis=0, keepdims=True)
    r.vec_own[3:4, :] += jnp.sum(dy, axis=0, keepdims=True)
    grad_two = norm_back(dy, n_two, r.f_two[v][:, 0:1], r.gain_two[...])
    r.down_low[v] = grad_two.astype(BF)
    r.work[...] = grad_two

    @pl.loop(0, 4)
    def _(j):
        cols = ds(j * 512, 512)
        grad = nt(r.down_low[v], r.w_down[cols, :])
        up = (grad * gelu_slope(r.pre[v, :, cols])).astype(BF)
        r.up_low[v, :, cols] = up
        r.work[...] += nt(up, r.w_up[:, cols])

    dz = r.work[...]
    n_one = r.n_one[v]
    r.vec_own[0:1, :] += jnp.sum(dz * n_one, axis=0, keepdims=True)
    r.vec_own[1:2, :] += jnp.sum(dz, axis=0, keepdims=True)
    grad_one = norm_back(dz, n_one, r.f_one[v][:, 0:1], r.gain_one[...])
    out_low = grad_one.astype(BF)
    r.out_low[v] = out_low
    r.work[...] = grad_one
    grad_att = nt(out_low, r.w_out[...]).astype(BF).astype(F32)
    ln = lanes((ROWS, 128))
    low = ln < 64
    deltas = jnp.zeros((ROWS, 128), F32)
    for h in range(HEADS):
        cols = slice(128 * (h // 2), 128 * (h // 2) + 128)
        product = grad_att[:, cols] * r.att[v, :, cols]
        mine = jnp.where(low, product, 0.0) if h % 2 == 0 else jnp.where(low, 0.0, product)
        deltas = jnp.where(ln == h, jnp.sum(mine, axis=1, keepdims=True), deltas)
    deltas = jnp.transpose(deltas)
    for h in range(HEADS):
        tile = grad_att[:, 128 * (h // 2) : 128 * (h // 2) + 128]
        r.do_out[v, h, 0:64] = pack(tile, h % 2 == 1).astype(BF)
        rows = split3(-deltas[h : h + 1]) + split3(-r.log_total[v, h : h + 1])
        r.do_out[v, h, 64:80] = parts_in_rows(rows)


def send_do(v, r, place):
    to_queries(
        lambda h: r.do_out.at[v, h], r.do_in.at[v], r.sems.at[6, v], r.sems.at[7, v], place
    )


def prepare_back(v, r):
    low = lanes((ROWS, 128)) < 64

    @pl.loop(0, 16)
    def _(n):
        rows = ds(n * 128, 128)
        r.qz[rows, :] = jnp.where(low, r.lq[v, rows, :].astype(F32), 0.0).astype(BF)

    @pl.loop(0, 8)
    def _(i):
        rows = ds(i * 512, 512)
        r.kat[:, rows] = jnp.transpose(r.ka[v, rows, :].astype(F32))[:64].astype(BF)

    r.dqt[...] = jnp.zeros_like(r.dqt)


def take_do(v, r):
    low = lanes((ROWS, 128)) < 64

    @pl.loop(0, 16)
    def _(n):
        do = spread(r.do_in[v, n, 0:64].astype(F32), True)
        r.ld[ds(n * 128, 128), :] = jnp.where(low, 0.0, do).astype(BF)
        x = r.do_in[v, n, 64:80].astype(F32)
        r.neg_delta[n] = jnp.broadcast_to(x[0:1] + x[1:2] + x[2:3], (8, 128))
        r.neg_log[n] = jnp.broadcast_to(x[3:4] + x[4:5] + x[5:6], (8, 128))


def bwd_body(v, c, tiles, masked, r, place):
    rows = ds(c * 512, 512)
    probs, grads = [], []
    for i in tiles:
        mine = ds(i * 256, 256)
        x = nt(r.ka[v, rows, :], r.lq[v, mine, :])
        x = x + jnp.concatenate([r.neg_log[2 * i][0:1], r.neg_log[2 * i + 1][0:1]], axis=1)
        if masked:
            row, col = subs((512, 256)), lanes((512, 256))
            shift = 1024 * c + 128 * place.s - 256 * tile_of(i, place.t)
            x = jnp.where(256 * (row // 128) + row % 128 + shift <= col, x, -BIG)
        p = jnp.exp(x)
        dp = nt(r.va[v, rows, :], r.ld[mine, :])
        dp = dp + jnp.concatenate([r.neg_delta[2 * i][0:1], r.neg_delta[2 * i + 1][0:1]], axis=1)
        probs.append(p.astype(BF))
        grads.append((p * dp).astype(BF))
    size = 256 * len(tiles)
    queries = pl.ds(pl.multiple_of(tiles[0] * 256, 256), size)
    r.dkv_acc[...] += nn(jnp.concatenate(grads, axis=1), r.qz[queries, :]) + nn(
        jnp.concatenate(probs, axis=1), r.ld[queries, :]
    )
    for i, dsc in zip(tiles, grads):
        r.dqt[i] += nn(r.kat[:, rows], dsc)


def bwd_finish(v, i, r, place):
    dq = jnp.transpose(jnp.concatenate([r.dqt[i], jnp.zeros((64, 256), F32)], axis=0))
    for k in range(2):
        r.dq_out[v, 2 * i + k] = pack(dq[128 * k : 128 * k + 128], False).astype(BF)
    for turn in range(2):
        half = (turn + place.s) % 2
        place.send(
            r.dq_out.at[v, 2 * i + half],
            r.dq_in.at[v, 2 * place.head + place.s],
            r.sems.at[8, v],
            r.sems.at[9, v],
            place.micro,
            2 * tile_of(i, place.t) + half,
        )


def chunk_at(a, place):
    first = (a // 2 + place.head) % 4
    return jnp.where(a % 2 == 0, first, 7 - first)


def chunk_at(a, place):
    first = (a // 2 + place.coords[0] + place.t) % 4
    return jnp.where((a + place.coords[1]) % 2 == 0, first, 7 - first)


def attention_back(v, r, place):
    take_do(v, r)

    @pl.when(v == 0)
    def _():
        wait_sent(r.dkv_in.at[1], r.sems.at[10, 1], place.self_kv, 32)

    @pl.loop(0, 8)
    def _(a):
        c = chunk_at(a, place)

        @pl.loop(0, jnp.where(a == 7, c, 0))
        def _(i):
            bwd_finish(v, i, r, place)

        r.dkv_acc[...] = jnp.zeros_like(r.dkv_acc)

        @pl.when(c % 2 == 0)
        def _():
            bwd_body(v, c, [c, c + 1], True, r, place)

        @pl.when(c % 2 == 1)
        def _():
            bwd_body(v, c, [c], True, r, place)

        @pl.loop(c // 2 + 1, 4)
        def _(m):
            bwd_body(v, c, [2 * m, 2 * m + 1], False, r, place)

        for b in range(4):
            k = (b + place.t) % 4
            n = 4 * c + k
            r.dkv_out[n] = r.dkv_acc[ds(k * 128, 128), :].astype(BF)
            place.send(
                r.dkv_out.at[n],
                r.dkv_in.at[v, 4 * place.head + place.t],
                r.sems.at[10, v],
                r.sems.at[11, v],
                place.micro,
                2 * n + place.s,
            )
        for after, step in SUM_DURING_BACK:

            @pl.when((v == 0) & (a == after))
            def _():
                SUM_STEPS[step](0, r, place)

    @pl.loop(chunk_at(7, place), 8)
    def _(i):
        bwd_finish(v, i, r, place)


def take_gradients(v, r):
    low = lanes((ROWS, 128)) < 64
    for i in range(HEADS // 2):
        cols = slice(128 * i, 128 * i + 128)
        dq, dkv = [], []
        for h in (2 * i, 2 * i + 1):
            both = r.dq_in[v, 2 * h].astype(F32) + r.dq_in[v, 2 * h + 1].astype(F32)
            dq.append(spread(both * 0.125, h % 2 == 1))
            four = [r.dkv_in[v, 4 * h + t].astype(F32) for t in range(4)]
            dkv.append((four[0] + four[1]) + (four[2] + four[3]))
        r.dq[v, :, cols] = jnp.where(low, dq[0], dq[1]).astype(BF)
        r.dk[v, :, cols] = jnp.where(low, dkv[0], pltpu.roll(dkv[1], 64, 1)).astype(BF)
        r.dv[v, :, cols] = jnp.where(low, pltpu.roll(dkv[0], 64, 1), dkv[1]).astype(BF)


def input_gradient(v, r):
    return (
        r.work[...]
        + nt(r.dq[v], r.w_query[...])
        + nt(r.dk[v], r.w_key[...])
        + nt(r.dv[v], r.w_value[...])
    ).astype(BF)


def both(ref):
    return jnp.concatenate([ref[0], ref[1]], axis=0)


def put(ref, unit, tile):
    ref[ds(unit * 512, 512), :] = tile.astype(BF)


def weight_grads_early(r):
    @pl.loop(0, 4)
    def _(j):
        cols = ds(j * 512, 512)
        up = jnp.concatenate([r.up_low[0, :, cols], r.up_low[1, :, cols]], axis=0)
        grad = tn(both(r.first_low), up)
        for k in range(4):
            put(r.sum_in0, 4 * j + k, grad[:, 128 * k : 128 * k + 128])
        act = jnp.concatenate([r.act[0, :, cols], r.act[1, :, cols]], axis=0)
        grad = tn(act, both(r.down_low))
        for k in range(4):
            put(r.sum_in0, 16 + 4 * k + j, grad[:, 128 * k : 128 * k + 128])

    grad = tn(both(r.att_low), both(r.out_low))
    for k in range(4):
        put(r.sum_in0, 32 + k, grad[:, 128 * k : 128 * k + 128])


def weight_grads_late(r):
    hid = jnp.concatenate([r.hid[0], r.hid[1]], axis=0)
    for i, ref in enumerate((r.dq, r.dk, r.dv)):
        grad = tn(hid, both(ref))
        for k in range(4):
            put(r.sum_in1, 4 * i + k, grad[:, 128 * k : 128 * k + 128])


SUM_ROWS = (3072, 1024)
ORDERS = ((0, 1, 2), (1, 2, 0), (2, 0, 1))
PLANE = [(d, e) for d in range(4) for e in range(4) if (d, e) != (0, 0)]


def sum_refs(g, r):
    names = ("in", "x", "r0", "r1", "s0", "t", "sems")
    return SimpleNamespace(**{n: getattr(r, "sum_" + n + str(g)) for n in names})


def offsets(p, rows, place):
    first, second, third = [place.coords[axis] for axis in ORDERS[p]]
    at = first * (rows // 4)
    return at, at + (4 * second + third) * (rows // 64)


def exchange_start(g, r, place):
    q, rows = sum_refs(g, r), SUM_ROWS[g]
    for p in range(3):
        remote(
            q.__dict__["in"].at[ds((1 - place.s) * 3 * rows + p * rows, rows)],
            q.x.at[pl.ds(p * rows, rows)],
            q.sems.at[0, 0, p],
            q.sems.at[1, 0, p],
            1 - place.s,
            place.me,
        )


def axis_send(p, base, q, g, src, place):
    size = SUM_ROWS[g] // 4
    axis = ORDERS[p][0]
    for d in (2, 1, 3):
        c = (place.coords[axis] + d) % 4
        remote(
            src.at[ds(base + c * size, size)],
            q.r0.at[p, d - 1],
            q.sems.at[0, 1, p],
            q.sems.at[1, 1, p],
            place.s,
            place.along(axis, d),
        )


def plane_send(p, q, g, place):
    size = SUM_ROWS[g] // 64
    second, third = ORDERS[p][1:]
    for d, e in PLANE:
        block = 4 * ((place.coords[second] + d) % 4) + (place.coords[third] + e) % 4
        remote(
            q.s0.at[p, ds(block * size, size)],
            q.r1.at[p, 4 * d + e - 1],
            q.sems.at[0, 2, p],
            q.sems.at[1, 2, p],
            place.s,
            place.along(second, d) + place.along(third, e) - place.me,
        )


def exchange_done(g, r, place):
    q, rows = sum_refs(g, r), SUM_ROWS[g]
    src = q.__dict__["in"]
    for p in range(3):
        base = place.s * 3 * rows + p * rows
        wait_all(q.x.at[pl.ds(p * rows, rows)], q.sems.at[1, 0, p])

        @pl.loop(0, rows // 512)
        def _(k):
            at = ds(base + k * 512, 512)
            other = q.x[ds(p * rows + k * 512, 512), :]
            src[at, :] = (src[at, :].astype(F32) + other.astype(F32)).astype(BF)

        axis_send(p, base, q, g, src, place)


def axis_done(g, r, place):
    q, rows = sum_refs(g, r), SUM_ROWS[g]
    size = rows // 4
    for p in range(3):
        wait_all(q.r0.at[p], q.sems.at[1, 1, p])
        at = place.s * 3 * rows + p * rows + place.coords[ORDERS[p][0]] * size
        total = q.__dict__["in"][ds(at, size), :].astype(F32)
        for d in range(3):
            total = total + q.r0[p, d].astype(F32)
        q.s0[p] = total.astype(BF)
        plane_send(p, q, g, place)


def plane_done(g, r, place):
    q, rows = sum_refs(g, r), SUM_ROWS[g]
    size = rows // 64
    for p in range(3):
        wait_all(q.r1.at[p], q.sems.at[1, 2, p])
        second, third = [place.coords[axis] for axis in ORDERS[p][1:]]
        total = q.s0[p, ds((4 * second + third) * size, size), :].astype(F32)
        for d in range(15):
            total = total + q.r1[p, d].astype(F32)
        block = q.t.at[place.s, p, ds(offsets(p, rows, place)[1], size)]
        block[...] = total.astype(BF)
        for d, e in PLANE:
            to = place.along(ORDERS[p][1], d) + place.along(ORDERS[p][2], e) - place.me
            remote(block, block, q.sems.at[0, 3, p], q.sems.at[1, 3, p], place.s, to)


def cross_send(p, start, size, q, place):
    block = q.t.at[place.s, p, ds(start, size)]
    remote(block, block, q.sems.at[0, 4, p], q.sems.at[1, 4, p], 1 - place.s, place.me)


def plane_back(g, r, place):
    q, rows = sum_refs(g, r), SUM_ROWS[g]
    for p in range(3):
        wait_all(q.t.at[0, p, pl.ds(0, 15 * rows // 64)], q.sems.at[1, 3, p])
        at, axis = offsets(p, rows, place)[0], ORDERS[p][0]
        block = q.t.at[place.s, p, ds(at, rows // 4)]
        for d in (2, 1, 3):
            send_sem, recv_sem = q.sems.at[0, 4 + d, p], q.sems.at[1, 4 + d, p]
            remote(block, block, send_sem, recv_sem, place.s, place.along(axis, d))
        cross_send(p, at, rows // 4, q, place)


def gather_last(g, r, place):
    q, rows = sum_refs(g, r), SUM_ROWS[g]
    size = rows // 4
    for d in (1, 3, 2):
        for p in range(3):
            wait_all(q.t.at[0, p, pl.ds(0, size)], q.sems.at[1, 4 + d, p])
            c = (place.coords[ORDERS[p][0]] - d + 4) % 4
            cross_send(p, c * size, size, q, place)


def half_out(half, sem, g, r):
    q = sum_refs(g, r)
    return pltpu.make_async_copy(q.t.at[half], (r.sums0, r.sums1)[g].at[half], r.vsems.at[2, sem])


def sum_out(g, r, place):
    q = sum_refs(g, r)
    for p in range(3):
        wait_all(q.t.at[0, p], q.sems.at[1, 4, p])
    half_out(1 - place.s, g, g, r).start()
    half_out(place.s, 2 + g, g, r).start()


def sum_drain(g, r, place):
    q, rows = sum_refs(g, r), SUM_ROWS[g]
    for p in range(3):
        wait_all(q.x.at[pl.ds(0, rows)], q.sems.at[0, 0, p])
        wait_all(q.r0.at[p], q.sems.at[0, 1, p])
        for k in (2, 3):
            wait_all(q.r1.at[p], q.sems.at[0, k, p])
        for d in range(1, 4):
            wait_all(q.t.at[0, p, pl.ds(0, rows // 4)], q.sems.at[0, 4 + d, p])
        wait_all(q.t.at[0, p], q.sems.at[0, 4, p])
    half_out(1 - place.s, g, g, r).wait()
    half_out(place.s, 2 + g, g, r).wait()


def vec_exchange(r, place):
    remote(r.vec_own, r.vec_x, r.vsems.at[0, 0], r.vsems.at[1, 0], 1 - place.s, place.me)


def vec_send(axis, r, place):
    c = place.coords[axis]
    for d in (1, 2, 3):
        remote(
            r.vec_in.at[axis, c],
            r.vec_in.at[axis, c],
            r.vsems.at[0, 1 + axis],
            r.vsems.at[1, 1 + axis],
            place.s,
            place.along(axis, d),
        )


def vec_step(axis, r, place):
    if axis == 0:
        wait_all(r.vec_x, r.vsems.at[1, 0])
        total = r.vec_own[...] + r.vec_x[...]
    else:
        wait_all(r.vec_in.at[axis - 1, pl.ds(0, 3)], r.vsems.at[1, axis])
        total = (r.vec_in[axis - 1, 0] + r.vec_in[axis - 1, 1]) + (
            r.vec_in[axis - 1, 2] + r.vec_in[axis - 1, 3]
        )
    if axis < 3:
        r.vec_in[axis, place.coords[axis]] = total
        vec_send(axis, r, place)
    else:
        r.vec[...] = total


def vec_drain(r):
    wait_all(r.vec_x, r.vsems.at[0, 0])
    for axis in range(3):
        wait_all(r.vec_in.at[axis, pl.ds(0, 3)], r.vsems.at[0, 1 + axis])


def step_exchange(g, r, place):
    exchange_start(g, r, place)
    if g == 0:
        vec_exchange(r, place)


def step_scatter(g, r, place):
    exchange_done(g, r, place)
    if g == 0:
        vec_step(0, r, place)


def step_axis(g, r, place):
    axis_done(g, r, place)
    if g == 0:
        vec_step(1, r, place)


def step_plane(g, r, place):
    plane_done(g, r, place)
    if g == 0:
        vec_step(2, r, place)


def step_back(g, r, place):
    plane_back(g, r, place)
    if g == 0:
        vec_step(3, r, place)


SUM_STEPS = (
    step_exchange,
    step_scatter,
    step_axis,
    step_plane,
    step_back,
    gather_last,
    sum_out,
)
SUM_DURING_BACK = ((7, 2),)
SUM_AFTER_BACK = (3,)
SUM_TAIL = ((1, 1), (1, 2), (0, 4), (1, 3), (1, 4), (0, 5), (1, 5), (0, 6), (1, 6))


WEIGHTS = ["w_query", "w_key", "w_value", "w_out", "w_up", "w_down"]
INPUTS = ["inputs", "groups_hbm", "cotangent"] + [name + "_hbm" for name in WEIGHTS]
INPUTS += [name + "_hbm" for name in ("gain_one", "shift_one", "gain_two", "shift_two")]
OUTPUTS = {
    "output": ((1, ROWS, D), BF),
    "input_grad": ((1, ROWS, D), BF),
    "sums0": ((2, 3, 3072, 128), BF),
    "sums1": ((2, 3, 1024, 128), BF),
    "vec_hbm": ((8, D), F32),
}
SCRATCH = {
    "w_query": ((D, D), BF),
    "w_key": ((D, D), BF),
    "w_value": ((D, D), BF),
    "w_out": ((D, D), BF),
    "w_up": ((D, FF), BF),
    "w_down": ((FF, D), BF),
    "cot": ((ROWS, D), BF),
    "groups": ((2, ROWS), jnp.int32),
    "gain_one": ((1, D), F32),
    "shift_one": ((1, D), F32),
    "gain_two": ((1, D), F32),
    "shift_two": ((1, D), F32),
    "last_grad": ((ROWS, D), BF),
    "vec": ((8, D), F32),
    "hid": ((3, ROWS, D), BF),
    "q_out": ((2, 8, 64, 128), BF),
    "q_in": ((2, 16, 64, 128), BF),
    "o_out": ((2, 16, 80, 128), BF),
    "o_in": ((2, 16, 80, 128), BF),
    "do_out": ((2, 8, 80, 128), BF),
    "do_in": ((2, 16, 80, 128), BF),
    "dq_out": ((2, 16, 64, 128), BF),
    "dq_in": ((2, 16, 64, 128), BF),
    "dkv_acc": ((512, 128), F32),
    "dqt": ((8, 64, 256), F32),
    "lq": ((2, 2048, 128), BF),
    "qz": ((2048, 128), BF),
    "ld": ((2048, 128), BF),
    "neg_log": ((16, 8, 128), F32),
    "neg_delta": ((16, 8, 128), F32),
    "f_acc": ((4, 512, 128), F32),
    "f_top": ((4, 512, 128), F32),
    "att": ((2, ROWS, D), F32),
    "log_total": ((2, 8, 128), F32),
    "grp_q": ((16, 8, 128), jnp.int32),
    "kv_out": ((2, 8, ROWS, 128), BF),
    "kv_in": ((2, 32, ROWS, 128), BF),
    "grp_out": ((1, 8, 128), jnp.int32),
    "grp_in": ((32, 8, 128), jnp.int32),
    "ka": ((2, 4096, 128), BF),
    "va": ((2, 4096, 128), BF),
    "kat": ((64, 4096), BF),
    "att_low": ((2, ROWS, D), BF),
    "n_one": ((2, ROWS, D), F32),
    "f_one": ((2, ROWS, 128), F32),
    "first_low": ((2, ROWS, D), BF),
    "pre": ((2, ROWS, FF), F32),
    "act": ((2, ROWS, FF), BF),
    "n_two": ((2, ROWS, D), F32),
    "f_two": ((2, ROWS, 128), F32),
    "work": ((ROWS, D), F32),
    "dy": ((ROWS, D), F32),
    "down_low": ((2, ROWS, D), BF),
    "up_low": ((2, ROWS, FF), BF),
    "out_low": ((2, ROWS, D), BF),
    "dkv_out": ((32, ROWS, 128), BF),
    "dkv_in": ((2, 32, ROWS, 128), BF),
    "dq": ((2, ROWS, D), BF),
    "dk": ((2, ROWS, D), BF),
    "dv": ((2, ROWS, D), BF),
    "vec_own": ((8, D), F32),
    "vec_x": ((8, D), F32),
    "vec_in": ((3, 4, 8, D), F32),
}
for g, rows in enumerate(SUM_ROWS):
    SCRATCH |= {
        f"sum_in{g}": ((6 * rows, 128), BF),
        f"sum_x{g}": ((3 * rows, 128), BF),
        f"sum_r0{g}": ((3, 3, rows // 4, 128), BF),
        f"sum_r1{g}": ((3, 15, rows // 64, 128), BF),
        f"sum_s0{g}": ((3, rows // 4, 128), BF),
        f"sum_t{g}": ((2, 3, rows, 128), BF),
    }
SEMS = {"sems": (12, 2), "gsems": (4,), "load_sems": (13,), "out_sems": (3,), "kv_sems": (2, 4), "plane_sems": (2, 8), "sum_sems0": (2, 8, 3), "sum_sems1": (2, 8, 3), "vsems": (3, 4)}


def kernel(*refs):
    names = INPUTS + list(OUTPUTS) + list(SCRATCH) + list(SEMS)
    r = SimpleNamespace(**dict(zip(names, refs)))
    place = Place()
    for name in LOADED[:5]:
        load(name, r, place).start()
    greet(place)
    for name in LOADED[5:]:
        load(name, r, place).start()
    r.vec_own[...] = jnp.zeros_like(r.vec_own)

    @pl.loop(0, 2)
    def _(v):
        @pl.when(v == 0)
        def _():
            for name in LOADED[:5]:
                load(name, r, place).wait()

        project_queries(v, r)

        @pl.when(v == 0)
        def _():
            project_keys_values(v, r)
            all_here()
            send_groups(r, place)

        send_queries(v, r, place)

        @pl.when(v == 1)
        def _():
            project_keys_values(v, r)

        send_keys_values(v, r, place)
        pass_on(v, r, place)

        @pl.when(v == 0)
        def _():
            wait_all(r.grp_in, r.gsems.at[1])
            wait_all(r.grp_q, r.gsems.at[3])
            make_aug(r)

        wait_all(r.q_in.at[v], r.sems.at[3, v])
        make_queries(v, r)
        attention(v, r, place)

        @pl.when(v == 0)
        def _():
            for name in LOADED[5:12]:
                load(name, r, place).wait()

        wait_all(r.o_in.at[v], r.sems.at[5, v])
        after_attention(v, r)

    finals = [
        pltpu.make_async_copy(r.hid.at[2], r.output.at[0], r.out_sems.at[0]),
        pltpu.make_async_copy(r.last_grad, r.input_grad.at[0], r.out_sems.at[1]),
        pltpu.make_async_copy(r.vec, r.vec_hbm, r.out_sems.at[2]),
    ]
    finals[0].start()
    load("cot", r, place).wait()
    r.dy[...] = r.cot[...].astype(F32)

    @pl.loop(0, 2)
    def _(step):
        v = 1 - step
        before_attention_back(v, r)
        send_do(v, r, place)

        @pl.when(v == 0)
        def _():
            weight_grads_early(r)
            SUM_STEPS[0](0, r, place)

        prepare_back(v, r)

        @pl.when(v == 0)
        def _():
            SUM_STEPS[1](0, r, place)

        wait_all(r.do_in.at[v], r.sems.at[7, v])

        attention_back(v, r, place)

        @pl.when(v == 0)
        def _():
            for step in SUM_AFTER_BACK:
                SUM_STEPS[step](0, r, place)

        wait_all(r.dq_in.at[v], r.sems.at[9, v])
        wait_all(r.dkv_in.at[v], r.sems.at[11, v])
        take_gradients(v, r)

        @pl.when(v == 1)
        def _():
            r.dy[...] = input_gradient(v, r).astype(F32)

    weight_grads_late(r)
    SUM_STEPS[0](1, r, place)
    r.last_grad[...] = input_gradient(0, r)
    finals[1].start()
    for g, step in SUM_TAIL:
        SUM_STEPS[step](g, r, place)

    finals[2].start()
    for copy in finals:
        copy.wait()
    vec_drain(r)
    for g in range(2):
        sum_drain(g, r, place)
    wait_sent(r.grp_in, r.gsems.at[0], place.self_kv, 32)
    wait_sent(r.grp_q, r.gsems.at[2], place.self_q, 16)

    @pl.loop(0, 2)
    def _(v):
        wait_sent(r.kv_in.at[v], r.sems.at[0, v], place.self_kv, 8)
        wait_all(r.kv_in.at[v, pl.ds(0, 24)], r.sems.at[1, v])
        wait_sent(r.q_in.at[v], r.sems.at[2, v], place.self_q, 16)
        wait_sent(r.o_in.at[v], r.sems.at[4, v], place.self_q, 16)
        wait_sent(r.do_in.at[v], r.sems.at[6, v], place.self_q, 16)
        wait_sent(r.dq_in.at[v], r.sems.at[8, v], place.self_q, 16)

    wait_sent(r.dkv_in.at[0], r.sems.at[10, 0], place.self_kv, 32)


def unpack(output, input_grad, early, late, vec):
    def body(*refs):
        output, input_grad, early, late, vec, output_to, input_grad_to = refs[:7]
        query, key, value, out, up, down = refs[7:13]
        got, small, up_f, down_f, vec_in, vec_out, sin, sout = refs[17:]
        loads = []
        for j in range(12):
            src = late.at[pl.ds(4 * j, 4)] if j < 3 else early.at[pl.ds(4 * (j - 3), 4)]
            loads.append(pltpu.make_async_copy(src, got.at[pl.ds(4 * j, 4)], sin.at[j]))
        order = [7, 8, 9, 10, 3, 4, 5, 6, 0, 1, 2, 11]
        for j in order:
            loads[j].start()
        get_vec = pltpu.make_async_copy(vec, vec_in, sin.at[12])
        get_vec.start()
        stores = [
            pltpu.make_async_copy(output, output_to, sout.at[12]),
            pltpu.make_async_copy(input_grad, input_grad_to, sout.at[13]),
        ]
        for copy in stores:
            copy.start()

        def store(j, src, dst):
            stores.append(pltpu.make_async_copy(src, dst, sout.at[j]))
            stores[-1].start()

        for j in order:
            loads[j].wait()
            tiles = [got[4 * j + k].astype(F32) for k in range(4)]
            cols = [slice(128 * k, 128 * k + 128) for k in range(4)]
            if j < 3 or j == 11:
                i = min(j, 3)
                for k in range(4):
                    small[i, :, cols[k]] = tiles[k]
                store(j, small.at[i], (query, key, value, out)[i])
            elif j < 7:
                at = 512 * (j - 3)
                for k in range(4):
                    up_f[:, at + 128 * k : at + 128 * k + 128] = tiles[k]
                store(j, up_f.at[:, pl.ds(at, 512)], up.at[:, pl.ds(at, 512)])
            else:
                for k in range(4):
                    down_f[512 * k : 512 * k + 512, cols[j - 7]] = tiles[k]
                if j == 10:
                    for k in range(4):
                        rows = pl.ds(512 * k, 512)
                        store(7 + k, down_f.at[rows], down.at[rows])
        get_vec.wait()
        for i in range(4):
            vec_out[i, 0] = vec_in[i]
            copy = pltpu.make_async_copy(vec_out.at[i, 0], refs[13 + i], sout.at[14 + i])
            copy.start()
            stores.append(copy)
        for copy in stores:
            copy.wait()

    square, hbm = jax.ShapeDtypeStruct((D, D), F32), pl.BlockSpec(memory_space=pl.ANY)
    rows = jax.ShapeDtypeStruct((1, ROWS, D), BF)
    shapes = [rows] * 2 + [square] * 4
    shapes += [jax.ShapeDtypeStruct((D, FF), F32), jax.ShapeDtypeStruct((FF, D), F32)]
    return pl.pallas_call(
        body,
        out_shape=shapes + [jax.ShapeDtypeStruct((D,), F32)] * 4,
        in_specs=[hbm] * 5,
        out_specs=[hbm] * 12,
        scratch_shapes=[
            pltpu.VMEM((48, 512, 128), BF),
            pltpu.VMEM((4, D, D), F32),
            pltpu.VMEM((D, FF), F32),
            pltpu.VMEM((FF, D), F32),
            pltpu.VMEM((8, D), F32),
            pltpu.VMEM((4, 1, D), F32),
            pltpu.SemaphoreType.DMA((13,)),
            pltpu.SemaphoreType.DMA((18,)),
        ],
        compiler_params=pltpu.CompilerParams(vmem_limit_bytes=60 * 2**20),
        name="unpack",
    )(output, input_grad, early, late, vec)


def on_device(inputs, groups, cotangent, *params):
    vectors = [x.reshape(1, D) for x in params[6:]]
    hbm = pl.BlockSpec(memory_space=pl.ANY)
    out = pl.pallas_call(
        kernel,
        out_shape=[jax.ShapeDtypeStruct(shape, kind) for shape, kind in OUTPUTS.values()],
        in_specs=[hbm] * len(INPUTS),
        out_specs=[hbm] * len(OUTPUTS),
        scratch_shapes=[pltpu.VMEM(shape, kind) for shape, kind in SCRATCH.values()]
        + [pltpu.SemaphoreType.DMA(shape) for shape in SEMS.values()],
        compiler_params=pltpu.CompilerParams(
            collective_id=0, has_side_effects=True, vmem_limit_bytes=62 * 2**20
        ),
        name="visits",
    )(inputs, groups, cotangent, *params[:6], *vectors)
    return unpack(*out[:2], out[2].reshape(36, 512, 128), out[3].reshape(12, 512, 128), out[4])


def solution(mesh):
    rows = P(None, "dp", None)
    return jax.shard_map(
        on_device,
        mesh=mesh,
        in_specs=(rows, P(None, "dp"), rows) + (P(),) * 10,
        out_specs=(P("section", "dp", None),) * 2 + (P(),) * 10,
        check_vma=False,
    )
```
